32 devices in a mesh: frag: 8 (over z, x), aux: 4 (over y, core).
Axes of the slice: x: 2, y: 2, z: 4, core: 2. Of those that a mesh axis runs over, the one named last changes fastest.
Arguments:
- vir_grid: bfloat16 [32, 128, 4096], P('frag', None, 'aux'), may hold values from -6 to 6
- vir_energy: bfloat16 [32, 128], P('frag'), may hold values from 0.29882812 to 2.5
- occ_grid: bfloat16 [8, 3, 4096], P('frag', None, 'aux'), may hold values from -0.21875 to 0.21875
- occ_energy: float32 [8, 3], P('frag'), may hold values from -1.5 to -0.3
- vir_list: int32 [8, 8], replicated, may hold values from 0 to 31, as said below
- vir_rows: int32 [8, 8], replicated, may hold values from 32 to 128
- owner_map: int32 [32], replicated, may hold values from 0 to 31, as said below
Outputs:
- density_blocks: float32 [32, 128, 128], P('frag', 'aux')
The draws below stay inside these ranges and needn't reach their ends.
Inputs may be any that keep to these rules, and one draw needn't show every extreme that they name: A permutation: block b is held in row owner_map[b] of vir_grid and vir_energy, and row s belongs to fragment index s // 4 of frag. `vir_list`: each row names 8 different blocks. For fragment f every named block b has |owner_map[b] // 4 - f| <= 3; at most 2 of them share one value of owner_map[b] // 4, and exactly 2 have the value f.
All inputs are finite; a program needn't handle non-finite values.
Results may differ from the reference program's by a relative error of at most 0.0018.
Values may be sent and summed in bfloat16 or wider, within the bound.
No kernel may reach another device: no remote copies, remote signals or barrier semaphores. Data moves between devices by JAX's collectives and lax.ppermute only.
A program may use at most 128 MiB of HBM per device.

```python
import jax
import jax.numpy as jnp
from jax import lax

BLOCK = 128
VIR_BLOCKS = 8
NAUX = 4096
EOS_OCC = 3
REACH = 3
CAP = 2
OWN_BLOCKS = 4
FRAGS = 8
NBLK = 32


def list_layout(key):
    span = 2 * REACH + 1
    perm_key, local_key, pick_key, order_key = jax.random.split(jax.random.fold_in(key, 11), 4)
    slot_of_block = jax.random.permutation(perm_key, NBLK).astype(jnp.int32)
    block_at_slot = jnp.argsort(slot_of_block).astype(jnp.int32)
    noise = jax.random.randint(local_key, (FRAGS, span, OWN_BLOCKS), 0, 2 ** 16)
    local_order = jnp.argsort(noise * OWN_BLOCKS + jnp.arange(OWN_BLOCKS)[None, None, :], axis=2)[:, :, :CAP]
    offsets = jnp.arange(span) - REACH
    owner = jnp.arange(FRAGS)[:, None] + offsets[None, :]
    inside = (owner >= 0) & (owner < FRAGS)
    is_self = offsets == 0
    draws = jax.random.randint(pick_key, (FRAGS, span, CAP), 0, 2 ** 16)
    score = jnp.where(is_self[None, :, None], 0, jnp.where(inside[:, :, None], draws + 1, 2 ** 20))
    flat_score = score.reshape(FRAGS, span * CAP) * 64 + jnp.arange(span * CAP)[None, :]
    taken = jnp.argsort(flat_score, axis=1)[:, :VIR_BLOCKS]
    slot_table = (jnp.clip(owner, 0, FRAGS - 1)[:, :, None] * OWN_BLOCKS + local_order).reshape(FRAGS, span * CAP)
    picked = jnp.take_along_axis(slot_table, taken, axis=1)
    shuffle_noise = jax.random.randint(order_key, (FRAGS, VIR_BLOCKS), 0, 2 ** 16)
    shuffle = jnp.argsort(shuffle_noise * 64 + jnp.arange(VIR_BLOCKS)[None, :], axis=1)
    picked = jnp.take_along_axis(picked, shuffle, axis=1)
    return (slot_of_block, jnp.take(block_at_slot, picked, axis=0).astype(jnp.int32))


def draw_owner_map(key, part):
    return list_layout(key)[0]


def draw_vir_list(key, part):
    return list_layout(key)[1]


def with_ends(values, key, smallest, largest):
    longest = values.shape.index(max(values.shape))
    spots = []
    for shift in (0, 1):
        where = [jax.random.randint(jax.random.fold_in(key, axis), (), 0, length) for axis, length in enumerate(values.shape)]
        where[longest] = (where[longest] + shift) % values.shape[longest]
        spots.append(tuple(where))
    return values.at[spots[0]].set(smallest).at[spots[1]].set(largest)


def shard_levels(own_key, extent, cuts, least, largest):
    gain = 1.0
    for dim, parts in cuts:
        heights = jax.random.uniform(jax.random.fold_in(jax.random.fold_in(own_key, 6), dim), (parts,), jnp.float32, least / len(cuts), largest / len(cuts))
        gain = gain * jnp.repeat(jnp.exp(heights), extent[dim] // parts).reshape((-1,) + (1,) * (len(extent) - 1 - dim))
    return gain


def normal_values(rng, shape, deviation, bound, pieces=(), held_as=jnp.bfloat16):
    level = shard_levels(rng, shape, pieces, -0.22, 0.18) if pieces else 1.0
    values = jax.random.normal(rng, shape, jnp.float32) * deviation * level
    return jnp.minimum(jnp.maximum(values, -bound), bound).astype(held_as)


def setup_inputs(seed: int = 0) -> dict:
    arg_keys = jax.random.split(jax.random.key(seed), 8)
    vir_grid = normal_values(arg_keys[0], (NBLK, BLOCK, NAUX), 1.0, 6.0, ((0, 8), (2, 4)))
    vir_energy = jnp.clip(0.29882812 + 2.2011719 * jax.random.uniform(arg_keys[1], (NBLK, BLOCK), jnp.float32) ** shard_levels(arg_keys[1], (NBLK, BLOCK), ((0, 8),), -0.2, 0.2), 0.29882812, 2.5).astype(jnp.bfloat16)
    occ_grid = normal_values(arg_keys[2], (FRAGS, EOS_OCC, NAUX), (NAUX // 5) ** -0.5, 0.21875, ((0, 8), (2, 4)))
    occ_energy = jnp.clip(-1.5 + 1.2 * jax.random.uniform(arg_keys[3], (FRAGS, EOS_OCC), jnp.float32) ** shard_levels(arg_keys[3], (FRAGS, EOS_OCC), ((0, 8),), -0.2, 0.2), -1.5, -0.3)
    vir_list = draw_vir_list(jax.random.fold_in(arg_keys[7], 71), 0)
    vir_rows = with_ends(jax.random.randint(arg_keys[5], (FRAGS, VIR_BLOCKS), BLOCK // 4, BLOCK + 1), jax.random.fold_in(arg_keys[5], 1), BLOCK // 4, BLOCK).astype(jnp.int32)
    owner_map = draw_owner_map(jax.random.fold_in(arg_keys[7], 71), 0)
    return {"vir_grid": vir_grid, "vir_energy": vir_energy, "occ_grid": occ_grid, "occ_energy": occ_energy, "vir_list": vir_list, "vir_rows": vir_rows, "owner_map": owner_map}


def fragment_density(vir_grid, vir_energy, occ_grid, occ_energy, vir_list, vir_rows, owner_map, frag_id):
    block_rows = vir_grid.shape[1]
    aux_cols = vir_grid.shape[2]
    list_len = vir_list.shape[1]
    nvir = list_len * block_rows
    slots = jnp.take(owner_map, vir_list[frag_id], axis=0).astype(jnp.int32)
    grid = jnp.take(vir_grid, slots, axis=0)
    live = jnp.arange(block_rows)[None, :] < vir_rows[frag_id][:, None]
    grid = jnp.where(live[:, :, None], grid, jnp.zeros_like(grid)).reshape(nvir, aux_cols)
    energies = jnp.take(vir_energy, slots, axis=0).astype(jnp.float32).reshape(nvir)
    occ_rows = occ_grid[frag_id].astype(jnp.float32)
    levels = occ_energy[frag_id].astype(jnp.float32)
    density = jnp.zeros((list_len, block_rows, block_rows), jnp.float32)
    for left_occ in range(EOS_OCC):
        for right_occ in range(left_occ, EOS_OCC):
            weight = occ_rows[left_occ] * occ_rows[right_occ]
            scaled = (grid.astype(jnp.float32) * weight[None, :]).astype(jnp.bfloat16)
            integrals = jnp.dot(scaled, grid.T, preferred_element_type=jnp.float32)
            energy_gap = levels[left_occ] + levels[right_occ] - energies[:, None] - energies[None, :]
            amplitude = (integrals / energy_gap).astype(jnp.bfloat16)
            blocks = amplitude.reshape(list_len, block_rows, nvir).astype(jnp.float32)
            density = density + jnp.einsum("kac,kbc->kab", blocks, blocks)
    return density, slots


def reference(vir_grid, vir_energy, occ_grid, occ_energy, vir_list, vir_rows, owner_map):
    nblk = vir_grid.shape[0]
    block_rows = vir_grid.shape[1]
    frags = vir_list.shape[0]

    def one_fragment(frag_id):
        return fragment_density(vir_grid, vir_energy, occ_grid, occ_energy, vir_list, vir_rows, owner_map, frag_id)

    densities, all_slots = lax.map(one_fragment, jnp.arange(frags, dtype=jnp.int32))
    result = jnp.zeros((nblk, block_rows, block_rows), jnp.float32)
    result = result.at[all_slots.reshape(-1)].add(densities.reshape(-1, block_rows, block_rows))
    return result
```

```python
import functools

import jax
import jax.numpy as jnp
from jax import lax
from jax.experimental import pallas as pl
from jax.experimental.pallas import tpu as pltpu
from jax.sharding import PartitionSpec as P

ROUNDS = ((1, 0), (1, 1), (2, 0), (2, 1), (3, 0), (3, 1))
CAP = 2
PAIRS = tuple((i, j) for i in range(3) for j in range(i, 3))
VMEM_LIMIT = 56 * 2**20
ANY = pl.BlockSpec(memory_space=pl.ANY)
SMEM = pl.BlockSpec(memory_space=pltpu.SMEM)
VMEM = pl.BlockSpec(memory_space=pltpu.VMEM)


def round_pairs(distance, parity, frags):
    up = [(i, i + distance) for i in range(frags - distance) if (i // distance) % 2 == parity]
    return up + [(b, a) for a, b in up]


def plan_kernel(frags, own_count, list_len, me_ref, map_ref, list_ref, table, *refs):
    outs, own, plan, sems = refs[:6], refs[6], refs[7], refs[8]
    me = me_ref[0]
    copies = []

    def pick(fragment, owner):
        count = jnp.int32(0)
        picked = [jnp.int32(0)] * CAP
        for k in range(list_len):
            row = map_ref[list_ref[fragment, k]]
            hit = row // own_count == owner
            for r in range(CAP):
                picked[r] = jnp.where(hit & (count == r), row % own_count, picked[r])
            count = count + hit.astype(jnp.int32)
        return picked, count

    for index, (distance, parity) in enumerate(ROUNDS):
        up = (me // distance) % 2 == parity
        partner = jnp.where(up, me + distance, me - distance)
        inside = (partner >= 0) & (partner < frags)
        picked, count = pick(jnp.clip(partner, 0, frags - 1), me)
        for r in range(CAP):
            copies.append((
                inside & (count > r),
                pltpu.make_async_copy(table.at[picked[r]], outs[index].at[r], sems.at[index, r]),
            ))
        if index == 0:
            picked, count = pick(me, me)
            for r in range(CAP):
                copies.append((
                    count > r,
                    pltpu.make_async_copy(table.at[picked[r]], own.at[r], sems.at[6, r]),
                ))
    for needed, copy in copies:
        pl.when(needed)(copy.start)

    rows, owners, codes, classes = [], [], [], []
    for k in range(list_len):
        row = map_ref[list_ref[me, k]]
        owner = row // own_count
        low = jnp.minimum(me, owner)
        far = jnp.abs(owner - me)
        code = jnp.int32(0)
        for index, (distance, parity) in enumerate(ROUNDS):
            code = jnp.where(
                (far == distance) & ((low // distance) % 2 == parity), index + 1, code
            )
        rows.append(row)
        owners.append(owner)
        codes.append(code)
        classes.append(jnp.where(code == 0, 0, jnp.maximum(code - 3, 1)))
    for k in range(list_len):
        place = jnp.int32(0)
        rank = jnp.int32(0)
        for j in range(list_len):
            if j < k:
                place += (classes[j] <= classes[k]).astype(jnp.int32)
                rank += (owners[j] == owners[k]).astype(jnp.int32)
            elif j > k:
                place += (classes[j] < classes[k]).astype(jnp.int32)
        plan[0, place] = codes[k]
        plan[1, place] = rank
        plan[2, place] = rows[k]
        plan[3, place] = jnp.int32(k)
    for needed, copy in copies:
        pl.when(needed)(copy.wait)


def plan_and_pack(me, owner_map, vir_list, table, frags):
    own_count, block_rows, cols = table.shape
    list_len = vir_list.shape[1]
    part = jax.ShapeDtypeStruct((CAP, block_rows, cols), table.dtype)
    return pl.pallas_call(
        functools.partial(plan_kernel, frags, own_count, list_len),
        out_shape=(part,) * 7 + (jax.ShapeDtypeStruct((4, list_len), jnp.int32),),
        in_specs=[SMEM, SMEM, SMEM, ANY],
        out_specs=(ANY,) * 7 + (SMEM,),
        scratch_shapes=[pltpu.SemaphoreType.DMA((7, CAP))],
        name="plan_and_pack",
    )(me, owner_map, vir_list, table)


def pack_kernel(first, codes, plan, *refs):
    arrived, out, sems = refs[: len(codes)], refs[len(codes)], refs[len(codes) + 1]
    for i in range(2):
        code = plan[0, first + i]
        rank = plan[1, first + i]
        for source, ref in zip(codes, arrived):

            @pl.when(code == source)
            def _(ref=ref):
                pltpu.make_async_copy(ref.at[rank], out.at[i], sems.at[i]).start()

    for i in range(2):
        pltpu.make_async_copy(arrived[0].at[0], out.at[i], sems.at[i]).wait()


def pack_group(first, plan, arrived):
    codes = tuple(arrived)
    refs = [arrived[c] for c in codes]
    return pl.pallas_call(
        functools.partial(pack_kernel, first, codes),
        out_shape=jax.ShapeDtypeStruct(refs[0].shape, refs[0].dtype),
        in_specs=[SMEM] + [ANY] * len(refs),
        out_specs=ANY,
        scratch_shapes=[pltpu.SemaphoreType.DMA((2,))],
        name="pack_group",
    )(plan, *refs)


def contract_kernel(
    list_len, block, width, where, plan, levels, rows_ref, weights, energy, *refs
):
    groups = list_len // 2
    parts, (out, grid, scaled, total, amps, sems) = refs[: groups * 4], refs[groups * 4 :]
    me, aux = where[0], where[1]
    quarter_of = (aux, aux ^ 2, aux ^ 1, aux ^ 3)
    copies = {}
    for quarter in range(4):
        for group in range(groups):
            for i in range(2):
                copy = pltpu.make_async_copy(
                    parts[group * 4 + quarter].at[i],
                    grid.at[pl.ds((group * 2 + i) * block, block), pl.ds(quarter * width, width)],
                    sems.at[quarter, group, i],
                )
                copy.start()
                copies[quarter, group, i] = copy
    nvir = list_len * block
    mine = (aux, list_len - 1 - aux)
    for quarter in range(4):
        for group in range(groups):
            for i in range(2):
                copies[quarter, group, i].wait()
        cols = pl.ds(quarter * width, width)
        begin = pl.multiple_of(quarter_of[quarter] * width, width)
        occ = [weights[i : i + 1, pl.ds(begin, width)] for i in range(3)]
        for b in range(2):
            left = grid[pl.ds(pl.multiple_of(mine[b] * block, block), block), cols].astype(
                jnp.float32
            )
            for p, (i, j) in enumerate(PAIRS):
                scaled[pl.ds((p * 2 + b) * block, block), :] = (
                    left * (occ[i] * occ[j])
                ).astype(jnp.bfloat16)

        def rows_step(step, carry, quarter=quarter, cols=cols):
            rows = pl.ds(pl.multiple_of(step * 512, 512), 512)
            for half in range(2):
                right = pl.ds(half * 512, 512)
                term = lax.dot_general(
                    scaled[rows, :],
                    grid[right, cols],
                    (((1,), (1,)), ((), ())),
                    preferred_element_type=jnp.float32,
                )
                if quarter == 0:
                    total[rows, right] = term
                else:
                    total[rows, right] += term
            return carry

        lax.fori_loop(0, 3, rows_step, 0)

    lane = lax.broadcasted_iota(jnp.int32, (block, block), 1)
    sub = lax.broadcasted_iota(jnp.int32, (block, block), 0)
    for b in range(2):
        own_row = energy[pl.ds(plan[2, mine[b]], 1), :]
        own_energy = jnp.transpose(jnp.broadcast_to(own_row, (block, block)))
        own_live = sub < rows_ref[me, plan[3, mine[b]]]
        for q in range(list_len):
            their_energy = energy[pl.ds(plan[2, q], 1), :]
            live = own_live & (lane < rows_ref[me, plan[3, q]])
            for p, (i, j) in enumerate(PAIRS):
                gap = (levels[0, i] + levels[0, j]) - own_energy - their_energy
                value = total[pl.ds((p * 2 + b) * block, block), pl.ds(q * block, block)]
                amps[:, pl.ds(p * nvir + q * block, block)] = jnp.where(
                    live, value / gap, 0.0
                ).astype(jnp.bfloat16)
        out[b] = lax.dot_general(
            amps[...], amps[...], (((1,), (1,)), ((), ())), preferred_element_type=jnp.float32
        )


def contract(where, plan, levels, vir_rows, weights, energy, parts):
    list_len = vir_rows.shape[1]
    block, width = parts[0].shape[1:]
    nvir = list_len * block
    pair_count = len(PAIRS)
    flops = 2 * pair_count * 2 * block * nvir * 4 * width
    return pl.pallas_call(
        functools.partial(contract_kernel, list_len, block, width),
        out_shape=jax.ShapeDtypeStruct((2, block, block), jnp.float32),
        in_specs=[SMEM, SMEM, SMEM, SMEM, VMEM, VMEM] + [ANY] * len(parts),
        out_specs=VMEM,
        scratch_shapes=[
            pltpu.VMEM((nvir, 4 * width), jnp.bfloat16),
            pltpu.VMEM((pair_count * 2 * block, width), jnp.bfloat16),
            pltpu.VMEM((pair_count * 2 * block, nvir), jnp.float32),
            pltpu.VMEM((block, pair_count * nvir), jnp.bfloat16),
            pltpu.SemaphoreType.DMA((4, list_len // 2, 2)),
        ],
        compiler_params=pltpu.CompilerParams(vmem_limit_bytes=VMEM_LIMIT),
        cost_estimate=pl.CostEstimate(
            flops=flops, bytes_accessed=nvir * 4 * width * 2, transcendentals=0
        ),
        name="contract",
    )(where, plan, levels, vir_rows, weights, energy, *parts)


def spread_kernel(own_count, list_len, where, plan, kept, came, out):
    aux = where[1]
    out[...] = jnp.zeros_like(out)
    holders = (aux, aux ^ 2, aux ^ 1, aux ^ 3)
    for index, holder in enumerate(holders):
        source = kept if index < 2 else came
        for b in range(2):
            place = holder if b == 0 else list_len - 1 - holder
            out[plan[2, place] // own_count, plan[1, place]] = source[2 * (index % 2) + b]


def spread(where, plan, kept, came, frags, own_count, list_len):
    return pl.pallas_call(
        functools.partial(spread_kernel, own_count, list_len),
        out_shape=jax.ShapeDtypeStruct((frags, CAP) + kept.shape[1:], kept.dtype),
        in_specs=[SMEM, SMEM, VMEM, VMEM],
        out_specs=VMEM,
        name="spread",
    )(where, plan, kept, came)


def collect_kernel(own_count, list_len, where, map_ref, list_ref, came, out):
    me = where[0]
    out[...] = jnp.zeros_like(out)

    def one(fragment, carry):
        count = jnp.int32(0)
        for k in range(list_len):
            row = map_ref[list_ref[fragment, k]]
            hit = row // own_count == me

            @pl.when(hit)
            def _(row=row, count=count):
                out[row % own_count] += came[fragment, count]

            count = count + hit.astype(jnp.int32)
        return carry

    lax.fori_loop(0, list_ref.shape[0], one, 0)


def collect(where, owner_map, vir_list, came, own_count):
    return pl.pallas_call(
        functools.partial(collect_kernel, own_count, vir_list.shape[1]),
        out_shape=jax.ShapeDtypeStruct((own_count,) + came.shape[2:], came.dtype),
        in_specs=[SMEM, SMEM, SMEM, VMEM],
        out_specs=VMEM,
        name="collect",
    )(where, owner_map, vir_list, came)


def body(vir_grid, vir_energy, occ_grid, occ_energy, vir_list, vir_rows, owner_map):
    frags = lax.axis_size("frag")
    aux_count = lax.axis_size("aux")
    me = lax.axis_index("frag").astype(jnp.int32)
    aux = lax.axis_index("aux").astype(jnp.int32)
    own_count, block, width = vir_grid.shape
    list_len = vir_list.shape[1]
    where = jnp.stack([me, aux])
    far_pairs = [(i, i ^ 2) for i in range(aux_count)]
    near_pairs = [(i, i ^ 1) for i in range(aux_count)]

    energy = lax.psum(
        lax.dynamic_update_slice(
            jnp.zeros((frags * own_count, block), jnp.float32),
            vir_energy.astype(jnp.float32),
            (me * own_count, 0),
        ),
        "frag",
    )
    weights = lax.psum(
        lax.dynamic_update_slice(
            jnp.zeros((occ_grid.shape[1], aux_count * width), jnp.float32),
            occ_grid[0].astype(jnp.float32),
            (0, aux * width),
        ),
        "aux",
    )
    *outgoing, own, plan = plan_and_pack(where, owner_map, vir_list, vir_grid, frags)
    arrived = {}
    for index, (distance, parity) in enumerate(ROUNDS):
        payload = outgoing[index]
        if index >= 4:
            payload = lax.optimization_barrier((payload, arrived[index - 3]))[0]
        arrived[index + 1] = lax.ppermute(
            payload, "frag", round_pairs(distance, parity, frags)
        )
    parts = []
    for group in range(list_len // 2):
        if group == 0:
            here = own
        else:
            known = {c: arrived[c] for c in range(1, 4 + group)}
            here = pack_group(2 * group, plan, known)
        far = lax.ppermute(here, "aux", far_pairs)
        near = lax.ppermute(here, "aux", near_pairs)
        far_near = lax.ppermute(far, "aux", near_pairs)
        parts += [here, far, near, far_near]
    density = contract(where, plan, occ_energy, vir_rows, weights, energy, parts)

    half = block // 2
    quarter = block // aux_count
    side = aux // 2
    sent = lax.dynamic_slice_in_dim(density, (1 - side) * half, half, 1)
    stay = lax.dynamic_slice_in_dim(density, side * half, half, 1)
    both = jnp.concatenate([stay, lax.ppermute(sent, "aux", far_pairs)], axis=0)
    core = aux % 2
    sent = lax.dynamic_slice_in_dim(both, (1 - core) * quarter, quarter, 1)
    kept = lax.dynamic_slice_in_dim(both, core * quarter, quarter, 1)
    came = lax.ppermute(sent, "aux", near_pairs)
    outgoing = spread(where, plan, kept, came, frags, own_count, list_len)
    incoming = lax.all_to_all(outgoing, "frag", 0, 0, tiled=True)
    return collect(where, owner_map, vir_list, incoming, own_count)


def solution(mesh):
    return jax.shard_map(
        body,
        mesh=mesh,
        in_specs=(
            P("frag", None, "aux"),
            P("frag", None),
            P("frag", None, "aux"),
            P("frag", None),
            P(),
            P(),
            P(),
        ),
        out_specs=P("frag", "aux", None),
        check_vma=False,
    )
```

```python
import functools

import jax
import jax.numpy as jnp
from jax import lax
from jax.experimental import pallas as pl
from jax.experimental.pallas import tpu as pltpu
from jax.sharding import PartitionSpec as P

ROUNDS = ((1, 0), (1, 1), (2, 0), (2, 1), (3, 0), (3, 1))
CAP = 2
TAIL = 8
PAIRS = tuple((i, j) for i in range(3) for j in range(i, 3))
VMEM_LIMIT = 56 * 2**20
ANY = pl.BlockSpec(memory_space=pl.ANY)
SMEM = pl.BlockSpec(memory_space=pltpu.SMEM)
VMEM = pl.BlockSpec(memory_space=pltpu.VMEM)


def round_pairs(distance, parity, frags):
    up = [(i, i + distance) for i in range(frags - distance) if (i // distance) % 2 == parity]
    return up + [(b, a) for a, b in up]


def plan_kernel(
    frags, own_count, list_len, where, map_ref, list_ref, frag_tail, aux_tail, table, *refs
):
    outs, own, plan, sems = refs[:6], refs[6], refs[7], refs[8]
    me = where[0]
    block = table.shape[1]
    copies = []

    def pick(fragment, owner):
        count = jnp.int32(0)
        picked = [jnp.int32(0)] * CAP
        for k in range(list_len):
            row = map_ref[list_ref[fragment, k]]
            hit = row // own_count == owner
            for r in range(CAP):
                picked[r] = jnp.where(hit & (count == r), row % own_count, picked[r])
            count = count + hit.astype(jnp.int32)
        return picked, count

    for index, (distance, parity) in enumerate(ROUNDS):
        up = (me // distance) % 2 == parity
        partner = jnp.where(up, me + distance, me - distance)
        inside = (partner >= 0) & (partner < frags)
        picked, count = pick(jnp.clip(partner, 0, frags - 1), me)
        for r in range(CAP):
            copies.append((
                inside & (count > r),
                pltpu.make_async_copy(
                    table.at[picked[r]], outs[index].at[pl.ds(r * block, block)], sems.at[index, r]
                ),
            ))
        if index == 0:
            picked, count = pick(me, me)
            for r in range(CAP):
                copies.append((
                    count > r,
                    pltpu.make_async_copy(
                        table.at[picked[r]], own.at[pl.ds(r * block, block)], sems.at[6, r]
                    ),
                ))
    for needed, copy in copies:
        pl.when(needed)(copy.start)
    for out in outs:
        out[pl.ds(CAP * block, TAIL), :] = frag_tail[...]
    own[pl.ds(CAP * block, TAIL), :] = aux_tail[...]

    rows, owners, codes, classes = [], [], [], []
    for k in range(list_len):
        row = map_ref[list_ref[me, k]]
        owner = row // own_count
        low = jnp.minimum(me, owner)
        far = jnp.abs(owner - me)
        code = jnp.int32(0)
        for index, (distance, parity) in enumerate(ROUNDS):
            code = jnp.where(
                (far == distance) & ((low // distance) % 2 == parity), index + 1, code
            )
        rows.append(row)
        owners.append(owner)
        codes.append(code)
        classes.append(jnp.where(code == 0, 0, jnp.maximum(code - 3, 1)))
    for k in range(list_len):
        place = jnp.int32(0)
        rank = jnp.int32(0)
        for j in range(list_len):
            if j < k:
                place += (classes[j] <= classes[k]).astype(jnp.int32)
                rank += (owners[j] == owners[k]).astype(jnp.int32)
            elif j > k:
                place += (classes[j] < classes[k]).astype(jnp.int32)
        plan[0, place] = codes[k]
        plan[1, place] = rank
        plan[2, place] = rows[k]
        plan[3, place] = jnp.int32(k)
    for needed, copy in copies:
        pl.when(needed)(copy.wait)


def plan_and_pack(where, owner_map, vir_list, frag_tail, aux_tail, table, frags):
    own_count, block_rows, cols = table.shape
    list_len = vir_list.shape[1]
    part = jax.ShapeDtypeStruct((CAP * block_rows + TAIL, cols), table.dtype)
    return pl.pallas_call(
        functools.partial(plan_kernel, frags, own_count, list_len),
        out_shape=(part,) * 7 + (jax.ShapeDtypeStruct((4, list_len), jnp.int32),),
        in_specs=[SMEM, SMEM, SMEM, VMEM, VMEM, ANY],
        out_specs=(VMEM,) * 7 + (SMEM,),
        scratch_shapes=[pltpu.SemaphoreType.DMA((7, CAP))],
        name="plan_and_pack",
    )(where, owner_map, vir_list, frag_tail, aux_tail, table)


def pack_kernel(first, codes, block, plan, *refs):
    arrived, out, sems = refs[: len(codes)], refs[len(codes)], refs[len(codes) + 1]
    for i in range(2):
        code = plan[0, first + i]
        begin = pl.multiple_of(plan[1, first + i] * block, block)
        rows = pl.ds(i * block, block)
        for source, ref in zip(codes, arrived):

            @pl.when(code == source)
            def _(ref=ref, begin=begin, rows=rows):
                pltpu.make_async_copy(
                    ref.at[pl.ds(begin, block)], out.at[rows], sems.at[i]
                ).start()

    for i in range(2):
        rows = pl.ds(i * block, block)
        pltpu.make_async_copy(arrived[0].at[rows], out.at[rows], sems.at[i]).wait()


def pack_group(first, block, plan, arrived):
    codes = tuple(arrived)
    refs = [arrived[c] for c in codes]
    return pl.pallas_call(
        functools.partial(pack_kernel, first, codes, block),
        out_shape=jax.ShapeDtypeStruct((2 * block, refs[0].shape[1]), refs[0].dtype),
        in_specs=[SMEM] + [ANY] * len(refs),
        out_specs=VMEM,
        scratch_shapes=[pltpu.SemaphoreType.DMA((2,))],
        name="pack_group",
    )(plan, *refs)


def contract_kernel(
    list_len, block, width, own_count, where, plan, levels, rows_ref, weights, energy, *refs
):
    groups = list_len // 2
    parts, (out, grid, scaled, total, amps, sems) = refs[: groups * 4], refs[groups * 4 :]
    me, aux = where[0], where[1]
    copies = {}
    for quarter in range(4):
        for group in range(groups):
            for i in range(2):
                copy = pltpu.make_async_copy(
                    parts[group * 4 + quarter].at[pl.ds(i * block, block)],
                    grid.at[pl.ds((group * 2 + i) * block, block), pl.ds(quarter * width, width)],
                    sems.at[quarter, group, i],
                )
                copy.start()
                copies[quarter, group, i] = copy
    nvir = list_len * block
    mine = (aux, list_len - 1 - aux)
    for quarter in range(4):
        for group in range(groups):
            for i in range(2):
                copies[quarter, group, i].wait()
        cols = pl.ds(quarter * width, width)
        occ = [weights[quarter, i : i + 1, :].astype(jnp.float32) for i in range(3)]
        for b in range(2):
            left = grid[pl.ds(pl.multiple_of(mine[b] * block, block), block), cols].astype(
                jnp.float32
            )
            for p, (i, j) in enumerate(PAIRS):
                scaled[pl.ds((p * 2 + b) * block, block), :] = (
                    left * (occ[i] * occ[j])
                ).astype(jnp.bfloat16)

        def rows_step(step, carry, quarter=quarter, cols=cols):
            rows = pl.ds(pl.multiple_of(step * 512, 512), 512)
            for half in range(2):
                right = pl.ds(half * 512, 512)
                term = lax.dot_general(
                    scaled[rows, :],
                    grid[right, cols],
                    (((1,), (1,)), ((), ())),
                    preferred_element_type=jnp.float32,
                )
                if quarter == 0:
                    total[rows, right] = term
                else:
                    total[rows, right] += term
            return carry

        lax.fori_loop(0, 3, rows_step, 0)

    lane = lax.broadcasted_iota(jnp.int32, (block, block), 1)
    sub = lax.broadcasted_iota(jnp.int32, (block, block), 0)

    def energy_of(place):
        row = plan[0, place] * own_count + plan[2, place] % own_count
        return energy[pl.ds(row, 1), :]

    for b in range(2):
        own_row = energy_of(mine[b])
        own_energy = jnp.transpose(jnp.broadcast_to(own_row, (block, block)))
        own_live = sub < rows_ref[me, plan[3, mine[b]]]
        for q in range(list_len):
            their_energy = energy_of(q)
            live = own_live & (lane < rows_ref[me, plan[3, q]])
            for p, (i, j) in enumerate(PAIRS):
                gap = (levels[0, i] + levels[0, j]) - own_energy - their_energy
                value = total[pl.ds((p * 2 + b) * block, block), pl.ds(q * block, block)]
                amps[:, pl.ds(p * nvir + q * block, block)] = jnp.where(
                    live, value / gap, 0.0
                ).astype(jnp.bfloat16)
        out[b] = lax.dot_general(
            amps[...], amps[...], (((1,), (1,)), ((), ())), preferred_element_type=jnp.float32
        )


def contract(where, plan, levels, vir_rows, weights, energy, parts, own_count):
    list_len = vir_rows.shape[1]
    width = parts[0].shape[1]
    block = parts[-1].shape[0] // 2
    nvir = list_len * block
    pair_count = len(PAIRS)
    flops = 2 * pair_count * 2 * block * nvir * 4 * width
    return pl.pallas_call(
        functools.partial(contract_kernel, list_len, block, width, own_count),
        out_shape=jax.ShapeDtypeStruct((2, block, block), jnp.float32),
        in_specs=[SMEM, SMEM, SMEM, SMEM, VMEM, VMEM] + [ANY] * len(parts),
        out_specs=VMEM,
        scratch_shapes=[
            pltpu.VMEM((nvir, 4 * width), jnp.bfloat16),
            pltpu.VMEM((pair_count * 2 * block, width), jnp.bfloat16),
            pltpu.VMEM((pair_count * 2 * block, nvir), jnp.float32),
            pltpu.VMEM((block, pair_count * nvir), jnp.bfloat16),
            pltpu.SemaphoreType.DMA((4, list_len // 2, 2)),
        ],
        compiler_params=pltpu.CompilerParams(vmem_limit_bytes=VMEM_LIMIT),
        cost_estimate=pl.CostEstimate(
            flops=flops, bytes_accessed=nvir * 4 * width * 2, transcendentals=0
        ),
        name="contract",
    )(where, plan, levels, vir_rows, weights, energy, *parts)


def spread_kernel(own_count, list_len, where, plan, kept, came, out):
    aux = where[1]
    out[...] = jnp.zeros_like(out)
    holders = (aux, aux ^ 2, aux ^ 1, aux ^ 3)
    for index, holder in enumerate(holders):
        source = kept if index < 2 else came
        for b in range(2):
            place = holder if b == 0 else list_len - 1 - holder
            out[plan[2, place] // own_count, plan[1, place]] = source[2 * (index % 2) + b]


def spread(where, plan, kept, came, frags, own_count, list_len):
    return pl.pallas_call(
        functools.partial(spread_kernel, own_count, list_len),
        out_shape=jax.ShapeDtypeStruct((frags, CAP) + kept.shape[1:], kept.dtype),
        in_specs=[SMEM, SMEM, VMEM, VMEM],
        out_specs=VMEM,
        name="spread",
    )(where, plan, kept, came)


def collect_kernel(own_count, list_len, where, map_ref, list_ref, came, out):
    me = where[0]
    out[...] = jnp.zeros_like(out)

    def one(fragment, carry):
        count = jnp.int32(0)
        for k in range(list_len):
            row = map_ref[list_ref[fragment, k]]
            hit = row // own_count == me

            @pl.when(hit)
            def _(row=row, count=count):
                out[row % own_count] += came[fragment, count]

            count = count + hit.astype(jnp.int32)
        return carry

    lax.fori_loop(0, list_ref.shape[0], one, 0)


def collect(where, owner_map, vir_list, came, own_count):
    return pl.pallas_call(
        functools.partial(collect_kernel, own_count, vir_list.shape[1]),
        out_shape=jax.ShapeDtypeStruct((own_count,) + came.shape[2:], came.dtype),
        in_specs=[SMEM, SMEM, SMEM, VMEM],
        out_specs=VMEM,
        name="collect",
    )(where, owner_map, vir_list, came)


def body(vir_grid, vir_energy, occ_grid, occ_energy, vir_list, vir_rows, owner_map):
    frags = lax.axis_size("frag")
    aux_count = lax.axis_size("aux")
    me = lax.axis_index("frag").astype(jnp.int32)
    aux = lax.axis_index("aux").astype(jnp.int32)
    own_count, block, width = vir_grid.shape
    list_len = vir_list.shape[1]
    where = jnp.stack([me, aux])
    far_pairs = [(i, i ^ 2) for i in range(aux_count)]
    near_pairs = [(i, i ^ 1) for i in range(aux_count)]

    frag_tail = jnp.pad(vir_energy, ((0, TAIL - own_count), (0, width - block)))
    aux_tail = jnp.pad(occ_grid[0], ((0, TAIL - occ_grid.shape[1]), (0, 0)))
    *outgoing, own, plan = plan_and_pack(
        where, owner_map, vir_list, frag_tail, aux_tail, vir_grid, frags
    )
    arrived = {}
    for index, (distance, parity) in enumerate(ROUNDS):
        payload = outgoing[index]
        if index >= 4:
            payload = lax.optimization_barrier((payload, arrived[index - 3]))[0]
        arrived[index + 1] = lax.ppermute(
            payload, "frag", round_pairs(distance, parity, frags)
        )
    parts = []
    for group in range(list_len // 2):
        if group == 0:
            here = own
        else:
            known = {c: arrived[c] for c in range(1, 4 + group)}
            here = pack_group(2 * group, block, plan, known)
        far = lax.ppermute(here, "aux", far_pairs)
        near = lax.ppermute(here, "aux", near_pairs)
        far_near = lax.ppermute(far, "aux", near_pairs)
        parts += [here, far, near, far_near]
    tail = CAP * block
    energy = jnp.concatenate(
        [vir_energy] + [arrived[c][tail : tail + own_count, :block] for c in sorted(arrived)]
    ).astype(jnp.float32)
    weights = jnp.stack([part[tail:] for part in parts[:4]])
    density = contract(
        where, plan, occ_energy, vir_rows, weights, energy, parts, own_count
    )

    half = block // 2
    quarter = block // aux_count
    side = aux // 2
    sent = lax.dynamic_slice_in_dim(density, (1 - side) * half, half, 1)
    stay = lax.dynamic_slice_in_dim(density, side * half, half, 1)
    both = jnp.concatenate([stay, lax.ppermute(sent, "aux", far_pairs)], axis=0)
    core = aux % 2
    sent = lax.dynamic_slice_in_dim(both, (1 - core) * quarter, quarter, 1)
    kept = lax.dynamic_slice_in_dim(both, core * quarter, quarter, 1)
    came = lax.ppermute(sent, "aux", near_pairs)
    outgoing = spread(where, plan, kept, came, frags, own_count, list_len)
    incoming = lax.all_to_all(outgoing, "frag", 0, 0, tiled=True)
    return collect(where, owner_map, vir_list, incoming, own_count)


def solution(mesh):
    return jax.shard_map(
        body,
        mesh=mesh,
        in_specs=(
            P("frag", None, "aux"),
            P("frag", None),
            P("frag", None, "aux"),
            P("frag", None),
            P(),
            P(),
            P(),
        ),
        out_specs=P("frag", "aux", None),
        check_vma=False,
    )
```

```python
import functools

import jax
import jax.numpy as jnp
from jax import lax
from jax.experimental import pallas as pl
from jax.experimental.pallas import tpu as pltpu
from jax.sharding import PartitionSpec as P

ROUNDS = ((1, 0), (1, 1), (2, 0), (2, 1), (3, 0), (3, 1))
CAP = 2
TAIL = 16
PAIRS = tuple((i, j) for i in range(3) for j in range(i, 3))
MIB = 2**20
ANY = pl.BlockSpec(memory_space=pl.ANY)
SMEM = pl.BlockSpec(memory_space=pltpu.SMEM)
VMEM = pl.BlockSpec(memory_space=pltpu.VMEM)


def round_pairs(distance, parity, frags):
    up = [(i, i + distance) for i in range(frags - distance) if (i // distance) % 2 == parity]
    return up + [(b, a) for a, b in up]


def plan_kernel(
    frags, own_count, list_len, where, map_ref, list_ref, energy, occ, table, *refs
):
    outs, own, plan, sems = refs[:6], refs[6], refs[7], refs[8]
    me = where[0]
    block = table.shape[1]
    copies = []

    def pick(fragment, owner):
        count = jnp.int32(0)
        picked = [jnp.int32(0)] * CAP
        for k in range(list_len):
            row = map_ref[list_ref[fragment, k]]
            hit = row // own_count == owner
            for r in range(CAP):
                picked[r] = jnp.where(hit & (count == r), row % own_count, picked[r])
            count = count + hit.astype(jnp.int32)
        return picked, count

    for index, (distance, parity) in enumerate(ROUNDS):
        up = (me // distance) % 2 == parity
        partner = jnp.where(up, me + distance, me - distance)
        inside = (partner >= 0) & (partner < frags)
        picked, count = pick(jnp.clip(partner, 0, frags - 1), me)
        for r in range(CAP):
            copies.append((
                inside & (count > r),
                pltpu.make_async_copy(
                    table.at[picked[r]], outs[index].at[pl.ds(r * block, block)], sems.at[index, r]
                ),
            ))
        if index == 0:
            picked, count = pick(me, me)
            for r in range(CAP):
                copies.append((
                    count > r,
                    pltpu.make_async_copy(
                        table.at[picked[r]], own.at[pl.ds(r * block, block)], sems.at[6, r]
                    ),
                ))
    for needed, copy in copies:
        pl.when(needed)(copy.start)
    for out in outs + (own,):
        out[pl.ds(CAP * block, TAIL), :] = jnp.zeros((TAIL, out.shape[1]), out.dtype)
    for out in outs:
        out[pl.ds(CAP * block, own_count), pl.ds(0, block)] = energy[...]
    own[pl.ds(CAP * block, occ.shape[0]), :] = occ[...]

    rows, owners, codes, classes = [], [], [], []
    for k in range(list_len):
        row = map_ref[list_ref[me, k]]
        owner = row // own_count
        low = jnp.minimum(me, owner)
        far = jnp.abs(owner - me)
        code = jnp.int32(0)
        for index, (distance, parity) in enumerate(ROUNDS):
            code = jnp.where(
                (far == distance) & ((low // distance) % 2 == parity), index + 1, code
            )
        rows.append(row)
        owners.append(owner)
        codes.append(code)
        classes.append(jnp.where(code == 0, 0, jnp.maximum(code - 3, 1)))
    for k in range(list_len):
        place = jnp.int32(0)
        rank = jnp.int32(0)
        for j in range(list_len):
            if j < k:
                place += (classes[j] <= classes[k]).astype(jnp.int32)
                rank += (owners[j] == owners[k]).astype(jnp.int32)
            elif j > k:
                place += (classes[j] < classes[k]).astype(jnp.int32)
        plan[0, place] = codes[k]
        plan[1, place] = rank
        plan[2, place] = rows[k]
        plan[3, place] = jnp.int32(k)
    for needed, copy in copies:
        pl.when(needed)(copy.wait)


def plan_and_pack(where, owner_map, vir_list, energy, occ, table, frags):
    own_count, block_rows, cols = table.shape
    list_len = vir_list.shape[1]
    part = jax.ShapeDtypeStruct((CAP * block_rows + TAIL, cols), table.dtype)
    return pl.pallas_call(
        functools.partial(plan_kernel, frags, own_count, list_len),
        out_shape=(part,) * 7 + (jax.ShapeDtypeStruct((4, list_len), jnp.int32),),
        in_specs=[SMEM, SMEM, SMEM, VMEM, VMEM, ANY],
        out_specs=(VMEM,) * 7 + (SMEM,),
        scratch_shapes=[pltpu.SemaphoreType.DMA((7, CAP))],
        compiler_params=pltpu.CompilerParams(vmem_limit_bytes=8 * MIB),
        cost_estimate=pl.CostEstimate(
            flops=0, bytes_accessed=4 * 7 * CAP * block_rows * cols, transcendentals=0
        ),
        name="plan_and_pack",
    )(where, owner_map, vir_list, energy, occ, table)


def pack_kernel(first, codes, block, with_energy, plan, *refs):
    count = len(codes)
    if with_energy:
        own_energy, arrived, (out, levels, raw, wide, sems, tail_sems) = (
            refs[0],
            refs[1 : count + 1],
            refs[count + 1 :],
        )
    else:
        arrived, (out, sems) = refs[:count], refs[count:]
    for i in range(2):
        code = plan[0, first + i]
        begin = pl.multiple_of(plan[1, first + i] * block, block)
        rows = pl.ds(i * block, block)
        for source, ref in zip(codes, arrived):

            @pl.when(code == source)
            def _(ref=ref, begin=begin, rows=rows):
                pltpu.make_async_copy(
                    ref.at[pl.ds(begin, block)], out.at[rows], sems.at[i]
                ).start()

    if with_energy:
        own_count = own_energy.shape[0]
        copies = [
            pltpu.make_async_copy(
                ref.at[pl.ds(2 * block, TAIL), pl.ds(0, block)],
                raw.at[pl.ds(n * TAIL, TAIL)],
                tail_sems.at[n],
            )
            for n, ref in enumerate(arrived)
        ]
        for copy in copies:
            copy.start()
        wide[0:own_count, :] = own_energy[...].astype(jnp.float32)
        for copy in copies:
            copy.wait()
        wide[TAIL:, :] = raw[...].astype(jnp.float32)
        for place in range(levels.shape[0]):
            row = plan[0, place] * TAIL + plan[2, place] % own_count
            levels[place : place + 1, :] = wide[pl.ds(row, 1), :]
    for i in range(2):
        rows = pl.ds(i * block, block)
        pltpu.make_async_copy(arrived[0].at[rows], out.at[rows], sems.at[i]).wait()


def pack_group(first, block, plan, arrived, own_energy=None):
    codes = tuple(arrived)
    refs = [arrived[c] for c in codes]
    cols, dtype = refs[0].shape[1], refs[0].dtype
    shapes = [jax.ShapeDtypeStruct((2 * block, cols), dtype)]
    scratch = [pltpu.SemaphoreType.DMA((2,))]
    extra = []
    if own_energy is not None:
        shapes.append(jax.ShapeDtypeStruct((plan.shape[1], block), jnp.float32))
        scratch = [
            pltpu.VMEM((len(codes) * TAIL, block), dtype),
            pltpu.VMEM(((len(codes) + 1) * TAIL, block), jnp.float32),
            *scratch,
            pltpu.SemaphoreType.DMA((len(codes),)),
        ]
        extra = [own_energy]
    return pl.pallas_call(
        functools.partial(pack_kernel, first, codes, block, own_energy is not None),
        out_shape=tuple(shapes),
        in_specs=[SMEM] + [VMEM] * len(extra) + [ANY] * len(refs),
        out_specs=(VMEM,) * len(shapes),
        scratch_shapes=scratch,
        compiler_params=pltpu.CompilerParams(vmem_limit_bytes=4 * MIB),
        cost_estimate=pl.CostEstimate(
            flops=0, bytes_accessed=8 * block * cols, transcendentals=0
        ),
        name="pack_group",
    )(plan, *extra, *refs)


def place_of(aux, b):
    return jnp.where(aux < 2, 2 * aux + b, aux + 2 + 2 * b)


def contract_kernel(stage, block, width, where, plan, levels, rows_ref, energy, *refs):
    groups = stage + 2
    parts, rest = refs[: groups * 4], refs[groups * 4 :]
    if stage == 2:
        before, rest = rest[:2], rest[2:]
        sent, stay, left, grid, occ, scaled, total, amps, tall, dens = rest[:10]
        left_sems, grid_sems, occ_sems = rest[10:]
    else:
        out, left, grid, occ, scaled, total, amps, left_sems, grid_sems, occ_sems = rest
    me, aux = where[0], where[1]
    places = (place_of(aux, 0), place_of(aux, 1))

    def occ_copy(quarter):
        return pltpu.make_async_copy(
            parts[quarter].at[pl.ds(2 * block, TAIL)],
            occ.at[pl.ds(quarter * TAIL, TAIL)],
            occ_sems.at[quarter],
        )

    def left_copy(b, group, begin, quarter):
        return pltpu.make_async_copy(
            parts[group * 4 + quarter].at[pl.ds(begin, block)],
            left.at[pl.ds(b * block, block), pl.ds(quarter * width, width)],
            left_sems.at[b, quarter],
        )

    def grid_copy(slot, group, quarter):
        return pltpu.make_async_copy(
            parts[group * 4 + quarter].at[pl.ds(0, 2 * block)],
            grid.at[pl.ds(slot * 2 * block, 2 * block), pl.ds(quarter * width, width)],
            grid_sems.at[slot, quarter],
        )

    def run(row_count, group_list):
        for quarter in range(4):
            occ_copy(quarter).start()
            for b in range(row_count):
                begin = pl.multiple_of((places[b] % 2) * block, block)
                for group in range(groups):

                    @pl.when(places[b] // 2 == group)
                    def _(b=b, group=group, begin=begin, quarter=quarter):
                        left_copy(b, group, begin, quarter).start()

            for slot, group in enumerate(group_list):
                grid_copy(slot, group, quarter).start()
        height = len(PAIRS) * row_count * block
        span = len(group_list) * 2 * block
        for quarter in range(4):
            cols = pl.ds(quarter * width, width)
            occ_copy(quarter).wait()
            for b in range(row_count):
                left_copy(b, 0, 0, quarter).wait()
            orbit = [
                occ[quarter * TAIL + i : quarter * TAIL + i + 1, :].astype(jnp.float32)
                for i in range(3)
            ]
            for b in range(row_count):
                rows = left[pl.ds(b * block, block), cols].astype(jnp.float32)
                for p, (i, j) in enumerate(PAIRS):
                    scaled[pl.ds((p * row_count + b) * block, block), :] = (
                        rows * (orbit[i] * orbit[j])
                    ).astype(jnp.bfloat16)
            for slot, group in enumerate(group_list):
                grid_copy(slot, group, quarter).wait()

            def rows_step(step, carry, quarter=quarter, cols=cols):
                rows = pl.ds(pl.multiple_of(step * 768, 768), 768)
                term = lax.dot_general(
                    scaled[rows, :],
                    grid[pl.ds(0, span), cols],
                    (((1,), (1,)), ((), ())),
                    preferred_element_type=jnp.float32,
                )
                if quarter == 0:
                    total[rows, pl.ds(0, span)] = term
                else:
                    total[rows, pl.ds(0, span)] += term
                return carry

            lax.fori_loop(0, height // 768, rows_step, 0)
        lane = lax.broadcasted_iota(jnp.int32, (block, block), 1)
        sub = lax.broadcasted_iota(jnp.int32, (block, block), 0)
        sums = []
        for b in range(row_count):
            own_row = energy[pl.ds(places[b], 1), :]
            own_energy = jnp.transpose(jnp.broadcast_to(own_row, (block, block)))
            own_live = sub < rows_ref[me, plan[3, places[b]]]
            for q in range(2 * len(group_list)):
                place = 2 * group_list[q // 2] + q % 2
                their_energy = energy[place : place + 1, :]
                live = own_live & (lane < rows_ref[me, plan[3, place]])
                for p, (i, j) in enumerate(PAIRS):
                    gap = (levels[0, i] + levels[0, j]) - own_energy - their_energy
                    rows = pl.ds((p * row_count + b) * block, block)
                    value = total[rows, pl.ds(q * block, block)]
                    amp = jnp.where(live, value / gap, 0.0).astype(jnp.bfloat16)
                    amps[:, pl.ds(p * span + q * block, block)] = amp
                    if stage == 2:
                        early = amp if b == 0 else jnp.where(aux < 2, amp, jnp.zeros_like(amp))
                        tall[rows, pl.ds(q * block, block)] = early
            wide = amps[:, pl.ds(0, len(PAIRS) * span)]
            sums.append(
                lax.dot_general(
                    wide, wide, (((1,), (1,)), ((), ())), preferred_element_type=jnp.float32
                )
            )
        return sums

    if stage == 0:

        @pl.when(aux < 2)
        def _():
            out[0], out[1] = run(2, (0, 1))

        @pl.when(aux >= 2)
        def _():
            out[...] = jnp.zeros_like(out)
    elif stage == 1:

        @pl.when(aux < 2)
        def _():
            out[0], out[1] = run(2, (2,))

        @pl.when(aux >= 2)
        def _():
            out[0] = run(1, (0, 1, 2))[0]
            out[1] = jnp.zeros(out.shape[1:], out.dtype)
    else:
        sums = run(2, (3,))
        for b in range(2):
            dens[b] = sums[b] + (before[0][b] + before[1][b])
        for q in range(2):
            late = tall[:, pl.ds(q * block, block)]
            dens[2 + q] = lax.dot_general(
                late, late, (((0,), (0,)), ((), ())), preferred_element_type=jnp.float32
            )
        half = block // 2
        side = aux // 2
        stay[...] = dens[:, pl.ds(pl.multiple_of(side * half, half), half), :]
        sent[...] = dens[:, pl.ds(pl.multiple_of((1 - side) * half, half), half), :]


def contract(stage, where, plan, levels, vir_rows, energy, parts, before=()):
    block, width = energy.shape[1], parts[0].shape[1]
    height = len(PAIRS) * 2 * block
    spans = {0: (4, 1), 1: (6, 1), 2: (2, 1)}
    span = spans[stage][0] * block
    scratch = [
        pltpu.VMEM((2 * block, 4 * width), jnp.bfloat16),
        pltpu.VMEM((span, 4 * width), jnp.bfloat16),
        pltpu.VMEM((4 * TAIL, width), jnp.bfloat16),
        pltpu.VMEM((height, width), jnp.bfloat16),
        pltpu.VMEM((height, span), jnp.float32),
        pltpu.VMEM((block, len(PAIRS) * span), jnp.bfloat16),
    ]
    if stage == 2:
        scratch += [
            pltpu.VMEM((height, span), jnp.bfloat16),
            pltpu.VMEM((4, block, block), jnp.float32),
        ]
        out_shape = (jax.ShapeDtypeStruct((4, block // 2, block), jnp.float32),) * 2
        out_specs = (VMEM, VMEM)
    else:
        out_shape = jax.ShapeDtypeStruct((2, block, block), jnp.float32)
        out_specs = VMEM
    scratch += [
        pltpu.SemaphoreType.DMA((2, 4)),
        pltpu.SemaphoreType.DMA((3, 4)),
        pltpu.SemaphoreType.DMA((4,)),
    ]
    return pl.pallas_call(
        functools.partial(contract_kernel, stage, block, width),
        out_shape=out_shape,
        in_specs=[SMEM] * 4 + [VMEM] + [ANY] * len(parts) + [VMEM] * len(before),
        out_specs=out_specs,
        scratch_shapes=scratch,
        compiler_params=pltpu.CompilerParams(vmem_limit_bytes=22 * MIB),
        cost_estimate=pl.CostEstimate(
            flops=2 * height * min(span, 4 * block) * 4 * width,
            bytes_accessed=span * 4 * width * 2,
            transcendentals=0,
        ),
        name="contract",
    )(where, plan, levels, vir_rows, energy, *parts, *before)


def spread_kernel(own_count, where, plan, kept, came, out):
    aux = where[1]
    out[...] = jnp.zeros_like(out)
    holders = (aux, aux ^ 2, aux ^ 1, aux ^ 3)
    late = [kept[4 + q] + came[4 + q] for q in range(2)]
    for index, holder in enumerate(holders):
        source = kept if index < 2 else came
        for b in range(2):
            place = place_of(holder, b)
            value = source[2 * (index % 2) + b]
            if b == 1:
                value += jnp.where(place == 6, late[0], jnp.where(place == 7, late[1], 0.0))
            out[plan[2, place] // own_count, plan[1, place]] = value


def spread(where, plan, kept, came, frags, own_count):
    return pl.pallas_call(
        functools.partial(spread_kernel, own_count),
        out_shape=jax.ShapeDtypeStruct((frags, CAP) + kept.shape[1:], kept.dtype),
        in_specs=[SMEM, SMEM, VMEM, VMEM],
        out_specs=VMEM,
        name="spread",
    )(where, plan, kept, came)


def collect_kernel(own_count, list_len, where, map_ref, list_ref, came, out):
    me = where[0]
    out[...] = jnp.zeros_like(out)

    def one(fragment, carry):
        count = jnp.int32(0)
        for k in range(list_len):
            row = map_ref[list_ref[fragment, k]]
            hit = row // own_count == me

            @pl.when(hit)
            def _(row=row, count=count):
                out[row % own_count] += came[fragment, count]

            count = count + hit.astype(jnp.int32)
        return carry

    lax.fori_loop(0, list_ref.shape[0], one, 0)


def collect(where, owner_map, vir_list, came, own_count):
    return pl.pallas_call(
        functools.partial(collect_kernel, own_count, vir_list.shape[1]),
        out_shape=jax.ShapeDtypeStruct((own_count,) + came.shape[2:], came.dtype),
        in_specs=[SMEM, SMEM, SMEM, VMEM],
        out_specs=VMEM,
        name="collect",
    )(where, owner_map, vir_list, came)


def body(vir_grid, vir_energy, occ_grid, occ_energy, vir_list, vir_rows, owner_map):
    frags = lax.axis_size("frag")
    aux_count = lax.axis_size("aux")
    me = lax.axis_index("frag").astype(jnp.int32)
    aux = lax.axis_index("aux").astype(jnp.int32)
    own_count, block, width = vir_grid.shape
    list_len = vir_list.shape[1]
    where = jnp.stack([me, aux])
    far_pairs = [(i, i ^ 2) for i in range(aux_count)]
    near_pairs = [(i, i ^ 1) for i in range(aux_count)]

    *outgoing, own, plan = plan_and_pack(
        where, owner_map, vir_list, vir_energy, occ_grid[0], vir_grid, frags
    )

    def over_aux(here):
        far = lax.ppermute(here, "aux", far_pairs)
        near = lax.ppermute(here, "aux", near_pairs)
        return [here, far, near, lax.ppermute(far, "aux", near_pairs)]

    def after(value, *others):
        return lax.optimization_barrier((value, *others))[0]

    def send(index, *others):
        distance, parity = ROUNDS[index]
        payload = after(outgoing[index], *others) if others else outgoing[index]
        return lax.ppermute(payload, "frag", round_pairs(distance, parity, frags))

    arrived = {code: send(code - 1) for code in (1, 2, 3, 4)}
    parts = over_aux(own)
    arrived[5] = send(4, *(arrived[c] for c in (1, 2, 3, 4)), parts[1])
    here = pack_group(2, block, plan, {c: arrived[c] for c in range(1, 5)})[0]
    arrived[6] = send(5, arrived[5], here)
    parts += over_aux(here)
    here = pack_group(4, block, plan, {c: arrived[c] for c in range(1, 6)})[0]
    parts += over_aux(here)
    here, energy = pack_group(6, block, plan, arrived, vir_energy)
    parts += over_aux(here)
    shared = (where, plan, occ_energy, vir_rows, energy)
    first = contract(0, *shared, parts[:8])
    second = contract(1, *shared, parts[:12])
    sent, stay = contract(2, *shared, parts, (first, second))

    quarter = block // aux_count
    core = aux % 2
    met = lax.ppermute(sent, "aux", far_pairs)
    both = jnp.concatenate([stay[:2], met[:2], stay[2:] + met[2:]], axis=0)
    sent = lax.dynamic_slice_in_dim(both, (1 - core) * quarter, quarter, 1)
    kept = lax.dynamic_slice_in_dim(both, core * quarter, quarter, 1)
    came = lax.ppermute(sent, "aux", near_pairs)
    outgoing = spread(where, plan, kept, came, frags, own_count)
    incoming = lax.all_to_all(outgoing, "frag", 0, 0, tiled=True)
    return collect(where, owner_map, vir_list, incoming, own_count)


def solution(mesh):
    return jax.shard_map(
        body,
        mesh=mesh,
        in_specs=(
            P("frag", None, "aux"),
            P("frag", None),
            P("frag", None, "aux"),
            P("frag", None),
            P(),
            P(),
            P(),
        ),
        out_specs=P("frag", "aux", None),
        check_vma=False,
    )
```

```python
import functools

import jax
import jax.numpy as jnp
from jax import lax
from jax.experimental import pallas as pl
from jax.experimental.pallas import tpu as pltpu
from jax.sharding import PartitionSpec as P

ROUNDS = ((1, 0), (1, 1), (2, 0), (2, 1), (3, 0), (3, 1))
CAP = 2
TAIL = 16
PAIRS = tuple((i, j) for i in range(3) for j in range(i, 3))
MIB = 2**20
NO_COST = pl.CostEstimate(flops=0, bytes_accessed=0, transcendentals=0)
ANY = pl.BlockSpec(memory_space=pl.ANY)
SMEM = pl.BlockSpec(memory_space=pltpu.SMEM)
VMEM = pl.BlockSpec(memory_space=pltpu.VMEM)


def round_pairs(distance, parity, frags):
    up = [(i, i + distance) for i in range(frags - distance) if (i // distance) % 2 == parity]
    return up + [(b, a) for a, b in up]


def plan_kernel(
    frags, own_count, list_len, where, map_ref, list_ref, energy, occ, table, *refs
):
    outs, own, plan, target, sems = refs[:6], refs[6], refs[7], refs[8], refs[9]
    me = where[0]
    block = table.shape[1]
    copies = []

    def pick(fragment, owner):
        count = jnp.int32(0)
        picked = [jnp.int32(0)] * CAP
        for k in range(list_len):
            row = map_ref[list_ref[fragment, k]]
            hit = row // own_count == owner
            for r in range(CAP):
                picked[r] = jnp.where(hit & (count == r), row % own_count, picked[r])
            count = count + hit.astype(jnp.int32)
        return picked, count

    for index, (distance, parity) in enumerate(ROUNDS):
        up = (me // distance) % 2 == parity
        partner = jnp.where(up, me + distance, me - distance)
        inside = (partner >= 0) & (partner < frags)
        picked, count = pick(jnp.clip(partner, 0, frags - 1), me)
        for r in range(CAP):
            copies.append((
                inside & (count > r),
                pltpu.make_async_copy(
                    table.at[picked[r]], outs[index].at[pl.ds(r * block, block)], sems.at[index, r]
                ),
            ))
        if index == 0:
            picked, count = pick(me, me)
            for r in range(CAP):
                copies.append((
                    count > r,
                    pltpu.make_async_copy(
                        table.at[picked[r]], own.at[pl.ds(r * block, block)], sems.at[6, r]
                    ),
                ))
    for needed, copy in copies:
        pl.when(needed)(copy.start)
    for out in outs + (own,):
        out[pl.ds(CAP * block, TAIL), :] = jnp.zeros((TAIL, out.shape[1]), out.dtype)
    for out in outs:
        out[pl.ds(CAP * block, own_count), pl.ds(0, block)] = energy[...]
    own[pl.ds(CAP * block, occ.shape[0]), :] = occ[...]

    rows, owners, codes, classes = [], [], [], []
    for k in range(list_len):
        row = map_ref[list_ref[me, k]]
        owner = row // own_count
        low = jnp.minimum(me, owner)
        far = jnp.abs(owner - me)
        code = jnp.int32(0)
        for index, (distance, parity) in enumerate(ROUNDS):
            code = jnp.where(
                (far == distance) & ((low // distance) % 2 == parity), index + 1, code
            )
        rows.append(row)
        owners.append(owner)
        codes.append(code)
        classes.append(jnp.where(code == 0, 0, jnp.maximum(code - 3, 1)))
    for k in range(list_len):
        place = jnp.int32(0)
        rank = jnp.int32(0)
        for j in range(list_len):
            if j < k:
                place += (classes[j] <= classes[k]).astype(jnp.int32)
                rank += (owners[j] == owners[k]).astype(jnp.int32)
            elif j > k:
                place += (classes[j] < classes[k]).astype(jnp.int32)
        plan[0, place] = codes[k]
        plan[1, place] = rank
        plan[2, place] = rows[k]
        plan[3, place] = jnp.int32(k)

    def one(fragment, carry):
        picked, _ = pick(fragment, me)
        for r in range(CAP):
            target[fragment, r] = picked[r]
        return carry

    lax.fori_loop(0, frags, one, 0)
    for needed, copy in copies:
        pl.when(needed)(copy.wait)


def plan_and_pack(where, owner_map, vir_list, energy, occ, table, frags):
    own_count, block_rows, cols = table.shape
    list_len = vir_list.shape[1]
    part = jax.ShapeDtypeStruct((CAP * block_rows + TAIL, cols), table.dtype)
    return pl.pallas_call(
        functools.partial(plan_kernel, frags, own_count, list_len),
        out_shape=(part,) * 7
        + (
            jax.ShapeDtypeStruct((4, list_len), jnp.int32),
            jax.ShapeDtypeStruct((frags, CAP), jnp.int32),
        ),
        in_specs=[SMEM, SMEM, SMEM, VMEM, VMEM, ANY],
        out_specs=(VMEM,) * 7 + (SMEM, SMEM),
        scratch_shapes=[pltpu.SemaphoreType.DMA((7, CAP))],
        compiler_params=pltpu.CompilerParams(vmem_limit_bytes=8 * MIB),
        cost_estimate=NO_COST,
        name="plan_and_pack",
    )(where, owner_map, vir_list, energy, occ, table)


def pack_kernel(first, codes, block, with_energy, plan, *refs):
    count = len(codes)
    if with_energy:
        own_energy, arrived, (out, levels, raw, wide, sems, tail_sems) = (
            refs[0],
            refs[1 : count + 1],
            refs[count + 1 :],
        )
    else:
        arrived, (out, sems) = refs[:count], refs[count:]
    for i in range(2):
        code = plan[0, first + i]
        begin = pl.multiple_of(plan[1, first + i] * block, block)
        rows = pl.ds(i * block, block)
        for source, ref in zip(codes, arrived):

            @pl.when(code == source)
            def _(ref=ref, begin=begin, rows=rows):
                pltpu.make_async_copy(
                    ref.at[pl.ds(begin, block)], out.at[rows], sems.at[i]
                ).start()

    if with_energy:
        own_count = own_energy.shape[0]
        copies = [
            pltpu.make_async_copy(
                ref.at[pl.ds(2 * block, TAIL), pl.ds(0, block)],
                raw.at[pl.ds(n * TAIL, TAIL)],
                tail_sems.at[n],
            )
            for n, ref in enumerate(arrived)
        ]
        for copy in copies:
            copy.start()
        wide[0:own_count, :] = own_energy[...].astype(jnp.float32)
        for copy in copies:
            copy.wait()
        wide[TAIL:, :] = raw[...].astype(jnp.float32)
        levels[...] = jnp.zeros_like(levels)
        for place in range(first + 2):
            row = plan[0, place] * TAIL + plan[2, place] % own_count
            levels[place : place + 1, :] = wide[pl.ds(row, 1), :]
    for i in range(2):
        rows = pl.ds(i * block, block)
        pltpu.make_async_copy(arrived[0].at[rows], out.at[rows], sems.at[i]).wait()


def pack_group(first, block, plan, arrived, own_energy=None):
    codes = tuple(arrived)
    refs = [arrived[c] for c in codes]
    cols, dtype = refs[0].shape[1], refs[0].dtype
    shapes = [jax.ShapeDtypeStruct((2 * block, cols), dtype)]
    scratch = [pltpu.SemaphoreType.DMA((2,))]
    extra = []
    if own_energy is not None:
        shapes.append(jax.ShapeDtypeStruct((plan.shape[1], block), jnp.float32))
        scratch = [
            pltpu.VMEM((len(codes) * TAIL, block), dtype),
            pltpu.VMEM(((len(codes) + 1) * TAIL, block), jnp.float32),
            *scratch,
            pltpu.SemaphoreType.DMA((len(codes),)),
        ]
        extra = [own_energy]
    return pl.pallas_call(
        functools.partial(pack_kernel, first, codes, block, own_energy is not None),
        out_shape=tuple(shapes),
        in_specs=[SMEM] + [VMEM] * len(extra) + [ANY] * len(refs),
        out_specs=(VMEM,) * len(shapes),
        scratch_shapes=scratch,
        compiler_params=pltpu.CompilerParams(vmem_limit_bytes=4 * MIB),
        cost_estimate=NO_COST,
        name="pack_group",
    )(plan, *extra, *refs)


def place_of(aux, b):
    return jnp.where(aux < 2, 2 * aux + b, aux + 2 + 2 * b)


def contract_kernel(stage, block, width, where, plan, levels, rows_ref, energy, *refs):
    groups = stage + 2
    parts, rest = refs[: groups * 4], refs[groups * 4 :]
    if stage == 2:
        before, rest = rest[:2], rest[2:]
        sent, stay, left, grid, occ, scaled, total, amps, tall, dens = rest[:10]
        left_sems, grid_sems, occ_sems = rest[10:]
    else:
        out, left, grid, occ, scaled, total, amps, left_sems, grid_sems, occ_sems = rest
    me, aux = where[0], where[1]
    places = (place_of(aux, 0), place_of(aux, 1))

    def occ_copy(quarter):
        return pltpu.make_async_copy(
            parts[quarter].at[pl.ds(2 * block, TAIL)],
            occ.at[pl.ds(quarter * TAIL, TAIL)],
            occ_sems.at[quarter],
        )

    def left_copy(b, group, begin, quarter):
        return pltpu.make_async_copy(
            parts[group * 4 + quarter].at[pl.ds(begin, block)],
            left.at[pl.ds(b * block, block), pl.ds(quarter * width, width)],
            left_sems.at[b, quarter],
        )

    def grid_copy(slot, group, quarter):
        return pltpu.make_async_copy(
            parts[group * 4 + quarter].at[pl.ds(0, 2 * block)],
            grid.at[pl.ds(slot * 2 * block, 2 * block), pl.ds(quarter * width, width)],
            grid_sems.at[slot, quarter],
        )

    def run(row_count, group_list):
        for quarter in range(4):
            occ_copy(quarter).start()
            for b in range(row_count):
                begin = pl.multiple_of((places[b] % 2) * block, block)
                for group in range(groups):

                    @pl.when(places[b] // 2 == group)
                    def _(b=b, group=group, begin=begin, quarter=quarter):
                        left_copy(b, group, begin, quarter).start()

            for slot, group in enumerate(group_list):
                grid_copy(slot, group, quarter).start()
        height = len(PAIRS) * row_count * block
        span = len(group_list) * 2 * block

        def scale(quarter):
            cols = pl.ds(quarter * width, width)
            orbit = [
                occ[quarter * TAIL + i : quarter * TAIL + i + 1, :].astype(jnp.float32)
                for i in range(3)
            ]
            for b in range(row_count):
                rows = left[pl.ds(b * block, block), cols].astype(jnp.float32)
                for p, (i, j) in enumerate(PAIRS):
                    scaled[quarter % 2, pl.ds((p * row_count + b) * block, block), :] = (
                        rows * (orbit[i] * orbit[j])
                    ).astype(jnp.bfloat16)

        def wait_left(quarter):
            occ_copy(quarter).wait()
            for b in range(row_count):
                left_copy(b, 0, 0, quarter).wait()

        wait_left(0)
        scale(0)
        for quarter in range(4):
            cols = pl.ds(quarter * width, width)
            for slot, group in enumerate(group_list):
                grid_copy(slot, group, quarter).wait()
            if quarter < 3:
                wait_left(quarter + 1)
                scale(quarter + 1)
            for step in range(height // 768):
                rows = pl.ds(step * 768, 768)
                term = lax.dot_general(
                    scaled[quarter % 2, rows, :],
                    grid[pl.ds(0, span), cols],
                    (((1,), (1,)), ((), ())),
                    preferred_element_type=jnp.float32,
                )
                if quarter == 0:
                    total[rows, pl.ds(0, span)] = term
                else:
                    total[rows, pl.ds(0, span)] += term
        lane = lax.broadcasted_iota(jnp.int32, (block, block), 1)
        sub = lax.broadcasted_iota(jnp.int32, (block, block), 0)
        sums = []
        for b in range(row_count):
            own_row = energy[pl.ds(places[b], 1), :]
            own_energy = jnp.transpose(jnp.broadcast_to(own_row, (block, block)))
            own_live = sub < rows_ref[me, plan[3, places[b]]]
            for q in range(2 * len(group_list)):
                place = 2 * group_list[q // 2] + q % 2
                their_energy = energy[place : place + 1, :]
                live = own_live & (lane < rows_ref[me, plan[3, place]])
                for p, (i, j) in enumerate(PAIRS):
                    gap = (levels[0, i] + levels[0, j]) - own_energy - their_energy
                    rows = pl.ds((p * row_count + b) * block, block)
                    value = total[rows, pl.ds(q * block, block)]
                    amp = jnp.where(live, value / gap, 0.0).astype(jnp.bfloat16)
                    amps[:, pl.ds(p * span + q * block, block)] = amp
                    if stage == 2:
                        early = amp if b == 0 else jnp.where(aux < 2, amp, jnp.zeros_like(amp))
                        tall[rows, pl.ds(q * block, block)] = early
            wide = amps[:, pl.ds(0, len(PAIRS) * span)]
            sums.append(
                lax.dot_general(
                    wide, wide, (((1,), (1,)), ((), ())), preferred_element_type=jnp.float32
                )
            )
        return sums

    if stage == 0:

        @pl.when(aux < 2)
        def _():
            out[0], out[1] = run(2, (0, 1))

        @pl.when(aux >= 2)
        def _():
            out[...] = jnp.zeros_like(out)
    elif stage == 1:

        @pl.when(aux < 2)
        def _():
            out[0], out[1] = run(2, (2,))

        @pl.when(aux >= 2)
        def _():
            out[0] = run(1, (0, 1, 2))[0]
            out[1] = jnp.zeros(out.shape[1:], out.dtype)
    else:
        sums = run(2, (3,))
        for b in range(2):
            dens[b] = sums[b] + (before[0][b] + before[1][b])
        for q in range(2):
            late = tall[:, pl.ds(q * block, block)]
            dens[2 + q] = lax.dot_general(
                late, late, (((0,), (0,)), ((), ())), preferred_element_type=jnp.float32
            )
        half = block // 2
        side = aux // 2
        stay[...] = dens[:, pl.ds(pl.multiple_of(side * half, half), half), :]
        sent[...] = dens[:, pl.ds(pl.multiple_of((1 - side) * half, half), half), :]


def contract(stage, where, plan, levels, vir_rows, energy, parts, before=()):
    block, width = energy.shape[1], parts[0].shape[1]
    height = len(PAIRS) * 2 * block
    spans = {0: (4, 1), 1: (6, 1), 2: (2, 1)}
    span = spans[stage][0] * block
    scratch = [
        pltpu.VMEM((2 * block, 4 * width), jnp.bfloat16),
        pltpu.VMEM((span, 4 * width), jnp.bfloat16),
        pltpu.VMEM((4 * TAIL, width), jnp.bfloat16),
        pltpu.VMEM((2, height, width), jnp.bfloat16),
        pltpu.VMEM((height, span), jnp.float32),
        pltpu.VMEM((block, len(PAIRS) * span), jnp.bfloat16),
    ]
    if stage == 2:
        scratch += [
            pltpu.VMEM((height, span), jnp.bfloat16),
            pltpu.VMEM((4, block, block), jnp.float32),
        ]
        out_shape = (jax.ShapeDtypeStruct((4, block // 2, block), jnp.float32),) * 2
        out_specs = (VMEM, VMEM)
    else:
        out_shape = jax.ShapeDtypeStruct((2, block, block), jnp.float32)
        out_specs = VMEM
    scratch += [
        pltpu.SemaphoreType.DMA((2, 4)),
        pltpu.SemaphoreType.DMA((3, 4)),
        pltpu.SemaphoreType.DMA((4,)),
    ]
    cost = NO_COST
    if stage < 2:
        units = (8, 6)[stage] * len(PAIRS) * block * block
        cost = pl.CostEstimate(
            flops=2 * units * 4 * width, bytes_accessed=units * 4, transcendentals=0
        )
    return pl.pallas_call(
        functools.partial(contract_kernel, stage, block, width),
        out_shape=out_shape,
        in_specs=[SMEM] * 4 + [VMEM] + [ANY] * len(parts) + [VMEM] * len(before),
        out_specs=out_specs,
        scratch_shapes=scratch,
        compiler_params=pltpu.CompilerParams(vmem_limit_bytes=26 * MIB),
        cost_estimate=cost,
        name="contract",
    )(where, plan, levels, vir_rows, energy, *parts, *before)


def spread_kernel(own_count, where, plan, kept, came, out):
    aux = where[1]
    out[...] = jnp.zeros_like(out)
    holders = (aux, aux ^ 2, aux ^ 1, aux ^ 3)
    late = [kept[4 + q] + came[4 + q] for q in range(2)]
    for index, holder in enumerate(holders):
        source = kept if index < 2 else came
        for b in range(2):
            place = place_of(holder, b)
            value = source[2 * (index % 2) + b]
            if b == 1:
                value += jnp.where(place == 6, late[0], jnp.where(place == 7, late[1], 0.0))
            out[plan[2, place] // own_count, plan[1, place]] = value


def spread(where, plan, kept, came, frags, own_count):
    return pl.pallas_call(
        functools.partial(spread_kernel, own_count),
        out_shape=jax.ShapeDtypeStruct((frags, CAP) + kept.shape[1:], kept.dtype),
        in_specs=[SMEM, SMEM, VMEM, VMEM],
        out_specs=VMEM,
        name="spread",
    )(where, plan, kept, came)


def collect_kernel(target, came, out):
    out[...] = jnp.zeros_like(out)

    def one(fragment, carry):
        for r in range(CAP):
            out[target[fragment, r]] += came[fragment, r]
        return carry

    lax.fori_loop(0, came.shape[0], one, 0)


def collect(target, came, own_count):
    return pl.pallas_call(
        collect_kernel,
        out_shape=jax.ShapeDtypeStruct((own_count,) + came.shape[2:], came.dtype),
        in_specs=[SMEM, VMEM],
        out_specs=VMEM,
        name="collect",
    )(target, came)


def body(vir_grid, vir_energy, occ_grid, occ_energy, vir_list, vir_rows, owner_map):
    frags = lax.axis_size("frag")
    aux_count = lax.axis_size("aux")
    me = lax.axis_index("frag").astype(jnp.int32)
    aux = lax.axis_index("aux").astype(jnp.int32)
    own_count, block, width = vir_grid.shape
    list_len = vir_list.shape[1]
    where = jnp.stack([me, aux])
    far_pairs = [(i, i ^ 2) for i in range(aux_count)]
    near_pairs = [(i, i ^ 1) for i in range(aux_count)]

    *outgoing, own, plan, target = plan_and_pack(
        where, owner_map, vir_list, vir_energy, occ_grid[0], vir_grid, frags
    )

    def over_aux(here, *others):
        far = lax.ppermute(here, "aux", far_pairs)
        near = lax.ppermute(here, "aux", near_pairs)
        onward = after(far, *others) if others else far
        return [here, far, near, lax.ppermute(onward, "aux", near_pairs)]

    def after(value, *others):
        return lax.optimization_barrier((value, *others))[0]

    def send(index, *others):
        distance, parity = ROUNDS[index]
        payload = after(outgoing[index], *others) if others else outgoing[index]
        return lax.ppermute(payload, "frag", round_pairs(distance, parity, frags))

    arrived = {code: send(code - 1) for code in (1, 2, 3, 4)}
    parts = over_aux(own)
    arrived[5] = send(4, *(arrived[c] for c in (1, 2, 3, 4)), parts[1])
    here = pack_group(2, block, plan, {c: arrived[c] for c in range(1, 5)})[0]
    parts += over_aux(here)
    arrived[6] = send(5, arrived[5], parts[5])
    here, early_energy = pack_group(
        4, block, plan, {c: arrived[c] for c in range(1, 6)}, vir_energy
    )
    shared = (where, plan, occ_energy, vir_rows)
    first = contract(0, *shared, early_energy, parts[:8])
    parts += over_aux(here, first)
    arrived[6] = after(arrived[6], first)
    here, energy = pack_group(6, block, plan, arrived, vir_energy)
    second = contract(1, *shared, early_energy, parts[:12])
    parts += over_aux(here, second)
    sent, stay = contract(2, *shared, energy, parts, (first, second))

    quarter = block // aux_count
    core = aux % 2
    met = lax.ppermute(sent, "aux", far_pairs)
    both = jnp.concatenate([stay[:2], met[:2], stay[2:] + met[2:]], axis=0)
    sent = lax.dynamic_slice_in_dim(both, (1 - core) * quarter, quarter, 1)
    kept = lax.dynamic_slice_in_dim(both, core * quarter, quarter, 1)
    came = lax.ppermute(sent, "aux", near_pairs)
    outgoing = spread(where, plan, kept, came, frags, own_count)
    incoming = lax.all_to_all(outgoing, "frag", 0, 0, tiled=True)
    return collect(target, incoming, own_count)


def solution(mesh):
    return jax.shard_map(
        body,
        mesh=mesh,
        in_specs=(
            P("frag", None, "aux"),
            P("frag", None),
            P("frag", None, "aux"),
            P("frag", None),
            P(),
            P(),
            P(),
        ),
        out_specs=P("frag", "aux", None),
        check_vma=False,
    )
```

```python
import functools

import jax
import jax.numpy as jnp
from jax import lax
from jax.experimental import pallas as pl
from jax.experimental.pallas import tpu as pltpu
from jax.sharding import PartitionSpec as P

ROUNDS = ((1, 0), (1, 1), (2, 0), (2, 1), (3, 0), (3, 1))
CAP = 2
TAIL = 16
PAIRS = tuple((i, j) for i in range(3) for j in range(i, 3))
MIB = 2**20
NO_COST = pl.CostEstimate(flops=0, bytes_accessed=0, transcendentals=0)
ANY = pl.BlockSpec(memory_space=pl.ANY)
SMEM = pl.BlockSpec(memory_space=pltpu.SMEM)
VMEM = pl.BlockSpec(memory_space=pltpu.VMEM)


def round_pairs(distance, parity, frags):
    up = [(i, i + distance) for i in range(frags - distance) if (i // distance) % 2 == parity]
    return up + [(b, a) for a, b in up]


def pick(map_ref, list_ref, list_len, own_count, fragment, owner):
    count = jnp.int32(0)
    picked = [jnp.int32(0)] * CAP
    for k in range(list_len):
        row = map_ref[list_ref[fragment, k]]
        hit = row // own_count == owner
        for r in range(CAP):
            picked[r] = jnp.where(hit & (count == r), row % own_count, picked[r])
        count = count + hit.astype(jnp.int32)
    return picked, count


def send_kernel(frags, own_count, list_len, where, map_ref, list_ref, energy, occ, table, *refs):
    outs, own, sems = refs[:6], refs[6], refs[7]
    me = where[0]
    block = table.shape[1]
    copies = []

    def start(out, index, fragment, inside):
        picked, count = pick(map_ref, list_ref, list_len, own_count, fragment, me)
        for r in range(CAP):
            copy = pltpu.make_async_copy(
                table.at[picked[r]], out.at[pl.ds(r * block, block)], sems.at[index, r]
            )
            needed = inside & (count > r)
            pl.when(needed)(copy.start)
            copies.append((needed, copy))

    for index, (distance, parity) in enumerate(ROUNDS):
        up = (me // distance) % 2 == parity
        partner = jnp.where(up, me + distance, me - distance)
        inside = (partner >= 0) & (partner < frags)
        start(outs[index], index, jnp.clip(partner, 0, frags - 1), inside)
    start(own, 6, me, me >= 0)
    for out in outs + (own,):
        out[pl.ds(CAP * block, TAIL), :] = jnp.zeros((TAIL, out.shape[1]), out.dtype)
    for out in outs:
        out[pl.ds(CAP * block, own_count), pl.ds(0, block)] = energy[...]
    own[pl.ds(CAP * block, occ.shape[0]), :] = occ[...]
    for needed, copy in copies:
        pl.when(needed)(copy.wait)


def pack_to_send(where, owner_map, vir_list, energy, occ, table, frags):
    own_count, block_rows, cols = table.shape
    list_len = vir_list.shape[1]
    part = jax.ShapeDtypeStruct((CAP * block_rows + TAIL, cols), table.dtype)
    return pl.pallas_call(
        functools.partial(send_kernel, frags, own_count, list_len),
        out_shape=(part,) * 7,
        in_specs=[SMEM, SMEM, SMEM, VMEM, VMEM, ANY],
        out_specs=(VMEM,) * 7,
        scratch_shapes=[pltpu.SemaphoreType.DMA((7, CAP))],
        compiler_params=pltpu.CompilerParams(vmem_limit_bytes=8 * MIB),
        cost_estimate=NO_COST,
        name="pack_to_send",
    )(where, owner_map, vir_list, energy, occ, table)


def plan_kernel(frags, own_count, list_len, where, map_ref, list_ref, plan, target):
    me = where[0]
    rows, owners, codes, classes = [], [], [], []
    for k in range(list_len):
        row = map_ref[list_ref[me, k]]
        owner = row // own_count
        low = jnp.minimum(me, owner)
        far = jnp.abs(owner - me)
        code = jnp.int32(0)
        for index, (distance, parity) in enumerate(ROUNDS):
            code = jnp.where(
                (far == distance) & ((low // distance) % 2 == parity), index + 1, code
            )
        rows.append(row)
        owners.append(owner)
        codes.append(code)
        classes.append(jnp.where(code == 0, 0, jnp.maximum(code - 3, 1)))
    for k in range(list_len):
        place = jnp.int32(0)
        rank = jnp.int32(0)
        for j in range(list_len):
            if j < k:
                place += (classes[j] <= classes[k]).astype(jnp.int32)
                rank += (owners[j] == owners[k]).astype(jnp.int32)
            elif j > k:
                place += (classes[j] < classes[k]).astype(jnp.int32)
        plan[0, place] = codes[k]
        plan[1, place] = rank
        plan[2, place] = rows[k]
        plan[3, place] = jnp.int32(k)

    def one(fragment, carry):
        picked, _ = pick(map_ref, list_ref, list_len, own_count, fragment, me)
        for r in range(CAP):
            target[fragment, r] = picked[r]
        return carry

    lax.fori_loop(0, frags, one, 0)


def plan_lists(where, owner_map, vir_list, own_count, frags):
    list_len = vir_list.shape[1]
    return pl.pallas_call(
        functools.partial(plan_kernel, frags, own_count, list_len),
        out_shape=(
            jax.ShapeDtypeStruct((4, list_len), jnp.int32),
            jax.ShapeDtypeStruct((frags, CAP), jnp.int32),
        ),
        in_specs=[SMEM, SMEM, SMEM],
        out_specs=(SMEM, SMEM),
        compiler_params=pltpu.CompilerParams(vmem_limit_bytes=4 * MIB),
        cost_estimate=NO_COST,
        name="plan_lists",
    )(where, owner_map, vir_list)


def pack_kernel(first, codes, block, with_energy, plan, *refs):
    count = len(codes)
    if with_energy:
        own_energy, arrived, (out, levels, raw, wide, sems, tail_sems) = (
            refs[0],
            refs[1 : count + 1],
            refs[count + 1 :],
        )
    else:
        arrived, (out, sems) = refs[:count], refs[count:]
    for i in range(2):
        code = plan[0, first + i]
        begin = pl.multiple_of(plan[1, first + i] * block, block)
        rows = pl.ds(i * block, block)
        for source, ref in zip(codes, arrived):

            @pl.when(code == source)
            def _(ref=ref, begin=begin, rows=rows):
                pltpu.make_async_copy(
                    ref.at[pl.ds(begin, block)], out.at[rows], sems.at[i]
                ).start()

    if with_energy:
        own_count = own_energy.shape[0]
        copies = [
            pltpu.make_async_copy(
                ref.at[pl.ds(2 * block, TAIL), pl.ds(0, block)],
                raw.at[pl.ds(n * TAIL, TAIL)],
                tail_sems.at[n],
            )
            for n, ref in enumerate(arrived)
        ]
        for copy in copies:
            copy.start()
        wide[0:own_count, :] = own_energy[...].astype(jnp.float32)
        for copy in copies:
            copy.wait()
        wide[TAIL:, :] = raw[...].astype(jnp.float32)
        levels[...] = jnp.zeros_like(levels)
        for place in range(first + 2):
            row = plan[0, place] * TAIL + plan[2, place] % own_count
            levels[place : place + 1, :] = wide[pl.ds(row, 1), :]
    for i in range(2):
        rows = pl.ds(i * block, block)
        pltpu.make_async_copy(arrived[0].at[rows], out.at[rows], sems.at[i]).wait()


def pack_group(first, block, plan, arrived, own_energy=None):
    codes = tuple(arrived)
    refs = [arrived[c] for c in codes]
    cols, dtype = refs[0].shape[1], refs[0].dtype
    shapes = [jax.ShapeDtypeStruct((2 * block, cols), dtype)]
    scratch = [pltpu.SemaphoreType.DMA((2,))]
    extra = []
    if own_energy is not None:
        shapes.append(jax.ShapeDtypeStruct((plan.shape[1], block), jnp.float32))
        scratch = [
            pltpu.VMEM((len(codes) * TAIL, block), dtype),
            pltpu.VMEM(((len(codes) + 1) * TAIL, block), jnp.float32),
            *scratch,
            pltpu.SemaphoreType.DMA((len(codes),)),
        ]
        extra = [own_energy]
    return pl.pallas_call(
        functools.partial(pack_kernel, first, codes, block, own_energy is not None),
        out_shape=tuple(shapes),
        in_specs=[SMEM] + [VMEM] * len(extra) + [ANY] * len(refs),
        out_specs=(VMEM,) * len(shapes),
        scratch_shapes=scratch,
        compiler_params=pltpu.CompilerParams(vmem_limit_bytes=4 * MIB),
        cost_estimate=NO_COST,
        name="pack_group",
    )(plan, *extra, *refs)


def place_of(aux, b):
    return jnp.where(aux < 2, 2 * aux + b, aux + 2 + 2 * b)


def contract_kernel(stage, block, width, where, plan, levels, rows_ref, energy, *refs):
    groups = min(stage + 2, 4)
    parts, rest = refs[: groups * 4], refs[groups * 4 :]
    quarters = {2: (0, 2), 3: (1, 3)}.get(stage, (0, 1, 2, 3))
    partial = None
    if stage == 2:
        total, left, grid, occ, scaled, left_sems, grid_sems, occ_sems = rest
    elif stage == 3:
        before, partial, rest = rest[:2], rest[2], rest[3:]
        sent, stay, left, grid, occ, scaled, total, amps, tall, dens = rest[:10]
        left_sems, grid_sems, occ_sems = rest[10:]
    else:
        out, left, grid, occ, scaled, total, amps, left_sems, grid_sems, occ_sems = rest
    me, aux = where[0], where[1]
    places = (place_of(aux, 0), place_of(aux, 1))

    def occ_copy(quarter):
        return pltpu.make_async_copy(
            parts[quarter].at[pl.ds(2 * block, TAIL)],
            occ.at[pl.ds(quarter * TAIL, TAIL)],
            occ_sems.at[quarter],
        )

    def left_copy(b, group, begin, quarter):
        return pltpu.make_async_copy(
            parts[group * 4 + quarter].at[pl.ds(begin, block)],
            left.at[pl.ds(b * block, block), pl.ds(quarter * width, width)],
            left_sems.at[b, quarter],
        )

    def grid_copy(slot, group, quarter):
        return pltpu.make_async_copy(
            parts[group * 4 + quarter].at[pl.ds(0, 2 * block)],
            grid.at[pl.ds(slot * 2 * block, 2 * block), pl.ds(quarter * width, width)],
            grid_sems.at[slot, quarter],
        )

    def run(row_count, group_list):
        for quarter in quarters:
            occ_copy(quarter).start()
            for b in range(row_count):
                begin = pl.multiple_of((places[b] % 2) * block, block)
                for group in range(groups):

                    @pl.when(places[b] // 2 == group)
                    def _(b=b, group=group, begin=begin, quarter=quarter):
                        left_copy(b, group, begin, quarter).start()

            for slot, group in enumerate(group_list):
                grid_copy(slot, group, quarter).start()
        height = len(PAIRS) * row_count * block
        span = len(group_list) * 2 * block

        def scale(turn):
            quarter = quarters[turn]
            cols = pl.ds(quarter * width, width)
            orbit = [
                occ[quarter * TAIL + i : quarter * TAIL + i + 1, :].astype(jnp.float32)
                for i in range(3)
            ]
            for b in range(row_count):
                rows = left[pl.ds(b * block, block), cols].astype(jnp.float32)
                for p, (i, j) in enumerate(PAIRS):
                    scaled[turn % 2, pl.ds((p * row_count + b) * block, block), :] = (
                        rows * (orbit[i] * orbit[j])
                    ).astype(jnp.bfloat16)

        def wait_left(turn):
            quarter = quarters[turn]
            occ_copy(quarter).wait()
            for b in range(row_count):
                left_copy(b, 0, 0, quarter).wait()

        wait_left(0)
        scale(0)
        for turn, quarter in enumerate(quarters):
            cols = pl.ds(quarter * width, width)
            for slot, group in enumerate(group_list):
                grid_copy(slot, group, quarter).wait()
            if turn + 1 < len(quarters):
                wait_left(turn + 1)
                scale(turn + 1)
            for step in range(height // 768):
                rows = pl.ds(step * 768, 768)
                term = lax.dot_general(
                    scaled[turn % 2, rows, :],
                    grid[pl.ds(0, span), cols],
                    (((1,), (1,)), ((), ())),
                    preferred_element_type=jnp.float32,
                )
                if turn:
                    total[rows, pl.ds(0, span)] += term
                elif partial is not None:
                    total[rows, pl.ds(0, span)] = term + partial[rows, :]
                else:
                    total[rows, pl.ds(0, span)] = term
        if stage == 2:
            return None
        lane = lax.broadcasted_iota(jnp.int32, (block, block), 1)
        sub = lax.broadcasted_iota(jnp.int32, (block, block), 0)
        sums = []
        for b in range(row_count):
            own_row = energy[pl.ds(places[b], 1), :]
            own_energy = jnp.transpose(jnp.broadcast_to(own_row, (block, block)))
            own_live = sub < rows_ref[me, plan[3, places[b]]]
            for q in range(2 * len(group_list)):
                place = 2 * group_list[q // 2] + q % 2
                their_energy = energy[place : place + 1, :]
                live = own_live & (lane < rows_ref[me, plan[3, place]])
                for p, (i, j) in enumerate(PAIRS):
                    gap = (levels[0, i] + levels[0, j]) - own_energy - their_energy
                    rows = pl.ds((p * row_count + b) * block, block)
                    value = total[rows, pl.ds(q * block, block)]
                    amp = jnp.where(live, value / gap, 0.0).astype(jnp.bfloat16)
                    amps[:, pl.ds(p * span + q * block, block)] = amp
                    if stage == 3:
                        early = amp if b == 0 else jnp.where(aux < 2, amp, jnp.zeros_like(amp))
                        tall[rows, pl.ds(q * block, block)] = early
            wide = amps[:, pl.ds(0, len(PAIRS) * span)]
            sums.append(
                lax.dot_general(
                    wide, wide, (((1,), (1,)), ((), ())), preferred_element_type=jnp.float32
                )
            )
        return sums

    if stage == 0:

        @pl.when(aux < 2)
        def _():
            out[0], out[1] = run(2, (0, 1))

        @pl.when(aux >= 2)
        def _():
            out[...] = jnp.zeros_like(out)
    elif stage == 1:

        @pl.when(aux < 2)
        def _():
            out[0], out[1] = run(2, (2,))

        @pl.when(aux >= 2)
        def _():
            out[0] = run(1, (0, 1, 2))[0]
            out[1] = jnp.zeros(out.shape[1:], out.dtype)
    elif stage == 2:
        run(2, (3,))
    else:
        sums = run(2, (3,))
        for b in range(2):
            dens[b] = sums[b] + (before[0][b] + before[1][b])
        for q in range(2):
            late = tall[:, pl.ds(q * block, block)]
            dens[2 + q] = lax.dot_general(
                late, late, (((0,), (0,)), ((), ())), preferred_element_type=jnp.float32
            )
        half = block // 2
        side = aux // 2
        stay[...] = dens[:, pl.ds(pl.multiple_of(side * half, half), half), :]
        sent[...] = dens[:, pl.ds(pl.multiple_of((1 - side) * half, half), half), :]


def contract(stage, where, plan, levels, vir_rows, energy, parts, before=()):
    block, width = energy.shape[1], parts[0].shape[1]
    height = len(PAIRS) * 2 * block
    span = (4, 6, 2, 2)[stage] * block
    scratch = [
        pltpu.VMEM((2 * block, 4 * width), jnp.bfloat16),
        pltpu.VMEM((span, 4 * width), jnp.bfloat16),
        pltpu.VMEM((4 * TAIL, width), jnp.bfloat16),
        pltpu.VMEM((2, height, width), jnp.bfloat16),
    ]
    if stage != 2:
        scratch += [
            pltpu.VMEM((height, span), jnp.float32),
            pltpu.VMEM((block, len(PAIRS) * span), jnp.bfloat16),
        ]
    out_specs = VMEM
    if stage == 3:
        scratch += [
            pltpu.VMEM((height, span), jnp.bfloat16),
            pltpu.VMEM((4, block, block), jnp.float32),
        ]
        out_shape = (jax.ShapeDtypeStruct((4, block // 2, block), jnp.float32),) * 2
        out_specs = (VMEM, VMEM)
    elif stage == 2:
        out_shape = jax.ShapeDtypeStruct((height, span), jnp.float32)
    else:
        out_shape = jax.ShapeDtypeStruct((2, block, block), jnp.float32)
    scratch += [
        pltpu.SemaphoreType.DMA((2, 4)),
        pltpu.SemaphoreType.DMA((3, 4)),
        pltpu.SemaphoreType.DMA((4,)),
    ]
    cost = NO_COST
    if stage in (1, 2):
        units = (8, 6, 2)[stage] * len(PAIRS) * block * block
        cost = pl.CostEstimate(
            flops=2 * units * 4 * width, bytes_accessed=units * 4, transcendentals=0
        )
    return pl.pallas_call(
        functools.partial(contract_kernel, stage, block, width),
        out_shape=out_shape,
        in_specs=[SMEM] * 4 + [VMEM] + [ANY] * len(parts) + [VMEM] * len(before),
        out_specs=out_specs,
        scratch_shapes=scratch,
        compiler_params=pltpu.CompilerParams(vmem_limit_bytes=26 * MIB),
        cost_estimate=cost,
        name="contract",
    )(where, plan, levels, vir_rows, energy, *parts, *before)


def spread_kernel(own_count, where, plan, kept, came, out):
    aux = where[1]
    out[...] = jnp.zeros_like(out)
    holders = (aux, aux ^ 2, aux ^ 1, aux ^ 3)
    late = [kept[4 + q] + came[4 + q] for q in range(2)]
    for index, holder in enumerate(holders):
        source = kept if index < 2 else came
        for b in range(2):
            place = place_of(holder, b)
            value = source[2 * (index % 2) + b]
            if b == 1:
                value += jnp.where(place == 6, late[0], jnp.where(place == 7, late[1], 0.0))
            out[plan[2, place] // own_count, plan[1, place]] = value


def spread(where, plan, kept, came, frags, own_count):
    return pl.pallas_call(
        functools.partial(spread_kernel, own_count),
        out_shape=jax.ShapeDtypeStruct((frags, CAP) + kept.shape[1:], kept.dtype),
        in_specs=[SMEM, SMEM, VMEM, VMEM],
        out_specs=VMEM,
        compiler_params=pltpu.CompilerParams(vmem_limit_bytes=4 * MIB),
        name="spread",
    )(where, plan, kept, came)


def collect_kernel(target, came, out):
    out[...] = jnp.zeros_like(out)

    def one(fragment, carry):
        for r in range(CAP):
            out[target[fragment, r]] += came[fragment, r]
        return carry

    lax.fori_loop(0, came.shape[0], one, 0)


def collect(target, came, own_count):
    return pl.pallas_call(
        collect_kernel,
        out_shape=jax.ShapeDtypeStruct((own_count,) + came.shape[2:], came.dtype),
        in_specs=[SMEM, VMEM],
        out_specs=VMEM,
        compiler_params=pltpu.CompilerParams(vmem_limit_bytes=4 * MIB),
        name="collect",
    )(target, came)


def body(vir_grid, vir_energy, occ_grid, occ_energy, vir_list, vir_rows, owner_map):
    frags = lax.axis_size("frag")
    aux_count = lax.axis_size("aux")
    me = lax.axis_index("frag").astype(jnp.int32)
    aux = lax.axis_index("aux").astype(jnp.int32)
    own_count, block, width = vir_grid.shape
    list_len = vir_list.shape[1]
    where = jnp.stack([me, aux])
    far_pairs = [(i, i ^ 2) for i in range(aux_count)]
    near_pairs = [(i, i ^ 1) for i in range(aux_count)]

    *outgoing, own = pack_to_send(
        where, owner_map, vir_list, vir_energy, occ_grid[0], vir_grid, frags
    )

    def over_aux(here, *others):
        far = lax.ppermute(here, "aux", far_pairs)
        near = lax.ppermute(here, "aux", near_pairs)
        onward = after(far, *others) if others else far
        return [here, far, near, lax.ppermute(onward, "aux", near_pairs)]

    def after(value, *others):
        return lax.optimization_barrier((value, *others))[0]

    def send(index, *others):
        distance, parity = ROUNDS[index]
        payload = after(outgoing[index], *others) if others else outgoing[index]
        return lax.ppermute(payload, "frag", round_pairs(distance, parity, frags))

    arrived = {code: send(code - 1) for code in (1, 2, 3, 4)}
    parts = over_aux(own)
    arrived[5] = send(4, arrived[3], arrived[4])
    plan, target = plan_lists(
        after(where, arrived[3]), owner_map, vir_list, own_count, frags
    )
    arrived[6] = send(5, arrived[5])
    known = {c: arrived[c] for c in range(1, 6)}
    here = pack_group(2, block, plan, known)[0]
    parts += over_aux(here)
    here, early_energy = pack_group(4, block, plan, known, vir_energy)
    here = after(here, parts[5])
    shared = (where, plan, occ_energy, vir_rows)
    first = contract(0, *shared, early_energy, parts[:8])
    parts += over_aux(here, first)
    arrived[6] = after(arrived[6], first)
    here, energy = pack_group(6, block, plan, arrived, vir_energy)
    here = after(here, parts[9])
    second = contract(1, *shared, early_energy, parts[:12])
    near = lax.ppermute(here, "aux", near_pairs)
    partial = contract(2, *shared, energy, parts + [here, here, near, near])
    far = lax.ppermute(here, "aux", far_pairs)
    far_near = lax.ppermute(after(far, second, partial), "aux", near_pairs)
    parts += [here, far, near, far_near]
    sent, stay = contract(3, *shared, energy, parts, (first, second, partial))

    quarter = block // aux_count
    core = aux % 2
    met = lax.ppermute(sent, "aux", far_pairs)
    both = jnp.concatenate([stay[:2], met[:2], stay[2:] + met[2:]], axis=0)
    sent = lax.dynamic_slice_in_dim(both, (1 - core) * quarter, quarter, 1)
    kept = lax.dynamic_slice_in_dim(both, core * quarter, quarter, 1)
    came = lax.ppermute(sent, "aux", near_pairs)
    outgoing = spread(where, plan, kept, came, frags, own_count)
    incoming = lax.all_to_all(outgoing, "frag", 0, 0, tiled=True)
    return collect(target, incoming, own_count)


def solution(mesh):
    return jax.shard_map(
        body,
        mesh=mesh,
        in_specs=(
            P("frag", None, "aux"),
            P("frag", None),
            P("frag", None, "aux"),
            P("frag", None),
            P(),
            P(),
            P(),
        ),
        out_specs=P("frag", "aux", None),
        check_vma=False,
    )
```

```python
import functools

import jax
import jax.numpy as jnp
from jax import lax
from jax.experimental import pallas as pl
from jax.experimental.pallas import tpu as pltpu
from jax.sharding import PartitionSpec as P

ROUNDS = ((1, 0), (1, 1), (2, 0), (2, 1), (3, 0), (3, 1))
CAP = 2
TAIL = 16
PAIRS = tuple((i, j) for i in range(3) for j in range(i, 3))
MIB = 2**20
NO_COST = pl.CostEstimate(flops=0, bytes_accessed=0, transcendentals=0)
ANY = pl.BlockSpec(memory_space=pl.ANY)
SMEM = pl.BlockSpec(memory_space=pltpu.SMEM)
VMEM = pl.BlockSpec(memory_space=pltpu.VMEM)


def round_pairs(distance, parity, frags):
    up = [(i, i + distance) for i in range(frags - distance) if (i // distance) % 2 == parity]
    return up + [(b, a) for a, b in up]


def pick(map_ref, list_ref, list_len, own_count, fragment, owner):
    count = jnp.int32(0)
    picked = [jnp.int32(0)] * CAP
    for k in range(list_len):
        row = map_ref[list_ref[fragment, k]]
        hit = row // own_count == owner
        for r in range(CAP):
            picked[r] = jnp.where(hit & (count == r), row % own_count, picked[r])
        count = count + hit.astype(jnp.int32)
    return picked, count


def send_kernel(frags, own_count, list_len, where, map_ref, list_ref, energy, occ, table, *refs):
    outs, own, sems = refs[:6], refs[6], refs[7]
    me = where[0]
    block = table.shape[1]
    copies = []

    def start(out, index, fragment, inside):
        picked, count = pick(map_ref, list_ref, list_len, own_count, fragment, me)
        for r in range(CAP):
            copy = pltpu.make_async_copy(
                table.at[picked[r]], out.at[pl.ds(r * block, block)], sems.at[index, r]
            )
            needed = inside & (count > r)
            pl.when(needed)(copy.start)
            copies.append((needed, copy))

    for index, (distance, parity) in enumerate(ROUNDS):
        up = (me // distance) % 2 == parity
        partner = jnp.where(up, me + distance, me - distance)
        inside = (partner >= 0) & (partner < frags)
        start(outs[index], index, jnp.clip(partner, 0, frags - 1), inside)
    start(own, 6, me, me >= 0)
    for out in outs + (own,):
        out[pl.ds(CAP * block, TAIL), :] = jnp.zeros((TAIL, out.shape[1]), out.dtype)
    for out in outs:
        out[pl.ds(CAP * block, own_count), pl.ds(0, block)] = energy[...]
    own[pl.ds(CAP * block, occ.shape[0]), :] = occ[...]
    for needed, copy in copies:
        pl.when(needed)(copy.wait)


def pack_to_send(where, owner_map, vir_list, energy, occ, table, frags):
    own_count, block_rows, cols = table.shape
    list_len = vir_list.shape[1]
    part = jax.ShapeDtypeStruct((CAP * block_rows + TAIL, cols), table.dtype)
    return pl.pallas_call(
        functools.partial(send_kernel, frags, own_count, list_len),
        out_shape=(part,) * 7,
        in_specs=[SMEM, SMEM, SMEM, VMEM, VMEM, ANY],
        out_specs=(VMEM,) * 7,
        scratch_shapes=[pltpu.SemaphoreType.DMA((7, CAP))],
        compiler_params=pltpu.CompilerParams(vmem_limit_bytes=8 * MIB),
        cost_estimate=NO_COST,
        name="pack_to_send",
    )(where, owner_map, vir_list, energy, occ, table)


def plan_kernel(frags, own_count, list_len, where, map_ref, list_ref, plan, target):
    me = where[0]
    rows, owners, codes, classes = [], [], [], []
    for k in range(list_len):
        row = map_ref[list_ref[me, k]]
        owner = row // own_count
        low = jnp.minimum(me, owner)
        far = jnp.abs(owner - me)
        code = jnp.int32(0)
        for index, (distance, parity) in enumerate(ROUNDS):
            code = jnp.where(
                (far == distance) & ((low // distance) % 2 == parity), index + 1, code
            )
        rows.append(row)
        owners.append(owner)
        codes.append(code)
        classes.append(jnp.where(code == 0, 0, jnp.maximum(code - 3, 1)))
    for k in range(list_len):
        place = jnp.int32(0)
        rank = jnp.int32(0)
        for j in range(list_len):
            if j < k:
                place += (classes[j] <= classes[k]).astype(jnp.int32)
                rank += (owners[j] == owners[k]).astype(jnp.int32)
            elif j > k:
                place += (classes[j] < classes[k]).astype(jnp.int32)
        plan[0, place] = codes[k]
        plan[1, place] = rank
        plan[2, place] = rows[k]
        plan[3, place] = jnp.int32(k)

    def one(fragment, carry):
        picked, _ = pick(map_ref, list_ref, list_len, own_count, fragment, me)
        for r in range(CAP):
            target[fragment, r] = picked[r]
        return carry

    lax.fori_loop(0, frags, one, 0)


def plan_lists(where, owner_map, vir_list, own_count, frags):
    list_len = vir_list.shape[1]
    return pl.pallas_call(
        functools.partial(plan_kernel, frags, own_count, list_len),
        out_shape=(
            jax.ShapeDtypeStruct((4, list_len), jnp.int32),
            jax.ShapeDtypeStruct((frags, CAP), jnp.int32),
        ),
        in_specs=[SMEM, SMEM, SMEM],
        out_specs=(SMEM, SMEM),
        compiler_params=pltpu.CompilerParams(vmem_limit_bytes=4 * MIB),
        cost_estimate=NO_COST,
        name="plan_lists",
    )(where, owner_map, vir_list)


def pack_kernel(first, codes, block, with_energy, plan, *refs):
    count = len(codes)
    if with_energy:
        own_energy, arrived, (out, levels, raw, wide, sems, tail_sems) = (
            refs[0],
            refs[1 : count + 1],
            refs[count + 1 :],
        )
    else:
        arrived, (out, sems) = refs[:count], refs[count:]
    for i in range(2):
        code = plan[0, first + i]
        begin = pl.multiple_of(plan[1, first + i] * block, block)
        rows = pl.ds(i * block, block)
        for source, ref in zip(codes, arrived):

            @pl.when(code == source)
            def _(ref=ref, begin=begin, rows=rows):
                pltpu.make_async_copy(
                    ref.at[pl.ds(begin, block)], out.at[rows], sems.at[i]
                ).start()

    if with_energy:
        own_count = own_energy.shape[0]
        copies = [
            pltpu.make_async_copy(
                ref.at[pl.ds(2 * block, TAIL), pl.ds(0, block)],
                raw.at[pl.ds(n * TAIL, TAIL)],
                tail_sems.at[n],
            )
            for n, ref in enumerate(arrived)
        ]
        for copy in copies:
            copy.start()
        wide[0:own_count, :] = own_energy[...].astype(jnp.float32)
        for copy in copies:
            copy.wait()
        wide[TAIL:, :] = raw[...].astype(jnp.float32)
        levels[...] = jnp.zeros_like(levels)
        for place in range(first + 2):
            row = plan[0, place] * TAIL + plan[2, place] % own_count
            levels[place : place + 1, :] = wide[pl.ds(row, 1), :]
    for i in range(2):
        rows = pl.ds(i * block, block)
        pltpu.make_async_copy(arrived[0].at[rows], out.at[rows], sems.at[i]).wait()


def pack_group(first, block, plan, arrived, own_energy=None):
    codes = tuple(arrived)
    refs = [arrived[c] for c in codes]
    cols, dtype = refs[0].shape[1], refs[0].dtype
    shapes = [jax.ShapeDtypeStruct((2 * block, cols), dtype)]
    scratch = [pltpu.SemaphoreType.DMA((2,))]
    extra = []
    if own_energy is not None:
        shapes.append(jax.ShapeDtypeStruct((plan.shape[1], block), jnp.float32))
        scratch = [
            pltpu.VMEM((len(codes) * TAIL, block), dtype),
            pltpu.VMEM(((len(codes) + 1) * TAIL, block), jnp.float32),
            *scratch,
            pltpu.SemaphoreType.DMA((len(codes),)),
        ]
        extra = [own_energy]
    return pl.pallas_call(
        functools.partial(pack_kernel, first, codes, block, own_energy is not None),
        out_shape=tuple(shapes),
        in_specs=[SMEM] + [VMEM] * len(extra) + [ANY] * len(refs),
        out_specs=(VMEM,) * len(shapes),
        scratch_shapes=scratch,
        compiler_params=pltpu.CompilerParams(vmem_limit_bytes=4 * MIB),
        cost_estimate=NO_COST,
        name="pack_group",
    )(plan, *extra, *refs)


def place_of(aux, b):
    return jnp.where(aux < 2, 2 * aux + b, aux + 2 + 2 * b)


def contract_kernel(stage, block, width, where, plan, levels, rows_ref, energy, *refs):
    groups = min(stage + 2, 4)
    parts, rest = refs[: groups * 4], refs[groups * 4 :]
    quarters = {2: (0, 2), 3: (1, 3)}.get(stage, (0, 1, 2, 3))
    partial = None
    if stage == 2:
        total, left, grid, occ, scaled, left_sems, grid_sems, occ_sems = rest
    elif stage == 3:
        before, partial, rest = rest[:2], rest[2], rest[3:]
        sent, stay, left, grid, occ, scaled, total, amps, tall, dens = rest[:10]
        left_sems, grid_sems, occ_sems = rest[10:]
    else:
        out, left, grid, occ, scaled, total, amps, left_sems, grid_sems, occ_sems = rest
    me, aux = where[0], where[1]
    places = (place_of(aux, 0), place_of(aux, 1))

    def occ_copy(quarter):
        return pltpu.make_async_copy(
            parts[quarter].at[pl.ds(2 * block, TAIL)],
            occ.at[pl.ds(quarter * TAIL, TAIL)],
            occ_sems.at[quarter],
        )

    def left_copy(b, group, begin, quarter):
        return pltpu.make_async_copy(
            parts[group * 4 + quarter].at[pl.ds(begin, block)],
            left.at[pl.ds(b * block, block), pl.ds(quarter * width, width)],
            left_sems.at[b, quarter],
        )

    def grid_copy(slot, group, quarter):
        return pltpu.make_async_copy(
            parts[group * 4 + quarter].at[pl.ds(0, 2 * block)],
            grid.at[pl.ds(slot * 2 * block, 2 * block), pl.ds(quarter * width, width)],
            grid_sems.at[slot, quarter],
        )

    def run(row_count, group_list):
        for quarter in quarters:
            occ_copy(quarter).start()
            for b in range(row_count):
                begin = pl.multiple_of((places[b] % 2) * block, block)
                for group in range(groups):

                    @pl.when(places[b] // 2 == group)
                    def _(b=b, group=group, begin=begin, quarter=quarter):
                        left_copy(b, group, begin, quarter).start()

            for slot, group in enumerate(group_list):
                grid_copy(slot, group, quarter).start()
        height = len(PAIRS) * row_count * block
        span = len(group_list) * 2 * block

        def scale(turn):
            quarter = quarters[turn]
            cols = pl.ds(quarter * width, width)
            orbit = [
                occ[quarter * TAIL + i : quarter * TAIL + i + 1, :].astype(jnp.float32)
                for i in range(3)
            ]
            for b in range(row_count):
                rows = left[pl.ds(b * block, block), cols].astype(jnp.float32)
                for p, (i, j) in enumerate(PAIRS):
                    scaled[turn % 2, pl.ds((p * row_count + b) * block, block), :] = (
                        rows * (orbit[i] * orbit[j])
                    ).astype(jnp.bfloat16)

        def wait_left(turn):
            quarter = quarters[turn]
            occ_copy(quarter).wait()
            for b in range(row_count):
                left_copy(b, 0, 0, quarter).wait()

        wait_left(0)
        scale(0)
        for turn, quarter in enumerate(quarters):
            cols = pl.ds(quarter * width, width)
            for slot, group in enumerate(group_list):
                grid_copy(slot, group, quarter).wait()
            if turn + 1 < len(quarters):
                wait_left(turn + 1)
                scale(turn + 1)
            for step in range(height // 768):
                rows = pl.ds(step * 768, 768)
                term = lax.dot_general(
                    scaled[turn % 2, rows, :],
                    grid[pl.ds(0, span), cols],
                    (((1,), (1,)), ((), ())),
                    preferred_element_type=jnp.float32,
                )
                if turn:
                    total[rows, pl.ds(0, span)] += term
                elif partial is not None:
                    total[rows, pl.ds(0, span)] = term + partial[rows, :]
                else:
                    total[rows, pl.ds(0, span)] = term
        if stage == 2:
            return None
        lane = lax.broadcasted_iota(jnp.int32, (block, block), 1)
        sub = lax.broadcasted_iota(jnp.int32, (block, block), 0)
        sums = []
        for b in range(row_count):
            own_row = energy[pl.ds(places[b], 1), :]
            own_energy = jnp.transpose(jnp.broadcast_to(own_row, (block, block)))
            own_live = sub < rows_ref[me, plan[3, places[b]]]
            for q in range(2 * len(group_list)):
                place = 2 * group_list[q // 2] + q % 2
                their_energy = energy[place : place + 1, :]
                live = own_live & (lane < rows_ref[me, plan[3, place]])
                for p, (i, j) in enumerate(PAIRS):
                    gap = (levels[0, i] + levels[0, j]) - own_energy - their_energy
                    rows = pl.ds((p * row_count + b) * block, block)
                    value = total[rows, pl.ds(q * block, block)]
                    amp = jnp.where(live, value * pl.reciprocal(gap), 0.0).astype(jnp.bfloat16)
                    amps[:, pl.ds(p * span + q * block, block)] = amp
                    if stage == 3:
                        early = amp if b == 0 else jnp.where(aux < 2, amp, jnp.zeros_like(amp))
                        tall[rows, pl.ds(q * block, block)] = early
            wide = amps[:, pl.ds(0, len(PAIRS) * span)]
            sums.append(
                lax.dot_general(
                    wide, wide, (((1,), (1,)), ((), ())), preferred_element_type=jnp.float32
                )
            )
        return sums

    if stage == 0:

        @pl.when(aux < 2)
        def _():
            out[0], out[1] = run(2, (0, 1))

        @pl.when(aux >= 2)
        def _():
            out[...] = jnp.zeros_like(out)
    elif stage == 1:

        @pl.when(aux < 2)
        def _():
            out[0], out[1] = run(2, (2,))

        @pl.when(aux >= 2)
        def _():
            out[0] = run(1, (0, 1, 2))[0]
            out[1] = jnp.zeros(out.shape[1:], out.dtype)
    elif stage == 2:
        run(2, (3,))
    else:
        sums = run(2, (3,))
        for b in range(2):
            dens[b] = sums[b] + (before[0][b] + before[1][b])
        for q in range(2):
            late = tall[:, pl.ds(q * block, block)]
            dens[2 + q] = lax.dot_general(
                late, late, (((0,), (0,)), ((), ())), preferred_element_type=jnp.float32
            )
        half = block // 2
        side = aux // 2
        stay[...] = dens[:, pl.ds(pl.multiple_of(side * half, half), half), :]
        sent[...] = dens[:, pl.ds(pl.multiple_of((1 - side) * half, half), half), :]


def contract(stage, where, plan, levels, vir_rows, energy, parts, before=()):
    block, width = energy.shape[1], parts[0].shape[1]
    height = len(PAIRS) * 2 * block
    span = (4, 6, 2, 2)[stage] * block
    scratch = [
        pltpu.VMEM((2 * block, 4 * width), jnp.bfloat16),
        pltpu.VMEM((span, 4 * width), jnp.bfloat16),
        pltpu.VMEM((4 * TAIL, width), jnp.bfloat16),
        pltpu.VMEM((2, height, width), jnp.bfloat16),
    ]
    if stage != 2:
        scratch += [
            pltpu.VMEM((height, span), jnp.float32),
            pltpu.VMEM((block, len(PAIRS) * span), jnp.bfloat16),
        ]
    out_specs = VMEM
    if stage == 3:
        scratch += [
            pltpu.VMEM((height, span), jnp.bfloat16),
            pltpu.VMEM((4, block, block), jnp.float32),
        ]
        out_shape = (jax.ShapeDtypeStruct((4, block // 2, block), jnp.float32),) * 2
        out_specs = (VMEM, VMEM)
    elif stage == 2:
        out_shape = jax.ShapeDtypeStruct((height, span), jnp.float32)
    else:
        out_shape = jax.ShapeDtypeStruct((2, block, block), jnp.float32)
    scratch += [
        pltpu.SemaphoreType.DMA((2, 4)),
        pltpu.SemaphoreType.DMA((3, 4)),
        pltpu.SemaphoreType.DMA((4,)),
    ]
    cost = NO_COST
    if stage in (1, 2):
        units = (8, 6, 2)[stage] * len(PAIRS) * block * block
        cost = pl.CostEstimate(
            flops=2 * units * 4 * width, bytes_accessed=units * 4, transcendentals=0
        )
    return pl.pallas_call(
        functools.partial(contract_kernel, stage, block, width),
        out_shape=out_shape,
        in_specs=[SMEM] * 4 + [VMEM] + [ANY] * len(parts) + [VMEM] * len(before),
        out_specs=out_specs,
        scratch_shapes=scratch,
        compiler_params=pltpu.CompilerParams(vmem_limit_bytes=26 * MIB),
        cost_estimate=cost,
        name="contract",
    )(where, plan, levels, vir_rows, energy, *parts, *before)


def spread_kernel(own_count, where, plan, kept, came, out):
    aux = where[1]
    out[...] = jnp.zeros_like(out)
    holders = (aux, aux ^ 2, aux ^ 1, aux ^ 3)
    late = [kept[4 + q] + came[4 + q] for q in range(2)]
    for index, holder in enumerate(holders):
        source = kept if index < 2 else came
        for b in range(2):
            place = place_of(holder, b)
            value = source[2 * (index % 2) + b]
            if b == 1:
                value += jnp.where(place == 6, late[0], jnp.where(place == 7, late[1], 0.0))
            out[plan[2, place] // own_count, plan[1, place]] = value


def spread(where, plan, kept, came, frags, own_count):
    return pl.pallas_call(
        functools.partial(spread_kernel, own_count),
        out_shape=jax.ShapeDtypeStruct((frags, CAP) + kept.shape[1:], kept.dtype),
        in_specs=[SMEM, SMEM, VMEM, VMEM],
        out_specs=VMEM,
        compiler_params=pltpu.CompilerParams(vmem_limit_bytes=4 * MIB),
        name="spread",
    )(where, plan, kept, came)


def collect_kernel(target, came, out):
    out[...] = jnp.zeros_like(out)

    def one(fragment, carry):
        for r in range(CAP):
            out[target[fragment, r]] += came[fragment, r]
        return carry

    lax.fori_loop(0, came.shape[0], one, 0)


def collect(target, came, own_count):
    return pl.pallas_call(
        collect_kernel,
        out_shape=jax.ShapeDtypeStruct((own_count,) + came.shape[2:], came.dtype),
        in_specs=[SMEM, VMEM],
        out_specs=VMEM,
        compiler_params=pltpu.CompilerParams(vmem_limit_bytes=4 * MIB),
        name="collect",
    )(target, came)


def body(vir_grid, vir_energy, occ_grid, occ_energy, vir_list, vir_rows, owner_map):
    frags = lax.axis_size("frag")
    aux_count = lax.axis_size("aux")
    me = lax.axis_index("frag").astype(jnp.int32)
    aux = lax.axis_index("aux").astype(jnp.int32)
    own_count, block, width = vir_grid.shape
    list_len = vir_list.shape[1]
    where = jnp.stack([me, aux])
    far_pairs = [(i, i ^ 2) for i in range(aux_count)]
    near_pairs = [(i, i ^ 1) for i in range(aux_count)]

    *outgoing, own = pack_to_send(
        where, owner_map, vir_list, vir_energy, occ_grid[0], vir_grid, frags
    )

    def over_aux(here, *others):
        far = lax.ppermute(here, "aux", far_pairs)
        near = lax.ppermute(here, "aux", near_pairs)
        onward = after(far, *others) if others else far
        return [here, far, near, lax.ppermute(onward, "aux", near_pairs)]

    def after(value, *others):
        return lax.optimization_barrier((value, *others))[0]

    def send(index, *others):
        distance, parity = ROUNDS[index]
        payload = after(outgoing[index], *others) if others else outgoing[index]
        return lax.ppermute(payload, "frag", round_pairs(distance, parity, frags))

    arrived = {code: send(code - 1) for code in (1, 2, 3, 4)}
    parts = over_aux(own)
    arrived[5] = send(4, *(arrived[c] for c in (1, 2, 3, 4)))
    plan, target = plan_lists(
        after(where, arrived[3]), owner_map, vir_list, own_count, frags
    )
    here = pack_group(2, block, plan, {c: arrived[c] for c in range(1, 5)})[0]
    parts += over_aux(here)
    arrived[6] = send(5, parts[5])
    here, early_energy = pack_group(
        4, block, plan, {c: arrived[c] for c in range(1, 6)}, vir_energy
    )
    shared = (where, plan, occ_energy, vir_rows)
    first = contract(0, *shared, early_energy, parts[:8])
    parts += over_aux(here, first)
    arrived[6] = after(arrived[6], first)
    here, energy = pack_group(6, block, plan, arrived, vir_energy)
    here = after(here, parts[9])
    second = contract(1, *shared, early_energy, parts[:12])
    near = lax.ppermute(here, "aux", near_pairs)
    partial = contract(2, *shared, energy, parts + [here, here, near, near])
    far = lax.ppermute(here, "aux", far_pairs)
    far_near = lax.ppermute(after(far, second, partial), "aux", near_pairs)
    parts += [here, far, near, far_near]
    sent, stay = contract(3, *shared, energy, parts, (first, second, partial))

    quarter = block // aux_count
    core = aux % 2
    met = lax.ppermute(sent, "aux", far_pairs)
    both = jnp.concatenate([stay[:2], met[:2], stay[2:] + met[2:]], axis=0)
    sent = lax.dynamic_slice_in_dim(both, (1 - core) * quarter, quarter, 1)
    kept = lax.dynamic_slice_in_dim(both, core * quarter, quarter, 1)
    came = lax.ppermute(sent, "aux", near_pairs)
    outgoing = spread(where, plan, kept, came, frags, own_count)
    incoming = lax.all_to_all(outgoing, "frag", 0, 0, tiled=True)
    return collect(target, incoming, own_count)


def solution(mesh):
    return jax.shard_map(
        body,
        mesh=mesh,
        in_specs=(
            P("frag", None, "aux"),
            P("frag", None),
            P("frag", None, "aux"),
            P("frag", None),
            P(),
            P(),
            P(),
        ),
        out_specs=P("frag", "aux", None),
        check_vma=False,
    )
```

```python
import functools

import jax
import jax.numpy as jnp
from jax import lax
from jax.experimental import pallas as pl
from jax.experimental.pallas import tpu as pltpu
from jax.sharding import PartitionSpec as P

ROUNDS = ((1, 0), (1, 1), (2, 0), (2, 1), (3, 0), (3, 1))
CAP = 2
TAIL = 16
PAIRS = tuple((i, j) for i in range(3) for j in range(i, 3))
MIB = 2**20
NO_COST = pl.CostEstimate(flops=0, bytes_accessed=0, transcendentals=0)
ANY = pl.BlockSpec(memory_space=pl.ANY)
SMEM = pl.BlockSpec(memory_space=pltpu.SMEM)
VMEM = pl.BlockSpec(memory_space=pltpu.VMEM)


def round_pairs(distance, parity, frags):
    up = [(i, i + distance) for i in range(frags - distance) if (i // distance) % 2 == parity]
    return up + [(b, a) for a, b in up]


def pick(map_ref, list_ref, list_len, own_count, fragment, owner):
    count = jnp.int32(0)
    picked = [jnp.int32(0)] * CAP
    for k in range(list_len):
        row = map_ref[list_ref[fragment, k]]
        hit = row // own_count == owner
        for r in range(CAP):
            picked[r] = jnp.where(hit & (count == r), row % own_count, picked[r])
        count = count + hit.astype(jnp.int32)
    return picked, count


def send_kernel(frags, own_count, list_len, where, map_ref, list_ref, energy, occ, table, *refs):
    outs, own, sems = refs[:6], refs[6], refs[7]
    me = where[0]
    block = table.shape[1]
    copies = []

    def start(out, index, fragment, inside):
        picked, count = pick(map_ref, list_ref, list_len, own_count, fragment, me)
        for r in range(CAP):
            copy = pltpu.make_async_copy(
                table.at[picked[r]], out.at[pl.ds(r * block, block)], sems.at[index, r]
            )
            needed = inside & (count > r)
            pl.when(needed)(copy.start)
            copies.append((needed, copy))

    for index, (distance, parity) in enumerate(ROUNDS):
        up = (me // distance) % 2 == parity
        partner = jnp.where(up, me + distance, me - distance)
        inside = (partner >= 0) & (partner < frags)
        start(outs[index], index, jnp.clip(partner, 0, frags - 1), inside)
    start(own, 6, me, me >= 0)
    for out in outs + (own,):
        out[pl.ds(CAP * block, TAIL), :] = jnp.zeros((TAIL, out.shape[1]), out.dtype)
    for out in outs:
        out[pl.ds(CAP * block, own_count), pl.ds(0, block)] = energy[...]
    own[pl.ds(CAP * block, occ.shape[0]), :] = occ[...]
    for needed, copy in copies:
        pl.when(needed)(copy.wait)


def pack_to_send(where, owner_map, vir_list, energy, occ, table, frags):
    own_count, block_rows, cols = table.shape
    list_len = vir_list.shape[1]
    part = jax.ShapeDtypeStruct((CAP * block_rows + TAIL, cols), table.dtype)
    return pl.pallas_call(
        functools.partial(send_kernel, frags, own_count, list_len),
        out_shape=(part,) * 7,
        in_specs=[SMEM, SMEM, SMEM, VMEM, VMEM, ANY],
        out_specs=(VMEM,) * 7,
        scratch_shapes=[pltpu.SemaphoreType.DMA((7, CAP))],
        compiler_params=pltpu.CompilerParams(vmem_limit_bytes=8 * MIB),
        cost_estimate=NO_COST,
        name="pack_to_send",
    )(where, owner_map, vir_list, energy, occ, table)


def plan_kernel(frags, own_count, list_len, where, map_ref, list_ref, plan, target):
    me = where[0]
    rows, owners, codes, classes = [], [], [], []
    for k in range(list_len):
        row = map_ref[list_ref[me, k]]
        owner = row // own_count
        low = jnp.minimum(me, owner)
        far = jnp.abs(owner - me)
        code = jnp.int32(0)
        for index, (distance, parity) in enumerate(ROUNDS):
            code = jnp.where(
                (far == distance) & ((low // distance) % 2 == parity), index + 1, code
            )
        rows.append(row)
        owners.append(owner)
        codes.append(code)
        classes.append(jnp.where(code == 0, 0, jnp.maximum(code - 3, 1)))
    for k in range(list_len):
        place = jnp.int32(0)
        rank = jnp.int32(0)
        for j in range(list_len):
            if j < k:
                place += (classes[j] <= classes[k]).astype(jnp.int32)
                rank += (owners[j] == owners[k]).astype(jnp.int32)
            elif j > k:
                place += (classes[j] < classes[k]).astype(jnp.int32)
        plan[0, place] = codes[k]
        plan[1, place] = rank
        plan[2, place] = rows[k]
        plan[3, place] = jnp.int32(k)

    def one(fragment, carry):
        picked, _ = pick(map_ref, list_ref, list_len, own_count, fragment, me)
        for r in range(CAP):
            target[fragment, r] = picked[r]
        return carry

    lax.fori_loop(0, frags, one, 0)


def plan_lists(where, owner_map, vir_list, own_count, frags):
    list_len = vir_list.shape[1]
    return pl.pallas_call(
        functools.partial(plan_kernel, frags, own_count, list_len),
        out_shape=(
            jax.ShapeDtypeStruct((4, list_len), jnp.int32),
            jax.ShapeDtypeStruct((frags, CAP), jnp.int32),
        ),
        in_specs=[SMEM, SMEM, SMEM],
        out_specs=(SMEM, SMEM),
        compiler_params=pltpu.CompilerParams(vmem_limit_bytes=4 * MIB),
        cost_estimate=NO_COST,
        name="plan_lists",
    )(where, owner_map, vir_list)


def pack_kernel(first, codes, block, with_energy, plan, *refs):
    count = len(codes)
    if with_energy:
        own_energy, arrived, (out, levels, raw, wide, sems, tail_sems) = (
            refs[0],
            refs[1 : count + 1],
            refs[count + 1 :],
        )
    else:
        arrived, (out, sems) = refs[:count], refs[count:]
    for i in range(2):
        code = plan[0, first + i]
        begin = pl.multiple_of(plan[1, first + i] * block, block)
        rows = pl.ds(i * block, block)
        for source, ref in zip(codes, arrived):

            @pl.when(code == source)
            def _(ref=ref, begin=begin, rows=rows):
                pltpu.make_async_copy(
                    ref.at[pl.ds(begin, block)], out.at[rows], sems.at[i]
                ).start()

    if with_energy:
        own_count = own_energy.shape[0]
        copies = [
            pltpu.make_async_copy(
                ref.at[pl.ds(2 * block, TAIL), pl.ds(0, block)],
                raw.at[pl.ds(n * TAIL, TAIL)],
                tail_sems.at[n],
            )
            for n, ref in enumerate(arrived)
        ]
        for copy in copies:
            copy.start()
        wide[0:own_count, :] = own_energy[...].astype(jnp.float32)
        for copy in copies:
            copy.wait()
        wide[TAIL:, :] = raw[...].astype(jnp.float32)
        levels[...] = jnp.zeros_like(levels)
        for place in range(first + 2):
            row = plan[0, place] * TAIL + plan[2, place] % own_count
            levels[place : place + 1, :] = wide[pl.ds(row, 1), :]
    for i in range(2):
        rows = pl.ds(i * block, block)
        pltpu.make_async_copy(arrived[0].at[rows], out.at[rows], sems.at[i]).wait()


def pack_group(first, block, plan, arrived, own_energy=None):
    codes = tuple(arrived)
    refs = [arrived[c] for c in codes]
    cols, dtype = refs[0].shape[1], refs[0].dtype
    shapes = [jax.ShapeDtypeStruct((2 * block, cols), dtype)]
    scratch = [pltpu.SemaphoreType.DMA((2,))]
    extra = []
    if own_energy is not None:
        shapes.append(jax.ShapeDtypeStruct((plan.shape[1], block), jnp.float32))
        scratch = [
            pltpu.VMEM((len(codes) * TAIL, block), dtype),
            pltpu.VMEM(((len(codes) + 1) * TAIL, block), jnp.float32),
            *scratch,
            pltpu.SemaphoreType.DMA((len(codes),)),
        ]
        extra = [own_energy]
    return pl.pallas_call(
        functools.partial(pack_kernel, first, codes, block, own_energy is not None),
        out_shape=tuple(shapes),
        in_specs=[SMEM] + [VMEM] * len(extra) + [ANY] * len(refs),
        out_specs=(VMEM,) * len(shapes),
        scratch_shapes=scratch,
        compiler_params=pltpu.CompilerParams(vmem_limit_bytes=4 * MIB),
        cost_estimate=NO_COST,
        name="pack_group",
    )(plan, *extra, *refs)


def place_of(aux, b):
    return aux + 4 * b


def contract_kernel(stage, block, width, where, plan, levels, rows_ref, energy, *refs):
    groups = min(stage + 2, 4)
    parts, rest = refs[: groups * 4], refs[groups * 4 :]
    quarters = {2: (0, 2), 3: (1, 3)}.get(stage, (0, 1, 2, 3))
    partial = None
    if stage == 2:
        total, left, grid, occ, scaled, left_sems, grid_sems, occ_sems = rest
    elif stage == 3:
        before, partial, rest = rest[:2], rest[2], rest[3:]
        sent, stay, left, grid, occ, scaled, total, amps, tall, dens = rest[:10]
        left_sems, grid_sems, occ_sems = rest[10:]
    elif stage == 1:
        out, left, grid, occ, scaled, total, amps, tall, left_sems, grid_sems, occ_sems = rest
    else:
        out, left, grid, occ, scaled, total, amps, left_sems, grid_sems, occ_sems = rest
    me, aux = where[0], where[1]
    places = (place_of(aux, 0), place_of(aux, 1))

    def occ_copy(quarter):
        return pltpu.make_async_copy(
            parts[quarter].at[pl.ds(2 * block, TAIL)],
            occ.at[pl.ds(quarter * TAIL, TAIL)],
            occ_sems.at[quarter],
        )

    def left_copy(b, group, begin, quarter):
        return pltpu.make_async_copy(
            parts[group * 4 + quarter].at[pl.ds(begin, block)],
            left.at[pl.ds(b * block, block), pl.ds(quarter * width, width)],
            left_sems.at[b, quarter],
        )

    def grid_copy(slot, group, quarter):
        return pltpu.make_async_copy(
            parts[group * 4 + quarter].at[pl.ds(0, 2 * block)],
            grid.at[pl.ds(slot * 2 * block, 2 * block), pl.ds(quarter * width, width)],
            grid_sems.at[slot, quarter],
        )

    def run(row_count, group_list):
        for quarter in quarters:
            occ_copy(quarter).start()
            for b in range(row_count):
                begin = pl.multiple_of((places[b] % 2) * block, block)
                for group in range(groups):

                    @pl.when(places[b] // 2 == group)
                    def _(b=b, group=group, begin=begin, quarter=quarter):
                        left_copy(b, group, begin, quarter).start()

            for slot, group in enumerate(group_list):
                grid_copy(slot, group, quarter).start()
        height = len(PAIRS) * row_count * block
        span = len(group_list) * 2 * block

        def scale(turn):
            quarter = quarters[turn]
            cols = pl.ds(quarter * width, width)
            orbit = [
                occ[quarter * TAIL + i : quarter * TAIL + i + 1, :].astype(jnp.float32)
                for i in range(3)
            ]
            for b in range(row_count):
                rows = left[pl.ds(b * block, block), cols].astype(jnp.float32)
                for p, (i, j) in enumerate(PAIRS):
                    scaled[turn % 2, pl.ds((p * row_count + b) * block, block), :] = (
                        rows * (orbit[i] * orbit[j])
                    ).astype(jnp.bfloat16)

        def wait_left(turn):
            quarter = quarters[turn]
            occ_copy(quarter).wait()
            for b in range(row_count):
                left_copy(b, 0, 0, quarter).wait()

        wait_left(0)
        scale(0)
        for turn, quarter in enumerate(quarters):
            cols = pl.ds(quarter * width, width)
            for slot, group in enumerate(group_list):
                grid_copy(slot, group, quarter).wait()
            if turn + 1 < len(quarters):
                wait_left(turn + 1)
                scale(turn + 1)
            for step in range(height // 768):
                rows = pl.ds(step * 768, 768)
                term = lax.dot_general(
                    scaled[turn % 2, rows, :],
                    grid[pl.ds(0, span), cols],
                    (((1,), (1,)), ((), ())),
                    preferred_element_type=jnp.float32,
                )
                if turn:
                    total[rows, pl.ds(0, span)] += term
                elif partial is not None:
                    total[rows, pl.ds(0, span)] = term + partial[rows, :]
                else:
                    total[rows, pl.ds(0, span)] = term
        if stage == 2:
            return None
        lane = lax.broadcasted_iota(jnp.int32, (block, block), 1)
        sub = lax.broadcasted_iota(jnp.int32, (block, block), 0)
        sums = []
        for b in range(row_count):
            own_row = energy[pl.ds(places[b], 1), :]
            own_energy = jnp.transpose(jnp.broadcast_to(own_row, (block, block)))
            own_live = sub < rows_ref[me, plan[3, places[b]]]
            for q in range(2 * len(group_list)):
                place = 2 * group_list[q // 2] + q % 2
                their_energy = energy[place : place + 1, :]
                live = own_live & (lane < rows_ref[me, plan[3, place]])
                for p, (i, j) in enumerate(PAIRS):
                    gap = (levels[0, i] + levels[0, j]) - own_energy - their_energy
                    rows = pl.ds((p * row_count + b) * block, block)
                    value = total[rows, pl.ds(q * block, block)]
                    amp = jnp.where(live, value * pl.reciprocal(gap), 0.0).astype(jnp.bfloat16)
                    amps[:, pl.ds(p * span + q * block, block)] = amp
                    if stage == 3:
                        early = amp if b == 0 else jnp.where(aux < 2, amp, jnp.zeros_like(amp))
                        tall[rows, pl.ds(q * block, block)] = early
                    elif stage == 1 and b == 0:
                        tall[pl.ds(p * block, block), pl.ds(q * block, block)] = amp
            wide = amps[:, pl.ds(0, len(PAIRS) * span)]
            sums.append(
                lax.dot_general(
                    wide, wide, (((1,), (1,)), ((), ())), preferred_element_type=jnp.float32
                )
            )
        return sums

    def late_sum(q):
        late = tall[:, pl.ds(q * block, block)]
        return lax.dot_general(
            late, late, (((0,), (0,)), ((), ())), preferred_element_type=jnp.float32
        )

    if stage == 0:
        out[0] = run(1, (0, 1))[0]
    elif stage == 1:

        @pl.when(aux < 2)
        def _():
            out[0], out[1] = run(2, (2,))

        @pl.when(aux >= 2)
        def _():
            out[0] = run(1, (2,))[0]
            out[1] = jnp.zeros(out.shape[1:], out.dtype)

        for q in range(2):
            out[2 + q] = late_sum(q)
    elif stage == 2:
        run(2, (3,))
    else:
        first, second = before
        sums = run(2, (3,))
        dens[0] = sums[0] + (first[0] + second[0])
        share = sums[1] + second[1]
        for q in range(4):
            late = second[2 + q] if q < 2 else late_sum(q - 2)
            dens[1 + q] = late + jnp.where(aux == q, share, 0.0)
        half = block // 2
        side = aux // 2
        stay[...] = dens[:, pl.ds(pl.multiple_of(side * half, half), half), :]
        sent[...] = dens[:, pl.ds(pl.multiple_of((1 - side) * half, half), half), :]


def contract(stage, where, plan, levels, vir_rows, energy, parts, before=()):
    block, width = energy.shape[1], parts[0].shape[1]
    height = len(PAIRS) * 2 * block
    span = (4, 2, 2, 2)[stage] * block
    scratch = [
        pltpu.VMEM((2 * block, 4 * width), jnp.bfloat16),
        pltpu.VMEM((span, 4 * width), jnp.bfloat16),
        pltpu.VMEM((4 * TAIL, width), jnp.bfloat16),
        pltpu.VMEM((2, height, width), jnp.bfloat16),
    ]
    if stage != 2:
        scratch += [
            pltpu.VMEM((height, span), jnp.float32),
            pltpu.VMEM((block, len(PAIRS) * span), jnp.bfloat16),
        ]
    out_specs = VMEM
    if stage == 3:
        scratch += [
            pltpu.VMEM((height, span), jnp.bfloat16),
            pltpu.VMEM((5, block, block), jnp.float32),
        ]
        out_shape = (jax.ShapeDtypeStruct((5, block // 2, block), jnp.float32),) * 2
        out_specs = (VMEM, VMEM)
    elif stage == 2:
        out_shape = jax.ShapeDtypeStruct((height, span), jnp.float32)
    elif stage == 1:
        scratch += [pltpu.VMEM((height // 2, span), jnp.bfloat16)]
        out_shape = jax.ShapeDtypeStruct((4, block, block), jnp.float32)
    else:
        out_shape = jax.ShapeDtypeStruct((1, block, block), jnp.float32)
    scratch += [
        pltpu.SemaphoreType.DMA((2, 4)),
        pltpu.SemaphoreType.DMA((3, 4)),
        pltpu.SemaphoreType.DMA((4,)),
    ]
    cost = NO_COST
    if stage in (1, 2):
        units = (4, 4, 2)[stage] * len(PAIRS) * block * block
        cost = pl.CostEstimate(
            flops=2 * units * 4 * width, bytes_accessed=units * 4, transcendentals=0
        )
    return pl.pallas_call(
        functools.partial(contract_kernel, stage, block, width),
        out_shape=out_shape,
        in_specs=[SMEM] * 4 + [VMEM] + [ANY] * len(parts) + [VMEM] * len(before),
        out_specs=out_specs,
        scratch_shapes=scratch,
        compiler_params=pltpu.CompilerParams(vmem_limit_bytes=26 * MIB),
        cost_estimate=cost,
        name="contract",
    )(where, plan, levels, vir_rows, energy, *parts, *before)


def spread_kernel(own_count, where, plan, kept, came, out):
    aux = where[1]
    out[...] = jnp.zeros_like(out)

    def put(place, value):
        out[plan[2, place] // own_count, plan[1, place]] = value

    put(aux, kept[0])
    put(aux ^ 2, kept[1])
    put(aux ^ 1, came[0])
    put(aux ^ 3, came[1])
    for q in range(4):
        put(4 + q, kept[2 + q] + came[2 + q])


def spread(where, plan, kept, came, frags, own_count):
    return pl.pallas_call(
        functools.partial(spread_kernel, own_count),
        out_shape=jax.ShapeDtypeStruct((frags, CAP) + kept.shape[1:], kept.dtype),
        in_specs=[SMEM, SMEM, VMEM, VMEM],
        out_specs=VMEM,
        compiler_params=pltpu.CompilerParams(vmem_limit_bytes=4 * MIB),
        name="spread",
    )(where, plan, kept, came)


def collect_kernel(target, came, out):
    out[...] = jnp.zeros_like(out)

    def one(fragment, carry):
        for r in range(CAP):
            out[target[fragment, r]] += came[fragment, r]
        return carry

    lax.fori_loop(0, came.shape[0], one, 0)


def collect(target, came, own_count):
    return pl.pallas_call(
        collect_kernel,
        out_shape=jax.ShapeDtypeStruct((own_count,) + came.shape[2:], came.dtype),
        in_specs=[SMEM, VMEM],
        out_specs=VMEM,
        compiler_params=pltpu.CompilerParams(vmem_limit_bytes=4 * MIB),
        name="collect",
    )(target, came)


def body(vir_grid, vir_energy, occ_grid, occ_energy, vir_list, vir_rows, owner_map):
    frags = lax.axis_size("frag")
    aux_count = lax.axis_size("aux")
    me = lax.axis_index("frag").astype(jnp.int32)
    aux = lax.axis_index("aux").astype(jnp.int32)
    own_count, block, width = vir_grid.shape
    list_len = vir_list.shape[1]
    where = jnp.stack([me, aux])
    far_pairs = [(i, i ^ 2) for i in range(aux_count)]
    near_pairs = [(i, i ^ 1) for i in range(aux_count)]

    *outgoing, own = pack_to_send(
        where, owner_map, vir_list, vir_energy, occ_grid[0], vir_grid, frags
    )

    def over_aux(here, *others):
        far = lax.ppermute(here, "aux", far_pairs)
        near = lax.ppermute(here, "aux", near_pairs)
        onward = after(far, *others) if others else far
        return [here, far, near, lax.ppermute(onward, "aux", near_pairs)]

    def after(value, *others):
        return lax.optimization_barrier((value, *others))[0]

    def send(index, *others):
        distance, parity = ROUNDS[index]
        payload = after(outgoing[index], *others) if others else outgoing[index]
        return lax.ppermute(payload, "frag", round_pairs(distance, parity, frags))

    arrived = {code: send(code - 1) for code in (1, 2, 3, 4)}
    parts = over_aux(own)
    arrived[5] = send(4, *(arrived[c] for c in (1, 2, 3, 4)))
    plan, target = plan_lists(
        after(where, arrived[3]), owner_map, vir_list, own_count, frags
    )
    here = pack_group(2, block, plan, {c: arrived[c] for c in range(1, 5)})[0]
    parts += over_aux(here)
    arrived[6] = send(5, parts[5])
    here, early_energy = pack_group(
        4, block, plan, {c: arrived[c] for c in range(1, 6)}, vir_energy
    )
    shared = (where, plan, occ_energy, vir_rows)
    first = contract(0, *shared, early_energy, parts[:8])
    parts += over_aux(here, first)
    arrived[6] = after(arrived[6], first)
    here, energy = pack_group(6, block, plan, arrived, vir_energy)
    here = after(here, parts[9])
    second = contract(1, *shared, early_energy, parts[:12])
    near = lax.ppermute(here, "aux", near_pairs)
    partial = contract(2, *shared, energy, parts + [here, here, near, near])
    far = lax.ppermute(here, "aux", far_pairs)
    far_near = lax.ppermute(after(far, second, partial), "aux", near_pairs)
    parts += [here, far, near, far_near]
    sent, stay = contract(3, *shared, energy, parts, (first, second, partial))

    quarter = block // aux_count
    core = aux % 2
    met = lax.ppermute(sent, "aux", far_pairs)
    both = jnp.concatenate([stay[:1], met[:1], stay[1:] + met[1:]], axis=0)
    sent = lax.dynamic_slice_in_dim(both, (1 - core) * quarter, quarter, 1)
    kept = lax.dynamic_slice_in_dim(both, core * quarter, quarter, 1)
    came = lax.ppermute(sent, "aux", near_pairs)
    outgoing = spread(where, plan, kept, came, frags, own_count)
    incoming = lax.all_to_all(outgoing, "frag", 0, 0, tiled=True)
    return collect(target, incoming, own_count)


def solution(mesh):
    return jax.shard_map(
        body,
        mesh=mesh,
        in_specs=(
            P("frag", None, "aux"),
            P("frag", None),
            P("frag", None, "aux"),
            P("frag", None),
            P(),
            P(),
            P(),
        ),
        out_specs=P("frag", "aux", None),
        check_vma=False,
    )
```

```python
import functools

import jax
import jax.numpy as jnp
from jax import lax
from jax.experimental import pallas as pl
from jax.experimental.pallas import tpu as pltpu
from jax.sharding import PartitionSpec as P

ROUNDS = ((1, 0), (1, 1), (2, 0), (2, 1), (3, 0), (3, 1))
CAP = 2
TAIL = 16
PAIRS = tuple((i, j) for i in range(3) for j in range(i, 3))
MIB = 2**20
NO_COST = pl.CostEstimate(flops=0, bytes_accessed=0, transcendentals=0)
ANY = pl.BlockSpec(memory_space=pl.ANY)
SMEM = pl.BlockSpec(memory_space=pltpu.SMEM)
VMEM = pl.BlockSpec(memory_space=pltpu.VMEM)


def round_pairs(distance, parity, frags):
    up = [(i, i + distance) for i in range(frags - distance) if (i // distance) % 2 == parity]
    return up + [(b, a) for a, b in up]


class Lists:
    def __init__(self, ref, frags, own_count, list_len):
        self.ref, self.frags, self.own_count, self.list_len = ref, frags, own_count, list_len
        self.listed = 2 + frags * own_count
        self.me, self.aux = ref[0], ref[1]

    def row(self, fragment, k):
        return self.ref[2 + self.ref[self.listed + fragment * self.list_len + k]]

    def live(self, fragment, k):
        return self.ref[self.listed + (self.frags + fragment) * self.list_len + k]

    def pick(self, fragment, owner):
        count = jnp.int32(0)
        picked = [jnp.int32(0)] * CAP
        for k in range(self.list_len):
            row = self.row(fragment, k)
            hit = row // self.own_count == owner
            for r in range(CAP):
                picked[r] = jnp.where(hit & (count == r), row % self.own_count, picked[r])
            count = count + hit.astype(jnp.int32)
        return picked, count


def send_kernel(sizes, ints, tails, table, *refs):
    outs, own, sems = refs[:6], refs[6], refs[7]
    lists = Lists(ints, *sizes)
    me, frags = lists.me, lists.frags
    block = table.shape[1]
    copies = []

    def start(out, index, fragment, inside):
        picked, count = lists.pick(fragment, me)
        for r in range(CAP):
            copy = pltpu.make_async_copy(
                table.at[picked[r]], out.at[pl.ds(r * block, block)], sems.at[index, r]
            )
            needed = inside & (count > r)
            pl.when(needed)(copy.start)
            copies.append((needed, copy))

    for index, (distance, parity) in enumerate(ROUNDS):
        up = (me // distance) % 2 == parity
        partner = jnp.where(up, me + distance, me - distance)
        inside = (partner >= 0) & (partner < frags)
        start(outs[index], index, jnp.clip(partner, 0, frags - 1), inside)
    start(own, 6, me, me >= 0)
    own[pl.ds(CAP * block, TAIL), :] = tails[pl.ds(0, TAIL), :]
    for out in outs:
        out[pl.ds(CAP * block, TAIL), :] = tails[pl.ds(TAIL, TAIL), :]
    for needed, copy in copies:
        pl.when(needed)(copy.wait)


def pack_to_send(ints, tails, table, sizes):
    _, block_rows, cols = table.shape
    part = jax.ShapeDtypeStruct((CAP * block_rows + TAIL, cols), table.dtype)
    return pl.pallas_call(
        functools.partial(send_kernel, sizes),
        out_shape=(part,) * 7,
        in_specs=[SMEM, VMEM, ANY],
        out_specs=(VMEM,) * 7,
        scratch_shapes=[pltpu.SemaphoreType.DMA((7, CAP))],
        compiler_params=pltpu.CompilerParams(vmem_limit_bytes=8 * MIB),
        cost_estimate=NO_COST,
        name="pack_to_send",
    )(ints, tails, table)


def plan_kernel(sizes, ints, plan, target):
    lists = Lists(ints, *sizes)
    me, (frags, own_count, list_len) = lists.me, sizes
    rows, owners, codes, classes = [], [], [], []
    for k in range(list_len):
        row = lists.row(me, k)
        owner = row // own_count
        low = jnp.minimum(me, owner)
        far = jnp.abs(owner - me)
        code = jnp.int32(0)
        for index, (distance, parity) in enumerate(ROUNDS):
            code = jnp.where(
                (far == distance) & ((low // distance) % 2 == parity), index + 1, code
            )
        rows.append(row)
        owners.append(owner)
        codes.append(code)
        classes.append(jnp.where(code == 0, 0, jnp.maximum(code - 3, 1)))
    for k in range(list_len):
        place = jnp.int32(0)
        rank = jnp.int32(0)
        for j in range(list_len):
            if j < k:
                place += (classes[j] <= classes[k]).astype(jnp.int32)
                rank += (owners[j] == owners[k]).astype(jnp.int32)
            elif j > k:
                place += (classes[j] < classes[k]).astype(jnp.int32)
        plan[0, place] = codes[k]
        plan[1, place] = rank
        plan[2, place] = rows[k]
        plan[3, place] = lists.live(me, k)

    def one(fragment, carry):
        picked, _ = lists.pick(fragment, me)
        for r in range(CAP):
            target[fragment, r] = picked[r]
        return carry

    lax.fori_loop(0, frags, one, 0)


def plan_lists(ints, sizes):
    frags, _, list_len = sizes
    return pl.pallas_call(
        functools.partial(plan_kernel, sizes),
        out_shape=(
            jax.ShapeDtypeStruct((4, list_len), jnp.int32),
            jax.ShapeDtypeStruct((frags, CAP), jnp.int32),
        ),
        in_specs=[SMEM],
        out_specs=(SMEM, SMEM),
        compiler_params=pltpu.CompilerParams(vmem_limit_bytes=4 * MIB),
        cost_estimate=NO_COST,
        name="plan_lists",
    )(ints)


def pack_kernel(first, codes, block, with_energy, plan, *refs):
    count = len(codes)
    if with_energy:
        own_energy, arrived, (out, levels, raw, wide, sems, tail_sems) = (
            refs[0],
            refs[1 : count + 1],
            refs[count + 1 :],
        )
    else:
        arrived, (out, sems) = refs[:count], refs[count:]
    for i in range(2):
        code = plan[0, first + i]
        begin = pl.multiple_of(plan[1, first + i] * block, block)
        rows = pl.ds(i * block, block)
        for source, ref in zip(codes, arrived):

            @pl.when(code == source)
            def _(ref=ref, begin=begin, rows=rows):
                pltpu.make_async_copy(
                    ref.at[pl.ds(begin, block)], out.at[rows], sems.at[i]
                ).start()

    if with_energy:
        own_count = own_energy.shape[0]
        copies = [
            pltpu.make_async_copy(
                ref.at[pl.ds(2 * block, TAIL), pl.ds(0, block)],
                raw.at[pl.ds(n * TAIL, TAIL)],
                tail_sems.at[n],
            )
            for n, ref in enumerate(arrived)
        ]
        for copy in copies:
            copy.start()
        wide[0:own_count, :] = own_energy[...].astype(jnp.float32)
        for copy in copies:
            copy.wait()
        wide[TAIL:, :] = raw[...].astype(jnp.float32)
        levels[...] = jnp.zeros_like(levels)
        for place in range(first + 2):
            row = plan[0, place] * TAIL + plan[2, place] % own_count
            levels[place : place + 1, :] = wide[pl.ds(row, 1), :]
    for i in range(2):
        rows = pl.ds(i * block, block)
        pltpu.make_async_copy(arrived[0].at[rows], out.at[rows], sems.at[i]).wait()


def pack_group(first, block, plan, arrived, own_energy=None):
    codes = tuple(arrived)
    refs = [arrived[c] for c in codes]
    cols, dtype = refs[0].shape[1], refs[0].dtype
    shapes = [jax.ShapeDtypeStruct((2 * block, cols), dtype)]
    scratch = [pltpu.SemaphoreType.DMA((2,))]
    extra = []
    if own_energy is not None:
        shapes.append(jax.ShapeDtypeStruct((plan.shape[1], block), jnp.float32))
        scratch = [
            pltpu.VMEM((len(codes) * TAIL, block), dtype),
            pltpu.VMEM(((len(codes) + 1) * TAIL, block), jnp.float32),
            *scratch,
            pltpu.SemaphoreType.DMA((len(codes),)),
        ]
        extra = [own_energy]
    return pl.pallas_call(
        functools.partial(pack_kernel, first, codes, block, own_energy is not None),
        out_shape=tuple(shapes),
        in_specs=[SMEM] + [VMEM] * len(extra) + [ANY] * len(refs),
        out_specs=(VMEM,) * len(shapes),
        scratch_shapes=scratch,
        compiler_params=pltpu.CompilerParams(vmem_limit_bytes=4 * MIB),
        cost_estimate=NO_COST,
        name="pack_group",
    )(plan, *extra, *refs)


def place_of(aux, b):
    return aux + 4 * b


def contract_kernel(stage, block, width, where, plan, levels, energy, *refs):
    groups = min(stage + 2, 4)
    parts, rest = refs[: groups * 4], refs[groups * 4 :]
    quarters = {2: (0, 2), 3: (1, 3)}.get(stage, (0, 1, 2, 3))
    partial = None
    if stage == 2:
        total, left, grid, occ, scaled, left_sems, grid_sems, occ_sems = rest
    elif stage == 3:
        before, partial, rest = rest[:2], rest[2], rest[3:]
        sent, stay, left, grid, occ, scaled, total, amps, tall, dens = rest[:10]
        left_sems, grid_sems, occ_sems = rest[10:]
    elif stage == 1:
        out, left, grid, occ, scaled, total, amps, tall, left_sems, grid_sems, occ_sems = rest
    else:
        out, left, grid, occ, scaled, total, amps, left_sems, grid_sems, occ_sems = rest
    aux = where[1]
    places = (place_of(aux, 0), place_of(aux, 1))

    def occ_copy(quarter):
        return pltpu.make_async_copy(
            parts[quarter].at[pl.ds(2 * block, TAIL)],
            occ.at[pl.ds(quarter * TAIL, TAIL)],
            occ_sems.at[quarter],
        )

    def left_copy(b, group, begin, quarter):
        return pltpu.make_async_copy(
            parts[group * 4 + quarter].at[pl.ds(begin, block)],
            left.at[pl.ds(b * block, block), pl.ds(quarter * width, width)],
            left_sems.at[b, quarter],
        )

    def grid_copy(slot, group, quarter):
        return pltpu.make_async_copy(
            parts[group * 4 + quarter].at[pl.ds(0, 2 * block)],
            grid.at[pl.ds(slot * 2 * block, 2 * block), pl.ds(quarter * width, width)],
            grid_sems.at[slot, quarter],
        )

    def run(row_count, group_list):
        for quarter in quarters:
            occ_copy(quarter).start()
            for b in range(row_count):
                begin = pl.multiple_of((places[b] % 2) * block, block)
                for group in range(groups):

                    @pl.when(places[b] // 2 == group)
                    def _(b=b, group=group, begin=begin, quarter=quarter):
                        left_copy(b, group, begin, quarter).start()

            for slot, group in enumerate(group_list):
                grid_copy(slot, group, quarter).start()
        height = len(PAIRS) * row_count * block
        span = len(group_list) * 2 * block

        def scale(turn):
            quarter = quarters[turn]
            cols = pl.ds(quarter * width, width)
            orbit = [
                occ[quarter * TAIL + i : quarter * TAIL + i + 1, :].astype(jnp.float32)
                for i in range(3)
            ]
            for b in range(row_count):
                rows = left[pl.ds(b * block, block), cols].astype(jnp.float32)
                for p, (i, j) in enumerate(PAIRS):
                    scaled[turn % 2, pl.ds((p * row_count + b) * block, block), :] = (
                        rows * (orbit[i] * orbit[j])
                    ).astype(jnp.bfloat16)

        def wait_left(turn):
            quarter = quarters[turn]
            occ_copy(quarter).wait()
            for b in range(row_count):
                left_copy(b, 0, 0, quarter).wait()

        wait_left(0)
        scale(0)
        for turn, quarter in enumerate(quarters):
            cols = pl.ds(quarter * width, width)
            for slot, group in enumerate(group_list):
                grid_copy(slot, group, quarter).wait()
            if turn + 1 < len(quarters):
                wait_left(turn + 1)
                scale(turn + 1)
            for step in range(height // 768):
                rows = pl.ds(step * 768, 768)
                term = lax.dot_general(
                    scaled[turn % 2, rows, :],
                    grid[pl.ds(0, span), cols],
                    (((1,), (1,)), ((), ())),
                    preferred_element_type=jnp.float32,
                )
                if turn:
                    total[rows, pl.ds(0, span)] += term
                elif partial is not None:
                    total[rows, pl.ds(0, span)] = term + partial[rows, :]
                else:
                    total[rows, pl.ds(0, span)] = term
        if stage == 2:
            return None
        lane = lax.broadcasted_iota(jnp.int32, (block, block), 1)
        sub = lax.broadcasted_iota(jnp.int32, (block, block), 0)
        sums = []
        for b in range(row_count):
            own_row = energy[pl.ds(places[b], 1), :]
            own_energy = jnp.transpose(jnp.broadcast_to(own_row, (block, block)))
            own_live = sub < plan[3, places[b]]
            for q in range(2 * len(group_list)):
                place = 2 * group_list[q // 2] + q % 2
                their_energy = energy[place : place + 1, :]
                live = own_live & (lane < plan[3, place])
                for p, (i, j) in enumerate(PAIRS):
                    gap = (levels[0, i] + levels[0, j]) - own_energy - their_energy
                    rows = pl.ds((p * row_count + b) * block, block)
                    value = total[rows, pl.ds(q * block, block)]
                    amp = jnp.where(live, value * pl.reciprocal(gap), 0.0).astype(jnp.bfloat16)
                    amps[:, pl.ds(p * span + q * block, block)] = amp
                    if stage == 3:
                        early = amp if b == 0 else jnp.where(aux < 2, amp, jnp.zeros_like(amp))
                        tall[rows, pl.ds(q * block, block)] = early
                    elif stage == 1 and b == 0:
                        tall[pl.ds(p * block, block), pl.ds(q * block, block)] = amp
            wide = amps[:, pl.ds(0, len(PAIRS) * span)]
            sums.append(
                lax.dot_general(
                    wide, wide, (((1,), (1,)), ((), ())), preferred_element_type=jnp.float32
                )
            )
        return sums

    def late_sum(q):
        late = tall[:, pl.ds(q * block, block)]
        return lax.dot_general(
            late, late, (((0,), (0,)), ((), ())), preferred_element_type=jnp.float32
        )

    if stage == 0:
        out[0] = run(1, (0, 1))[0]
    elif stage == 1:

        @pl.when(aux < 2)
        def _():
            out[0], out[1] = run(2, (2,))

        @pl.when(aux >= 2)
        def _():
            out[0] = run(1, (2,))[0]
            out[1] = jnp.zeros(out.shape[1:], out.dtype)

        for q in range(2):
            out[2 + q] = late_sum(q)
    elif stage == 2:
        run(2, (3,))
    else:
        first, second = before
        sums = run(2, (3,))
        dens[0] = sums[0] + (first[0] + second[0])
        share = sums[1] + second[1]
        for q in range(4):
            late = second[2 + q] if q < 2 else late_sum(q - 2)
            dens[1 + q] = late + jnp.where(aux == q, share, 0.0)
        half = block // 2
        side = aux // 2
        stay[...] = dens[:, pl.ds(pl.multiple_of(side * half, half), half), :]
        sent[...] = dens[:, pl.ds(pl.multiple_of((1 - side) * half, half), half), :]


def contract(stage, where, plan, levels, energy, parts, before=()):
    block, width = energy.shape[1], parts[0].shape[1]
    height = len(PAIRS) * 2 * block
    span = (4, 2, 2, 2)[stage] * block
    scratch = [
        pltpu.VMEM((2 * block, 4 * width), jnp.bfloat16),
        pltpu.VMEM((span, 4 * width), jnp.bfloat16),
        pltpu.VMEM((4 * TAIL, width), jnp.bfloat16),
        pltpu.VMEM((2, height, width), jnp.bfloat16),
    ]
    if stage != 2:
        scratch += [
            pltpu.VMEM((height, span), jnp.float32),
            pltpu.VMEM((block, len(PAIRS) * span), jnp.bfloat16),
        ]
    out_specs = VMEM
    if stage == 3:
        scratch += [
            pltpu.VMEM((height, span), jnp.bfloat16),
            pltpu.VMEM((5, block, block), jnp.float32),
        ]
        out_shape = (jax.ShapeDtypeStruct((5, block // 2, block), jnp.float32),) * 2
        out_specs = (VMEM, VMEM)
    elif stage == 2:
        out_shape = jax.ShapeDtypeStruct((height, span), jnp.float32)
    elif stage == 1:
        scratch += [pltpu.VMEM((height // 2, span), jnp.bfloat16)]
        out_shape = jax.ShapeDtypeStruct((4, block, block), jnp.float32)
    else:
        out_shape = jax.ShapeDtypeStruct((1, block, block), jnp.float32)
    scratch += [
        pltpu.SemaphoreType.DMA((2, 4)),
        pltpu.SemaphoreType.DMA((3, 4)),
        pltpu.SemaphoreType.DMA((4,)),
    ]
    cost = NO_COST
    if stage in (1, 2):
        units = (4, 4, 2)[stage] * len(PAIRS) * block * block
        cost = pl.CostEstimate(
            flops=2 * units * 4 * width, bytes_accessed=units * 4, transcendentals=0
        )
    return pl.pallas_call(
        functools.partial(contract_kernel, stage, block, width),
        out_shape=out_shape,
        in_specs=[SMEM] * 3 + [VMEM] + [ANY] * len(parts) + [VMEM] * len(before),
        out_specs=out_specs,
        scratch_shapes=scratch,
        compiler_params=pltpu.CompilerParams(vmem_limit_bytes=26 * MIB),
        cost_estimate=cost,
        name="contract",
    )(where, plan, levels, energy, *parts, *before)


def spread_kernel(own_count, where, plan, kept, came, out):
    aux = where[1]
    out[...] = jnp.zeros_like(out)

    def put(place, value):
        out[plan[2, place] // own_count, plan[1, place]] = value

    put(aux, kept[0])
    put(aux ^ 2, kept[1])
    put(aux ^ 1, came[0])
    put(aux ^ 3, came[1])
    for q in range(4):
        put(4 + q, kept[2 + q] + came[2 + q])


def spread(ints, plan, kept, came, frags, own_count):
    return pl.pallas_call(
        functools.partial(spread_kernel, own_count),
        out_shape=jax.ShapeDtypeStruct((frags, CAP) + kept.shape[1:], kept.dtype),
        in_specs=[SMEM, SMEM, VMEM, VMEM],
        out_specs=VMEM,
        compiler_params=pltpu.CompilerParams(vmem_limit_bytes=4 * MIB),
        name="spread",
    )(ints, plan, kept, came)


def collect_kernel(target, came, out):
    out[...] = jnp.zeros_like(out)

    def one(fragment, carry):
        for r in range(CAP):
            out[target[fragment, r]] += came[fragment, r]
        return carry

    lax.fori_loop(0, came.shape[0], one, 0)


def collect(target, came, own_count):
    return pl.pallas_call(
        collect_kernel,
        out_shape=jax.ShapeDtypeStruct((own_count,) + came.shape[2:], came.dtype),
        in_specs=[SMEM, VMEM],
        out_specs=VMEM,
        compiler_params=pltpu.CompilerParams(vmem_limit_bytes=4 * MIB),
        name="collect",
    )(target, came)


def body(vir_grid, vir_energy, occ_grid, occ_energy, vir_list, vir_rows, owner_map):
    frags = lax.axis_size("frag")
    aux_count = lax.axis_size("aux")
    me = lax.axis_index("frag").astype(jnp.int32)
    aux = lax.axis_index("aux").astype(jnp.int32)
    own_count, block, width = vir_grid.shape
    list_len = vir_list.shape[1]
    sizes = (frags, own_count, list_len)
    ints = jnp.concatenate(
        [me[None], aux[None], owner_map, vir_list.reshape(-1), vir_rows.reshape(-1)]
    )
    occ_count = occ_grid.shape[1]
    tails = jnp.concatenate([
        jnp.pad(occ_grid[0], ((0, TAIL - occ_count), (0, 0))),
        jnp.pad(vir_energy, ((0, TAIL - own_count), (0, width - block))),
    ])
    far_pairs = [(i, i ^ 2) for i in range(aux_count)]
    near_pairs = [(i, i ^ 1) for i in range(aux_count)]

    *outgoing, own = pack_to_send(ints, tails, vir_grid, sizes)

    def over_aux(here, *others):
        far = lax.ppermute(here, "aux", far_pairs)
        near = lax.ppermute(here, "aux", near_pairs)
        onward = after(far, *others) if others else far
        return [here, far, near, lax.ppermute(onward, "aux", near_pairs)]

    def after(value, *others):
        return lax.optimization_barrier((value, *others))[0]

    def send(index, *others):
        distance, parity = ROUNDS[index]
        payload = after(outgoing[index], *others) if others else outgoing[index]
        return lax.ppermute(payload, "frag", round_pairs(distance, parity, frags))

    arrived = {code: send(code - 1) for code in (1, 2, 3, 4)}
    parts = over_aux(own)
    arrived[5] = send(4, *(arrived[c] for c in (1, 2, 3, 4)))
    plan, target = plan_lists(after(ints, arrived[3]), sizes)
    here = pack_group(2, block, plan, {c: arrived[c] for c in range(1, 5)})[0]
    parts += over_aux(here)
    arrived[6] = send(5, parts[5])
    here, early_energy = pack_group(
        4, block, plan, {c: arrived[c] for c in range(1, 6)}, vir_energy
    )
    shared = (ints, plan, occ_energy)
    first = contract(0, *shared, early_energy, parts[:8])
    arrived[6] = after(arrived[6], first)
    last, energy = pack_group(6, block, plan, arrived, vir_energy)
    near = lax.ppermute(last, "aux", near_pairs)
    far = lax.ppermute(last, "aux", far_pairs)
    parts += over_aux(here, near)
    second = contract(1, *shared, early_energy, parts[:12])
    partial = contract(2, *shared, energy, parts + [last, last, near, near])
    far_near = lax.ppermute(after(far, second, partial), "aux", near_pairs)
    parts += [last, far, near, far_near]
    sent, stay = contract(3, *shared, energy, parts, (first, second, partial))

    quarter = block // aux_count
    core = aux % 2
    met = lax.ppermute(sent, "aux", far_pairs)
    both = jnp.concatenate([stay[:1], met[:1], stay[1:] + met[1:]], axis=0)
    sent = lax.dynamic_slice_in_dim(both, (1 - core) * quarter, quarter, 1)
    kept = lax.dynamic_slice_in_dim(both, core * quarter, quarter, 1)
    came = lax.ppermute(sent, "aux", near_pairs)
    outgoing = spread(ints, plan, kept, came, frags, own_count)
    incoming = lax.all_to_all(outgoing, "frag", 0, 0, tiled=True)
    return collect(target, incoming, own_count)


def solution(mesh):
    return jax.shard_map(
        body,
        mesh=mesh,
        in_specs=(
            P("frag", None, "aux"),
            P("frag", None),
            P("frag", None, "aux"),
            P("frag", None),
            P(),
            P(),
            P(),
        ),
        out_specs=P("frag", "aux", None),
        check_vma=False,
    )
```

```python
import functools

import jax
import jax.numpy as jnp
from jax import lax
from jax.experimental import pallas as pl
from jax.experimental.pallas import tpu as pltpu
from jax.sharding import PartitionSpec as P

ROUNDS = ((1, 0), (1, 1), (2, 0), (2, 1), (3, 0), (3, 1))
CAP = 2
TAIL = 16
PAIRS = tuple((i, j) for i in range(3) for j in range(i, 3))
MIB = 2**20
NO_COST = pl.CostEstimate(flops=0, bytes_accessed=0, transcendentals=0)
ANY = pl.BlockSpec(memory_space=pl.ANY)
SMEM = pl.BlockSpec(memory_space=pltpu.SMEM)
VMEM = pl.BlockSpec(memory_space=pltpu.VMEM)


def round_pairs(distance, parity, frags):
    up = [(i, i + distance) for i in range(frags - distance) if (i // distance) % 2 == parity]
    return up + [(b, a) for a, b in up]


def pick(row_of, sizes, fragment, owner):
    _, own_count, list_len = sizes
    count = jnp.int32(0)
    picked = [jnp.int32(0)] * CAP
    for k in range(list_len):
        row = row_of(fragment, k)
        hit = row // own_count == owner
        for r in range(CAP):
            picked[r] = jnp.where(hit & (count == r), row % own_count, picked[r])
        count = count + hit.astype(jnp.int32)
    return picked, count


def send_kernel(sizes, where, map_ref, list_ref, live_ref, energy, occ, table, *refs):
    outs, own, rows, plan, sems = refs[:6], refs[6], refs[7], refs[8], refs[9]
    me, frags = where[0], sizes[0]
    block = table.shape[1]
    copies = []

    def start(out, index, fragment, inside):
        picked, count = pick(lambda f, k: map_ref[list_ref[f, k]], sizes, fragment, me)
        for r in range(CAP):
            copy = pltpu.make_async_copy(
                table.at[picked[r]], out.at[pl.ds(r * block, block)], sems.at[index, r]
            )
            needed = inside & (count > r)
            pl.when(needed)(copy.start)
            copies.append((needed, copy))

    for index, (distance, parity) in enumerate(ROUNDS):
        up = (me // distance) % 2 == parity
        partner = jnp.where(up, me + distance, me - distance)
        inside = (partner >= 0) & (partner < frags)
        start(outs[index], index, jnp.clip(partner, 0, frags - 1), inside)
    start(own, 6, me, me >= 0)

    def look_up(fragment, carry):
        for k in range(sizes[2]):
            rows[fragment, k] = map_ref[list_ref[fragment, k]]
        return carry

    lax.fori_loop(0, frags, look_up, 0)
    make_plan(sizes, me, rows, live_ref, plan)
    for out in outs + (own,):
        out[pl.ds(CAP * block, TAIL), :] = jnp.zeros((TAIL, out.shape[1]), out.dtype)
    for out in outs:
        out[pl.ds(CAP * block, energy.shape[0]), pl.ds(0, block)] = energy[...]
    own[pl.ds(CAP * block, occ.shape[0]), :] = occ[...]
    for needed, copy in copies:
        pl.when(needed)(copy.wait)


def pack_to_send(where, owner_map, vir_list, vir_rows, energy, occ, table, sizes):
    _, block_rows, cols = table.shape
    part = jax.ShapeDtypeStruct((CAP * block_rows + TAIL, cols), table.dtype)
    return pl.pallas_call(
        functools.partial(send_kernel, sizes),
        out_shape=(part,) * 7
        + (
            jax.ShapeDtypeStruct(vir_list.shape, jnp.int32),
            jax.ShapeDtypeStruct((4, vir_list.shape[1]), jnp.int32),
        ),
        in_specs=[SMEM, SMEM, SMEM, SMEM, VMEM, VMEM, ANY],
        out_specs=(VMEM,) * 7 + (SMEM, SMEM),
        scratch_shapes=[pltpu.SemaphoreType.DMA((7, CAP))],
        compiler_params=pltpu.CompilerParams(vmem_limit_bytes=58 * MIB),
        cost_estimate=NO_COST,
        name="pack_to_send",
    )(where, owner_map, vir_list, vir_rows, energy, occ, table)


def make_plan(sizes, me, rows_ref, live_ref, plan):
    _, own_count, list_len = sizes
    rows, owners, codes, classes = [], [], [], []
    for k in range(list_len):
        row = rows_ref[me, k]
        owner = row // own_count
        low = jnp.minimum(me, owner)
        far = jnp.abs(owner - me)
        code = jnp.int32(0)
        for index, (distance, parity) in enumerate(ROUNDS):
            code = jnp.where(
                (far == distance) & ((low // distance) % 2 == parity), index + 1, code
            )
        rows.append(row)
        owners.append(owner)
        codes.append(code)
        classes.append(jnp.where(code == 0, 0, jnp.maximum(code - 3, 1)))
    for k in range(list_len):
        place = jnp.int32(0)
        rank = jnp.int32(0)
        for j in range(list_len):
            if j < k:
                place += (classes[j] <= classes[k]).astype(jnp.int32)
                rank += (owners[j] == owners[k]).astype(jnp.int32)
            elif j > k:
                place += (classes[j] < classes[k]).astype(jnp.int32)
        plan[0, place] = codes[k]
        plan[1, place] = rank
        plan[2, place] = rows[k]
        plan[3, place] = live_ref[me, k]


def pack_kernel(first, codes, block, with_energy, plan, *refs):
    count = len(codes)
    if with_energy:
        own_energy, arrived, (out, levels, raw, wide, sems, tail_sems) = (
            refs[0],
            refs[1 : count + 1],
            refs[count + 1 :],
        )
    else:
        arrived, (out, sems) = refs[:count], refs[count:]
    for i in range(2):
        code = plan[0, first + i]
        begin = pl.multiple_of(plan[1, first + i] * block, block)
        rows = pl.ds(i * block, block)
        for source, ref in zip(codes, arrived):

            @pl.when(code == source)
            def _(ref=ref, begin=begin, rows=rows):
                pltpu.make_async_copy(
                    ref.at[pl.ds(begin, block)], out.at[rows], sems.at[i]
                ).start()

    if with_energy:
        own_count = own_energy.shape[0]
        copies = [
            pltpu.make_async_copy(
                ref.at[pl.ds(2 * block, TAIL), pl.ds(0, block)],
                raw.at[pl.ds(n * TAIL, TAIL)],
                tail_sems.at[n],
            )
            for n, ref in enumerate(arrived)
        ]
        for copy in copies:
            copy.start()
        wide[0:own_count, :] = own_energy[...].astype(jnp.float32)
        for copy in copies:
            copy.wait()
        wide[TAIL:, :] = raw[...].astype(jnp.float32)
        levels[...] = jnp.zeros_like(levels)
        for place in range(first + 2):
            row = plan[0, place] * TAIL + plan[2, place] % own_count
            levels[place : place + 1, :] = wide[pl.ds(row, 1), :]
    for i in range(2):
        rows = pl.ds(i * block, block)
        pltpu.make_async_copy(arrived[0].at[rows], out.at[rows], sems.at[i]).wait()


def pack_group(first, block, plan, arrived, own_energy=None):
    codes = tuple(arrived)
    refs = [arrived[c] for c in codes]
    cols, dtype = refs[0].shape[1], refs[0].dtype
    shapes = [jax.ShapeDtypeStruct((2 * block, cols), dtype)]
    scratch = [pltpu.SemaphoreType.DMA((2,))]
    extra = []
    if own_energy is not None:
        shapes.append(jax.ShapeDtypeStruct((plan.shape[1], block), jnp.float32))
        scratch = [
            pltpu.VMEM((len(codes) * TAIL, block), dtype),
            pltpu.VMEM(((len(codes) + 1) * TAIL, block), jnp.float32),
            *scratch,
            pltpu.SemaphoreType.DMA((len(codes),)),
        ]
        extra = [own_energy]
    return pl.pallas_call(
        functools.partial(pack_kernel, first, codes, block, own_energy is not None),
        out_shape=tuple(shapes),
        in_specs=[SMEM] + [VMEM] * len(extra) + [ANY] * len(refs),
        out_specs=(VMEM,) * len(shapes),
        scratch_shapes=scratch,
        compiler_params=pltpu.CompilerParams(vmem_limit_bytes=4 * MIB),
        cost_estimate=NO_COST,
        name="pack_group",
    )(plan, *extra, *refs)


def place_of(aux, b):
    return aux + 4 * b


def contract_kernel(stage, block, width, own_count, where, plan, levels, energy, *refs):
    groups = min(stage + 2, 4)
    parts, rest = refs[: groups * 4], refs[groups * 4 :]
    quarters = {2: (0, 2), 3: (1, 3)}.get(stage, (0, 1, 2, 3))
    partial = None
    if stage == 2:
        total, left, grid, occ, scaled, left_sems, grid_sems, occ_sems = rest
    elif stage == 3:
        before, partial, rest = rest[:2], rest[2], rest[3:]
        sent, stay, left, grid, occ, scaled, total, amps, tall, dens = rest[:10]
        left_sems, grid_sems, occ_sems = rest[10:]
    elif stage == 1:
        (out, left, grid, occ, scaled, total, amps, tall), rest = rest[:8], rest[8:]
        left_sems, grid_sems, occ_sems = rest
    elif stage == 0:
        rows_ref, out, target, left, grid, occ, scaled, total, amps = rest[:9]
        left_sems, grid_sems, occ_sems = rest[9:]
    aux = where[1]
    places = (place_of(aux, 0), place_of(aux, 1))

    def occ_copy(quarter):
        return pltpu.make_async_copy(
            parts[quarter].at[pl.ds(2 * block, TAIL)],
            occ.at[pl.ds(quarter * TAIL, TAIL)],
            occ_sems.at[quarter],
        )

    def left_copy(b, group, begin, quarter):
        return pltpu.make_async_copy(
            parts[group * 4 + quarter].at[pl.ds(begin, block)],
            left.at[pl.ds(b * block, block), pl.ds(quarter * width, width)],
            left_sems.at[b, quarter],
        )

    def grid_copy(slot, group, quarter):
        return pltpu.make_async_copy(
            parts[group * 4 + quarter].at[pl.ds(0, 2 * block)],
            grid.at[pl.ds(slot * 2 * block, 2 * block), pl.ds(quarter * width, width)],
            grid_sems.at[slot, quarter],
        )

    def run(row_count, group_list):
        for quarter in quarters:
            occ_copy(quarter).start()
            for b in range(row_count):
                begin = pl.multiple_of((places[b] % 2) * block, block)
                for group in range(groups):

                    @pl.when(places[b] // 2 == group)
                    def _(b=b, group=group, begin=begin, quarter=quarter):
                        left_copy(b, group, begin, quarter).start()

            for slot, group in enumerate(group_list):
                grid_copy(slot, group, quarter).start()
        height = len(PAIRS) * row_count * block
        span = len(group_list) * 2 * block

        def scale(turn):
            quarter = quarters[turn]
            cols = pl.ds(quarter * width, width)
            orbit = [
                occ[quarter * TAIL + i : quarter * TAIL + i + 1, :].astype(jnp.float32)
                for i in range(3)
            ]
            for b in range(row_count):
                rows = left[pl.ds(b * block, block), cols].astype(jnp.float32)
                for p, (i, j) in enumerate(PAIRS):
                    scaled[turn % 2, pl.ds((p * row_count + b) * block, block), :] = (
                        rows * (orbit[i] * orbit[j])
                    ).astype(jnp.bfloat16)

        def wait_left(turn):
            quarter = quarters[turn]
            occ_copy(quarter).wait()
            for b in range(row_count):
                left_copy(b, 0, 0, quarter).wait()

        wait_left(0)
        scale(0)
        for turn, quarter in enumerate(quarters):
            cols = pl.ds(quarter * width, width)
            for slot, group in enumerate(group_list):
                grid_copy(slot, group, quarter).wait()
            if turn + 1 < len(quarters):
                wait_left(turn + 1)
                scale(turn + 1)
            for step in range(height // 768):
                rows = pl.ds(step * 768, 768)
                term = lax.dot_general(
                    scaled[turn % 2, rows, :],
                    grid[pl.ds(0, span), cols],
                    (((1,), (1,)), ((), ())),
                    preferred_element_type=jnp.float32,
                )
                if turn:
                    total[rows, pl.ds(0, span)] += term
                elif partial is not None:
                    total[rows, pl.ds(0, span)] = term + partial[rows, :]
                else:
                    total[rows, pl.ds(0, span)] = term
        if stage == 2:
            return None
        lane = lax.broadcasted_iota(jnp.int32, (block, block), 1)
        sub = lax.broadcasted_iota(jnp.int32, (block, block), 0)
        sums = []
        for b in range(row_count):
            own_row = energy[pl.ds(places[b], 1), :]
            own_energy = jnp.transpose(jnp.broadcast_to(own_row, (block, block)))
            own_live = sub < plan[3, places[b]]
            for q in range(2 * len(group_list)):
                place = 2 * group_list[q // 2] + q % 2
                their_energy = energy[place : place + 1, :]
                live = own_live & (lane < plan[3, place])
                for p, (i, j) in enumerate(PAIRS):
                    gap = (levels[0, i] + levels[0, j]) - own_energy - their_energy
                    rows = pl.ds((p * row_count + b) * block, block)
                    value = total[rows, pl.ds(q * block, block)]
                    amp = jnp.where(live, value * pl.reciprocal(gap), 0.0).astype(jnp.bfloat16)
                    amps[:, pl.ds(p * span + q * block, block)] = amp
                    if stage == 3:
                        early = amp if b == 0 else jnp.where(aux < 2, amp, jnp.zeros_like(amp))
                        tall[rows, pl.ds(q * block, block)] = early
                    elif stage == 1 and b == 0:
                        tall[pl.ds(p * block, block), pl.ds(q * block, block)] = amp
            wide = amps[:, pl.ds(0, len(PAIRS) * span)]
            sums.append(
                lax.dot_general(
                    wide, wide, (((1,), (1,)), ((), ())), preferred_element_type=jnp.float32
                )
            )
        return sums

    def late_sum(q):
        late = tall[:, pl.ds(q * block, block)]
        return lax.dot_general(
            late, late, (((0,), (0,)), ((), ())), preferred_element_type=jnp.float32
        )

    if stage == 0:
        frags, list_len = rows_ref.shape

        def one(fragment, carry):
            sizes = (frags, own_count, list_len)
            picked, _ = pick(lambda f, k: rows_ref[f, k], sizes, fragment, where[0])
            for r in range(CAP):
                target[fragment, r] = picked[r]
            return carry

        lax.fori_loop(0, frags, one, 0)
        out[0] = run(1, (0, 1))[0]
    elif stage == 1:

        @pl.when(aux < 2)
        def _():
            out[0], out[1] = run(2, (2,))

        @pl.when(aux >= 2)
        def _():
            out[0] = run(1, (2,))[0]
            out[1] = jnp.zeros(out.shape[1:], out.dtype)

        for q in range(2):
            out[2 + q] = late_sum(q)
    elif stage == 2:
        run(2, (3,))
    else:
        first, second = before
        sums = run(2, (3,))
        dens[0] = sums[0] + (first[0] + second[0])
        share = sums[1] + second[1]
        for q in range(4):
            late = second[2 + q] if q < 2 else late_sum(q - 2)
            dens[1 + q] = late + jnp.where(aux == q, share, 0.0)
        half = block // 2
        side = aux // 2
        stay[...] = dens[:, pl.ds(pl.multiple_of(side * half, half), half), :]
        sent[...] = dens[:, pl.ds(pl.multiple_of((1 - side) * half, half), half), :]


def contract(stage, where, plan, levels, energy, parts, before=(), rows=None, own_count=0):
    block, width = energy.shape[1], parts[0].shape[1]
    height = len(PAIRS) * 2 * block
    span = (4, 2, 2, 2)[stage] * block
    scratch = [
        pltpu.VMEM((2 * block, 4 * width), jnp.bfloat16),
        pltpu.VMEM((span, 4 * width), jnp.bfloat16),
        pltpu.VMEM((4 * TAIL, width), jnp.bfloat16),
        pltpu.VMEM((2, height, width), jnp.bfloat16),
    ]
    if stage != 2:
        scratch += [
            pltpu.VMEM((height, span), jnp.float32),
            pltpu.VMEM((block, len(PAIRS) * span), jnp.bfloat16),
        ]
    out_specs = VMEM
    if stage == 3:
        scratch += [
            pltpu.VMEM((height, span), jnp.bfloat16),
            pltpu.VMEM((5, block, block), jnp.float32),
        ]
        out_shape = (jax.ShapeDtypeStruct((5, block // 2, block), jnp.float32),) * 2
        out_specs = (VMEM, VMEM)
    elif stage == 2:
        out_shape = jax.ShapeDtypeStruct((height, span), jnp.float32)
    elif stage == 1:
        scratch += [pltpu.VMEM((height // 2, span), jnp.bfloat16)]
        out_shape = jax.ShapeDtypeStruct((4, block, block), jnp.float32)
    else:
        out_shape = (
            jax.ShapeDtypeStruct((1, block, block), jnp.float32),
            jax.ShapeDtypeStruct((rows.shape[0], CAP), jnp.int32),
        )
        out_specs = (VMEM, SMEM)
    scratch += [
        pltpu.SemaphoreType.DMA((2, 4)),
        pltpu.SemaphoreType.DMA((3, 4)),
        pltpu.SemaphoreType.DMA((4,)),
    ]
    tables = () if rows is None else (rows,)
    cost = NO_COST
    if stage in (1, 2):
        units = (4, 4, 2)[stage] * len(PAIRS) * block * block
        cost = pl.CostEstimate(
            flops=2 * units * 4 * width, bytes_accessed=units * 4, transcendentals=0
        )
    return pl.pallas_call(
        functools.partial(contract_kernel, stage, block, width, own_count),
        out_shape=out_shape,
        in_specs=[SMEM] * 3
        + [VMEM]
        + [ANY] * len(parts)
        + [VMEM] * len(before)
        + [SMEM] * len(tables),
        out_specs=out_specs,
        scratch_shapes=scratch,
        compiler_params=pltpu.CompilerParams(vmem_limit_bytes=26 * MIB),
        cost_estimate=cost,
        name="contract",
    )(where, plan, levels, energy, *parts, *before, *tables)


def spread_kernel(own_count, where, plan, kept, came, out):
    aux = where[1]
    out[...] = jnp.zeros_like(out)

    def put(place, value):
        out[plan[2, place] // own_count, plan[1, place]] = value

    put(aux, kept[0])
    put(aux ^ 2, kept[1])
    put(aux ^ 1, came[0])
    put(aux ^ 3, came[1])
    for q in range(4):
        put(4 + q, kept[2 + q] + came[2 + q])


def spread(where, plan, kept, came, frags, own_count):
    return pl.pallas_call(
        functools.partial(spread_kernel, own_count),
        out_shape=jax.ShapeDtypeStruct((frags, CAP) + kept.shape[1:], kept.dtype),
        in_specs=[SMEM, SMEM, VMEM, VMEM],
        out_specs=VMEM,
        compiler_params=pltpu.CompilerParams(vmem_limit_bytes=4 * MIB),
        name="spread",
    )(where, plan, kept, came)


def collect_kernel(target, came, out):
    out[...] = jnp.zeros_like(out)

    def one(fragment, carry):
        for r in range(CAP):
            out[target[fragment, r]] += came[fragment, r]
        return carry

    lax.fori_loop(0, came.shape[0], one, 0)


def collect(target, came, own_count):
    return pl.pallas_call(
        collect_kernel,
        out_shape=jax.ShapeDtypeStruct((own_count,) + came.shape[2:], came.dtype),
        in_specs=[SMEM, VMEM],
        out_specs=VMEM,
        compiler_params=pltpu.CompilerParams(vmem_limit_bytes=4 * MIB),
        name="collect",
    )(target, came)


def body(vir_grid, vir_energy, occ_grid, occ_energy, vir_list, vir_rows, owner_map):
    frags = lax.axis_size("frag")
    aux_count = lax.axis_size("aux")
    me = lax.axis_index("frag").astype(jnp.int32)
    aux = lax.axis_index("aux").astype(jnp.int32)
    own_count, block, width = vir_grid.shape
    list_len = vir_list.shape[1]
    sizes = (frags, own_count, list_len)
    where = jnp.stack([me, aux])
    far_pairs = [(i, i ^ 2) for i in range(aux_count)]
    near_pairs = [(i, i ^ 1) for i in range(aux_count)]

    *outgoing, own, rows, plan = pack_to_send(
        where, owner_map, vir_list, vir_rows, vir_energy, occ_grid[0], vir_grid, sizes
    )

    def over_aux(here, *others):
        far = lax.ppermute(here, "aux", far_pairs)
        near = lax.ppermute(here, "aux", near_pairs)
        onward = after(far, *others) if others else far
        return [here, far, near, lax.ppermute(onward, "aux", near_pairs)]

    def after(value, *others):
        return lax.optimization_barrier((value, *others))[0]

    def send(index, *others):
        distance, parity = ROUNDS[index]
        payload = after(outgoing[index], *others) if others else outgoing[index]
        return lax.ppermute(payload, "frag", round_pairs(distance, parity, frags))

    arrived = {code: send(code - 1) for code in (1, 2, 3, 4)}
    parts = over_aux(own)
    arrived[5] = send(4, *(arrived[c] for c in (1, 2, 3, 4)))
    here = pack_group(2, block, plan, {c: arrived[c] for c in range(1, 5)})[0]
    parts += over_aux(here)
    arrived[6] = send(5, parts[5])
    here, early_energy = pack_group(
        4, block, plan, {c: arrived[c] for c in range(1, 6)}, vir_energy
    )
    shared = (where, plan, occ_energy)
    first, target = contract(
        0, *shared, early_energy, parts[:8], rows=rows, own_count=own_count
    )
    arrived[6] = after(arrived[6], first)
    last, energy = pack_group(6, block, plan, arrived, vir_energy)
    near = lax.ppermute(last, "aux", near_pairs)
    far = lax.ppermute(last, "aux", far_pairs)
    parts += over_aux(here, near)
    second = contract(1, *shared, early_energy, parts[:12])
    partial = contract(2, *shared, energy, parts + [last, last, near, near])
    far_near = lax.ppermute(after(far, second, partial), "aux", near_pairs)
    parts += [last, far, near, far_near]
    sent, stay = contract(3, *shared, energy, parts, (first, second, partial))

    quarter = block // aux_count
    core = aux % 2
    met = lax.ppermute(sent, "aux", far_pairs)
    both = jnp.concatenate([stay[:1], met[:1], stay[1:] + met[1:]], axis=0)
    sent = lax.dynamic_slice_in_dim(both, (1 - core) * quarter, quarter, 1)
    kept = lax.dynamic_slice_in_dim(both, core * quarter, quarter, 1)
    came = lax.ppermute(sent, "aux", near_pairs)
    outgoing = spread(where, plan, kept, came, frags, own_count)
    incoming = lax.all_to_all(outgoing, "frag", 0, 0, tiled=True)
    return collect(target, incoming, own_count)


def solution(mesh):
    return jax.shard_map(
        body,
        mesh=mesh,
        in_specs=(
            P("frag", None, "aux"),
            P("frag", None),
            P("frag", None, "aux"),
            P("frag", None),
            P(),
            P(),
            P(),
        ),
        out_specs=P("frag", "aux", None),
        check_vma=False,
    )
```

```python
import functools

import jax
import jax.numpy as jnp
from jax import lax
from jax.experimental import pallas as pl
from jax.experimental.pallas import tpu as pltpu
from jax.sharding import PartitionSpec as P

ROUNDS = ((1, 0), (1, 1), (2, 0), (2, 1), (3, 0), (3, 1))
CAP = 2
TAIL = 16
PAIRS = tuple((i, j) for i in range(3) for j in range(i, 3))
MIB = 2**20
NO_COST = pl.CostEstimate(flops=0, bytes_accessed=0, transcendentals=0)
ANY = pl.BlockSpec(memory_space=pl.ANY)
SMEM = pl.BlockSpec(memory_space=pltpu.SMEM)
VMEM = pl.BlockSpec(memory_space=pltpu.VMEM)


def round_pairs(distance, parity, frags):
    up = [(i, i + distance) for i in range(frags - distance) if (i // distance) % 2 == parity]
    return up + [(b, a) for a, b in up]


class Lists:
    def __init__(self, ref, frags, own_count, list_len):
        self.ref, self.frags, self.own_count, self.list_len = ref, frags, own_count, list_len
        self.listed = 2 + frags * own_count
        self.me, self.aux = ref[0], ref[1]

    def row(self, fragment, k):
        return self.ref[2 + self.ref[self.listed + fragment * self.list_len + k]]

    def live(self, fragment, k):
        return self.ref[self.listed + (self.frags + fragment) * self.list_len + k]

    def pick(self, fragment, owner):
        count = jnp.int32(0)
        picked = [jnp.int32(0)] * CAP
        for k in range(self.list_len):
            row = self.row(fragment, k)
            hit = row // self.own_count == owner
            for r in range(CAP):
                picked[r] = jnp.where(hit & (count == r), row % self.own_count, picked[r])
            count = count + hit.astype(jnp.int32)
        return picked, count


def send_kernel(sizes, ints, tails, table, *refs):
    outs, own, sems = refs[:6], refs[6], refs[7]
    lists = Lists(ints, *sizes)
    me, frags = lists.me, lists.frags
    block = table.shape[1]
    copies = []

    def start(out, index, fragment, inside):
        picked, count = lists.pick(fragment, me)
        for r in range(CAP):
            copy = pltpu.make_async_copy(
                table.at[picked[r]], out.at[pl.ds(r * block, block)], sems.at[index, r]
            )
            needed = inside & (count > r)
            pl.when(needed)(copy.start)
            copies.append((needed, copy))

    for index, (distance, parity) in enumerate(ROUNDS):
        up = (me // distance) % 2 == parity
        partner = jnp.where(up, me + distance, me - distance)
        inside = (partner >= 0) & (partner < frags)
        start(outs[index], index, jnp.clip(partner, 0, frags - 1), inside)
    start(own, 6, me, me >= 0)
    own[pl.ds(CAP * block, TAIL), :] = tails[pl.ds(0, TAIL), :]
    for out in outs:
        out[pl.ds(CAP * block, TAIL), :] = tails[pl.ds(TAIL, TAIL), :]
    for needed, copy in copies:
        pl.when(needed)(copy.wait)


def pack_to_send(ints, tails, table, sizes):
    _, block_rows, cols = table.shape
    part = jax.ShapeDtypeStruct((CAP * block_rows + TAIL, cols), table.dtype)
    return pl.pallas_call(
        functools.partial(send_kernel, sizes),
        out_shape=(part,) * 7,
        in_specs=[SMEM, VMEM, ANY],
        out_specs=(VMEM,) * 7,
        scratch_shapes=[pltpu.SemaphoreType.DMA((7, CAP))],
        compiler_params=pltpu.CompilerParams(vmem_limit_bytes=8 * MIB),
        cost_estimate=NO_COST,
        name="pack_to_send",
    )(ints, tails, table)


def plan_kernel(sizes, ints, plan, target):
    lists = Lists(ints, *sizes)
    me, (frags, own_count, list_len) = lists.me, sizes
    rows, owners, codes, classes = [], [], [], []
    for k in range(list_len):
        row = lists.row(me, k)
        owner = row // own_count
        low = jnp.minimum(me, owner)
        far = jnp.abs(owner - me)
        code = jnp.int32(0)
        for index, (distance, parity) in enumerate(ROUNDS):
            code = jnp.where(
                (far == distance) & ((low // distance) % 2 == parity), index + 1, code
            )
        rows.append(row)
        owners.append(owner)
        codes.append(code)
        classes.append(jnp.where(code == 0, 0, jnp.maximum(code - 3, 1)))
    for k in range(list_len):
        place = jnp.int32(0)
        rank = jnp.int32(0)
        for j in range(list_len):
            if j < k:
                place += (classes[j] <= classes[k]).astype(jnp.int32)
                rank += (owners[j] == owners[k]).astype(jnp.int32)
            elif j > k:
                place += (classes[j] < classes[k]).astype(jnp.int32)
        plan[0, place] = codes[k]
        plan[1, place] = rank
        plan[2, place] = rows[k]
        plan[3, place] = lists.live(me, k)

    def one(fragment, carry):
        picked, _ = lists.pick(fragment, me)
        for r in range(CAP):
            target[fragment, r] = picked[r]
        return carry

    lax.fori_loop(0, frags, one, 0)


def plan_lists(ints, sizes):
    frags, _, list_len = sizes
    return pl.pallas_call(
        functools.partial(plan_kernel, sizes),
        out_shape=(
            jax.ShapeDtypeStruct((4, list_len), jnp.int32),
            jax.ShapeDtypeStruct((frags, CAP), jnp.int32),
        ),
        in_specs=[SMEM],
        out_specs=(SMEM, SMEM),
        compiler_params=pltpu.CompilerParams(vmem_limit_bytes=4 * MIB),
        cost_estimate=NO_COST,
        name="plan_lists",
    )(ints)


def pack_kernel(first, codes, block, with_energy, plan, *refs):
    count = len(codes)
    if with_energy:
        own_energy, arrived, (out, levels, raw, wide, sems, tail_sems) = (
            refs[0],
            refs[1 : count + 1],
            refs[count + 1 :],
        )
    else:
        arrived, (out, sems) = refs[:count], refs[count:]
    for i in range(2):
        code = plan[0, first + i]
        begin = pl.multiple_of(plan[1, first + i] * block, block)
        rows = pl.ds(i * block, block)
        for source, ref in zip(codes, arrived):

            @pl.when(code == source)
            def _(ref=ref, begin=begin, rows=rows):
                pltpu.make_async_copy(
                    ref.at[pl.ds(begin, block)], out.at[rows], sems.at[i]
                ).start()

    if with_energy:
        own_count = own_energy.shape[0]
        copies = [
            pltpu.make_async_copy(
                ref.at[pl.ds(2 * block, TAIL), pl.ds(0, block)],
                raw.at[pl.ds(n * TAIL, TAIL)],
                tail_sems.at[n],
            )
            for n, ref in enumerate(arrived)
        ]
        for copy in copies:
            copy.start()
        wide[0:own_count, :] = own_energy[...].astype(jnp.float32)
        for copy in copies:
            copy.wait()
        wide[TAIL:, :] = raw[...].astype(jnp.float32)
        levels[...] = jnp.zeros_like(levels)
        for place in range(first + 2):
            row = plan[0, place] * TAIL + plan[2, place] % own_count
            levels[place : place + 1, :] = wide[pl.ds(row, 1), :]
    for i in range(2):
        rows = pl.ds(i * block, block)
        pltpu.make_async_copy(arrived[0].at[rows], out.at[rows], sems.at[i]).wait()


def pack_group(first, block, plan, arrived, own_energy=None):
    codes = tuple(arrived)
    refs = [arrived[c] for c in codes]
    cols, dtype = refs[0].shape[1], refs[0].dtype
    shapes = [jax.ShapeDtypeStruct((2 * block, cols), dtype)]
    scratch = [pltpu.SemaphoreType.DMA((2,))]
    extra = []
    if own_energy is not None:
        shapes.append(jax.ShapeDtypeStruct((plan.shape[1], block), jnp.float32))
        scratch = [
            pltpu.VMEM((len(codes) * TAIL, block), dtype),
            pltpu.VMEM(((len(codes) + 1) * TAIL, block), jnp.float32),
            *scratch,
            pltpu.SemaphoreType.DMA((len(codes),)),
        ]
        extra = [own_energy]
    return pl.pallas_call(
        functools.partial(pack_kernel, first, codes, block, own_energy is not None),
        out_shape=tuple(shapes),
        in_specs=[SMEM] + [VMEM] * len(extra) + [ANY] * len(refs),
        out_specs=(VMEM,) * len(shapes),
        scratch_shapes=scratch,
        compiler_params=pltpu.CompilerParams(vmem_limit_bytes=4 * MIB),
        cost_estimate=NO_COST,
        name="pack_group",
    )(plan, *extra, *refs)


def place_of(aux, b):
    return aux + 4 * b


def contract_kernel(stage, block, width, where, plan, levels, energy, *refs):
    groups = min(stage + 2, 4)
    parts, rest = refs[: groups * 4], refs[groups * 4 :]
    quarters = {2: (0, 2), 3: (1, 3)}.get(stage, (0, 1, 2, 3))
    partial = None
    if stage == 2:
        total, left, grid, occ, scaled, left_sems, grid_sems, occ_sems = rest
    elif stage == 3:
        before, partial, rest = rest[:2], rest[2], rest[3:]
        sent, stay, left, grid, occ, scaled, total, amps, tall, dens = rest[:10]
        left_sems, grid_sems, occ_sems = rest[10:]
    elif stage == 1:
        out, left, grid, occ, scaled, total, amps, tall, left_sems, grid_sems, occ_sems = rest
    else:
        out, left, grid, occ, scaled, total, amps, left_sems, grid_sems, occ_sems = rest
    aux = where[1]
    places = (place_of(aux, 0), place_of(aux, 1))

    def occ_copy(quarter):
        return pltpu.make_async_copy(
            parts[quarter].at[pl.ds(2 * block, TAIL)],
            occ.at[pl.ds(quarter * TAIL, TAIL)],
            occ_sems.at[quarter],
        )

    def left_copy(b, group, begin, quarter):
        return pltpu.make_async_copy(
            parts[group * 4 + quarter].at[pl.ds(begin, block)],
            left.at[pl.ds(b * block, block), pl.ds(quarter * width, width)],
            left_sems.at[b, quarter],
        )

    def grid_copy(slot, group, quarter):
        return pltpu.make_async_copy(
            parts[group * 4 + quarter].at[pl.ds(0, 2 * block)],
            grid.at[pl.ds(slot * 2 * block, 2 * block), pl.ds(quarter * width, width)],
            grid_sems.at[slot, quarter],
        )

    def run(row_count, group_list):
        for quarter in quarters:
            occ_copy(quarter).start()
            for b in range(row_count):
                begin = pl.multiple_of((places[b] % 2) * block, block)
                for group in range(groups):

                    @pl.when(places[b] // 2 == group)
                    def _(b=b, group=group, begin=begin, quarter=quarter):
                        left_copy(b, group, begin, quarter).start()

            for slot, group in enumerate(group_list):
                grid_copy(slot, group, quarter).start()
        height = len(PAIRS) * row_count * block
        span = len(group_list) * 2 * block

        def scale(turn):
            quarter = quarters[turn]
            cols = pl.ds(quarter * width, width)
            orbit = [
                occ[quarter * TAIL + i : quarter * TAIL + i + 1, :].astype(jnp.float32)
                for i in range(3)
            ]
            for b in range(row_count):
                rows = left[pl.ds(b * block, block), cols].astype(jnp.float32)
                for p, (i, j) in enumerate(PAIRS):
                    scaled[turn % 2, pl.ds((p * row_count + b) * block, block), :] = (
                        rows * (orbit[i] * orbit[j])
                    ).astype(jnp.bfloat16)

        def wait_left(turn):
            quarter = quarters[turn]
            occ_copy(quarter).wait()
            for b in range(row_count):
                left_copy(b, 0, 0, quarter).wait()

        wait_left(0)
        scale(0)
        for turn, quarter in enumerate(quarters):
            cols = pl.ds(quarter * width, width)
            for slot, group in enumerate(group_list):
                grid_copy(slot, group, quarter).wait()
            if turn + 1 < len(quarters):
                wait_left(turn + 1)
                scale(turn + 1)
            for step in range(height // 768):
                rows = pl.ds(step * 768, 768)
                term = lax.dot_general(
                    scaled[turn % 2, rows, :],
                    grid[pl.ds(0, span), cols],
                    (((1,), (1,)), ((), ())),
                    preferred_element_type=jnp.float32,
                )
                if turn:
                    total[rows, pl.ds(0, span)] += term
                elif partial is not None:
                    total[rows, pl.ds(0, span)] = term + partial[rows, :]
                else:
                    total[rows, pl.ds(0, span)] = term
        if stage == 2:
            return None
        lane = lax.broadcasted_iota(jnp.int32, (block, block), 1)
        sub = lax.broadcasted_iota(jnp.int32, (block, block), 0)
        sums = []
        for b in range(row_count):
            own_row = energy[pl.ds(places[b], 1), :]
            own_energy = jnp.transpose(jnp.broadcast_to(own_row, (block, block)))
            own_live = sub < plan[3, places[b]]
            for q in range(2 * len(group_list)):
                place = 2 * group_list[q // 2] + q % 2
                their_energy = energy[place : place + 1, :]
                live = own_live & (lane < plan[3, place])
                for p, (i, j) in enumerate(PAIRS):
                    gap = (levels[0, i] + levels[0, j]) - own_energy - their_energy
                    rows = pl.ds((p * row_count + b) * block, block)
                    value = total[rows, pl.ds(q * block, block)]
                    amp = jnp.where(live, value * pl.reciprocal(gap), 0.0).astype(jnp.bfloat16)
                    amps[:, pl.ds(p * span + q * block, block)] = amp
                    if stage == 3:
                        early = amp if b == 0 else jnp.where(aux < 2, amp, jnp.zeros_like(amp))
                        tall[rows, pl.ds(q * block, block)] = early
                    elif stage == 1 and b == 0:
                        tall[pl.ds(p * block, block), pl.ds(q * block, block)] = amp
            wide = amps[:, pl.ds(0, len(PAIRS) * span)]
            sums.append(
                lax.dot_general(
                    wide, wide, (((1,), (1,)), ((), ())), preferred_element_type=jnp.float32
                )
            )
        return sums

    def late_sum(q):
        late = tall[:, pl.ds(q * block, block)]
        return lax.dot_general(
            late, late, (((0,), (0,)), ((), ())), preferred_element_type=jnp.float32
        )

    if stage == 0:
        out[0] = run(1, (0, 1))[0]
    elif stage == 1:

        @pl.when(aux < 2)
        def _():
            out[0], out[1] = run(2, (2,))

        @pl.when(aux >= 2)
        def _():
            out[0] = run(1, (2,))[0]
            out[1] = jnp.zeros(out.shape[1:], out.dtype)

        for q in range(2):
            out[2 + q] = late_sum(q)
    elif stage == 2:
        run(2, (3,))
    else:
        first, second = before
        sums = run(2, (3,))
        dens[0] = sums[0] + (first[0] + second[0])
        share = sums[1] + second[1]
        for q in range(4):
            late = second[2 + q] if q < 2 else late_sum(q - 2)
            dens[1 + q] = late + jnp.where(aux == q, share, 0.0)
        half = block // 2
        side = aux // 2
        stay[...] = dens[:, pl.ds(pl.multiple_of(side * half, half), half), :]
        away = dens[:, pl.ds(pl.multiple_of((1 - side) * half, half), half), :]
        sent[...] = away.astype(jnp.bfloat16)


def contract(stage, where, plan, levels, energy, parts, before=()):
    block, width = energy.shape[1], parts[0].shape[1]
    height = len(PAIRS) * 2 * block
    span = (4, 2, 2, 2)[stage] * block
    scratch = [
        pltpu.VMEM((2 * block, 4 * width), jnp.bfloat16),
        pltpu.VMEM((span, 4 * width), jnp.bfloat16),
        pltpu.VMEM((4 * TAIL, width), jnp.bfloat16),
        pltpu.VMEM((2, height, width), jnp.bfloat16),
    ]
    if stage != 2:
        scratch += [
            pltpu.VMEM((height, span), jnp.float32),
            pltpu.VMEM((block, len(PAIRS) * span), jnp.bfloat16),
        ]
    out_specs = VMEM
    if stage == 3:
        scratch += [
            pltpu.VMEM((height, span), jnp.bfloat16),
            pltpu.VMEM((5, block, block), jnp.float32),
        ]
        out_shape = tuple(
            jax.ShapeDtypeStruct((5, block // 2, block), dtype)
            for dtype in (jnp.bfloat16, jnp.float32)
        )
        out_specs = (VMEM, VMEM)
    elif stage == 2:
        out_shape = jax.ShapeDtypeStruct((height, span), jnp.float32)
    elif stage == 1:
        scratch += [pltpu.VMEM((height // 2, span), jnp.bfloat16)]
        out_shape = jax.ShapeDtypeStruct((4, block, block), jnp.float32)
    else:
        out_shape = jax.ShapeDtypeStruct((1, block, block), jnp.float32)
    scratch += [
        pltpu.SemaphoreType.DMA((2, 4)),
        pltpu.SemaphoreType.DMA((3, 4)),
        pltpu.SemaphoreType.DMA((4,)),
    ]
    cost = NO_COST
    if stage in (1, 2):
        units = (4, 4, 2)[stage] * len(PAIRS) * block * block
        cost = pl.CostEstimate(
            flops=2 * units * 4 * width, bytes_accessed=units * 4, transcendentals=0
        )
    return pl.pallas_call(
        functools.partial(contract_kernel, stage, block, width),
        out_shape=out_shape,
        in_specs=[SMEM] * 3 + [VMEM] + [ANY] * len(parts) + [VMEM] * len(before),
        out_specs=out_specs,
        scratch_shapes=scratch,
        compiler_params=pltpu.CompilerParams(vmem_limit_bytes=26 * MIB),
        cost_estimate=cost,
        name="contract",
    )(where, plan, levels, energy, *parts, *before)


def spread_kernel(own_count, where, plan, kept, came, out):
    aux = where[1]
    out[...] = jnp.zeros_like(out)

    def put(place, value):
        out[plan[2, place] // own_count, plan[1, place]] = value.astype(out.dtype)

    put(aux, kept[0])
    put(aux ^ 2, kept[1])
    put(aux ^ 1, came[0])
    put(aux ^ 3, came[1])
    for q in range(4):
        put(4 + q, kept[2 + q] + came[2 + q])


def spread(ints, plan, kept, came, frags, own_count):
    return pl.pallas_call(
        functools.partial(spread_kernel, own_count),
        out_shape=jax.ShapeDtypeStruct((frags, CAP) + kept.shape[1:], jnp.bfloat16),
        in_specs=[SMEM, SMEM, VMEM, VMEM],
        out_specs=VMEM,
        compiler_params=pltpu.CompilerParams(vmem_limit_bytes=4 * MIB),
        name="spread",
    )(ints, plan, kept, came)


def collect_kernel(target, came, out):
    out[...] = jnp.zeros_like(out)

    def one(fragment, carry):
        for r in range(CAP):
            out[target[fragment, r]] += came[fragment, r].astype(jnp.float32)
        return carry

    lax.fori_loop(0, came.shape[0], one, 0)


def collect(target, came, own_count):
    return pl.pallas_call(
        collect_kernel,
        out_shape=jax.ShapeDtypeStruct((own_count,) + came.shape[2:], jnp.float32),
        in_specs=[SMEM, VMEM],
        out_specs=VMEM,
        compiler_params=pltpu.CompilerParams(vmem_limit_bytes=4 * MIB),
        name="collect",
    )(target, came)


def body(vir_grid, vir_energy, occ_grid, occ_energy, vir_list, vir_rows, owner_map):
    frags = lax.axis_size("frag")
    aux_count = lax.axis_size("aux")
    me = lax.axis_index("frag").astype(jnp.int32)
    aux = lax.axis_index("aux").astype(jnp.int32)
    own_count, block, width = vir_grid.shape
    list_len = vir_list.shape[1]
    sizes = (frags, own_count, list_len)
    ints = jnp.concatenate(
        [me[None], aux[None], owner_map, vir_list.reshape(-1), vir_rows.reshape(-1)]
    )
    occ_count = occ_grid.shape[1]
    tails = jnp.concatenate([
        jnp.pad(occ_grid[0], ((0, TAIL - occ_count), (0, 0))),
        jnp.pad(vir_energy, ((0, TAIL - own_count), (0, width - block))),
    ])
    far_pairs = [(i, i ^ 2) for i in range(aux_count)]
    near_pairs = [(i, i ^ 1) for i in range(aux_count)]

    *outgoing, own = pack_to_send(ints, tails, vir_grid, sizes)

    def over_aux(here, *others):
        far = lax.ppermute(here, "aux", far_pairs)
        near = lax.ppermute(here, "aux", near_pairs)
        onward = after(far, *others) if others else far
        return [here, far, near, lax.ppermute(onward, "aux", near_pairs)]

    def after(value, *others):
        return lax.optimization_barrier((value, *others))[0]

    def send(index, *others):
        distance, parity = ROUNDS[index]
        payload = after(outgoing[index], *others) if others else outgoing[index]
        return lax.ppermute(payload, "frag", round_pairs(distance, parity, frags))

    arrived = {code: send(code - 1) for code in (1, 2, 3, 4)}
    parts = over_aux(own)
    arrived[5] = send(4, *(arrived[c] for c in (1, 2, 3, 4)))
    plan, target = plan_lists(after(ints, arrived[3]), sizes)
    here = pack_group(2, block, plan, {c: arrived[c] for c in range(1, 5)})[0]
    parts += over_aux(here)
    arrived[6] = send(5, parts[5])
    here, early_energy = pack_group(
        4, block, plan, {c: arrived[c] for c in range(1, 6)}, vir_energy
    )
    shared = (ints, plan, occ_energy)
    first = contract(0, *shared, early_energy, parts[:8])
    arrived[6] = after(arrived[6], first)
    last, energy = pack_group(6, block, plan, arrived, vir_energy)
    near = lax.ppermute(last, "aux", near_pairs)
    far = lax.ppermute(last, "aux", far_pairs)
    parts += over_aux(here, near)
    second = contract(1, *shared, early_energy, parts[:12])
    partial = contract(2, *shared, energy, parts + [last, last, near, near])
    far_near = lax.ppermute(after(far, second, partial), "aux", near_pairs)
    parts += [last, far, near, far_near]
    sent, stay = contract(3, *shared, energy, parts, (first, second, partial))

    quarter = block // aux_count
    core = aux % 2
    met = lax.ppermute(sent, "aux", far_pairs).astype(jnp.float32)
    both = jnp.concatenate([stay[:1], met[:1], stay[1:] + met[1:]], axis=0)
    sent = lax.dynamic_slice_in_dim(both, (1 - core) * quarter, quarter, 1)
    kept = lax.dynamic_slice_in_dim(both, core * quarter, quarter, 1)
    came = lax.ppermute(sent, "aux", near_pairs)
    outgoing = spread(ints, plan, kept, came, frags, own_count)
    incoming = lax.all_to_all(outgoing, "frag", 0, 0, tiled=True)
    return collect(target, incoming, own_count)


def solution(mesh):
    return jax.shard_map(
        body,
        mesh=mesh,
        in_specs=(
            P("frag", None, "aux"),
            P("frag", None),
            P("frag", None, "aux"),
            P("frag", None),
            P(),
            P(),
            P(),
        ),
        out_specs=P("frag", "aux", None),
        check_vma=False,
    )
```

```python
import functools

import jax
import jax.numpy as jnp
from jax import lax
from jax.experimental import pallas as pl
from jax.experimental.pallas import tpu as pltpu
from jax.sharding import PartitionSpec as P

ROUNDS = ((1, 0), (1, 1), (2, 0), (2, 1), (3, 0), (3, 1))
CAP = 2
TAIL = 16
PAIRS = tuple((i, j) for i in range(3) for j in range(i, 3))
MIB = 2**20
NO_COST = pl.CostEstimate(flops=0, bytes_accessed=0, transcendentals=0)
ANY = pl.BlockSpec(memory_space=pl.ANY)
SMEM = pl.BlockSpec(memory_space=pltpu.SMEM)
VMEM = pl.BlockSpec(memory_space=pltpu.VMEM)


def round_pairs(distance, parity, frags):
    up = [(i, i + distance) for i in range(frags - distance) if (i // distance) % 2 == parity]
    return up + [(b, a) for a, b in up]


class Lists:
    def __init__(self, ints, listed, frags, own_count, list_len):
        self.ints, self.listed = ints, listed
        self.frags, self.own_count, self.list_len = frags, own_count, list_len
        self.me = ints[0]

    def row(self, fragment, k):
        return self.ints[2 + self.listed[fragment, k]]

    def pick(self, fragment, owner):
        count = jnp.int32(0)
        picked = [jnp.int32(0)] * CAP
        for k in range(self.list_len):
            row = self.row(fragment, k)
            hit = row // self.own_count == owner
            for r in range(CAP):
                picked[r] = jnp.where(hit & (count == r), row % self.own_count, picked[r])
            count = count + hit.astype(jnp.int32)
        return picked, count


def send_kernel(sizes, ints, listed, tails, table, *refs):
    outs, own, sems = refs[:6], refs[6], refs[7]
    lists = Lists(ints, listed, *sizes)
    me, frags = lists.me, lists.frags
    block = table.shape[1]
    copies = []

    def start(out, index, fragment, inside):
        picked, count = lists.pick(fragment, me)
        for r in range(CAP):
            copy = pltpu.make_async_copy(
                table.at[picked[r]], out.at[pl.ds(r * block, block)], sems.at[index, r]
            )
            needed = inside & (count > r)
            pl.when(needed)(copy.start)
            copies.append((needed, copy))

    for index, (distance, parity) in enumerate(ROUNDS):
        up = (me // distance) % 2 == parity
        partner = jnp.where(up, me + distance, me - distance)
        inside = (partner >= 0) & (partner < frags)
        start(outs[index], index, jnp.clip(partner, 0, frags - 1), inside)
    start(own, 6, me, me >= 0)
    own[pl.ds(CAP * block, TAIL), :] = tails[pl.ds(0, TAIL), :]
    for out in outs:
        out[pl.ds(CAP * block, TAIL), :] = tails[pl.ds(TAIL, TAIL), :]
    for needed, copy in copies:
        pl.when(needed)(copy.wait)


def pack_to_send(ints, vir_list, tails, table, sizes):
    _, block_rows, cols = table.shape
    part = jax.ShapeDtypeStruct((CAP * block_rows + TAIL, cols), table.dtype)
    return pl.pallas_call(
        functools.partial(send_kernel, sizes),
        out_shape=(part,) * 7,
        in_specs=[SMEM, SMEM, VMEM, ANY],
        out_specs=(VMEM,) * 7,
        scratch_shapes=[pltpu.SemaphoreType.DMA((7, CAP))],
        compiler_params=pltpu.CompilerParams(vmem_limit_bytes=8 * MIB),
        cost_estimate=NO_COST,
        name="pack_to_send",
    )(ints, vir_list, tails, table)


def plan_kernel(sizes, ints, listed, plan, target):
    lists = Lists(ints, listed, *sizes)
    me, (frags, own_count, list_len) = lists.me, sizes
    rows, owners, codes, classes = [], [], [], []
    for k in range(list_len):
        row = lists.row(me, k)
        owner = row // own_count
        low = jnp.minimum(me, owner)
        far = jnp.abs(owner - me)
        code = jnp.int32(0)
        for index, (distance, parity) in enumerate(ROUNDS):
            code = jnp.where(
                (far == distance) & ((low // distance) % 2 == parity), index + 1, code
            )
        rows.append(row)
        owners.append(owner)
        codes.append(code)
        classes.append(jnp.where(code == 0, 0, jnp.maximum(code - 3, 1)))
    for k in range(list_len):
        place = jnp.int32(0)
        rank = jnp.int32(0)
        for j in range(list_len):
            if j < k:
                place += (classes[j] <= classes[k]).astype(jnp.int32)
                rank += (owners[j] == owners[k]).astype(jnp.int32)
            elif j > k:
                place += (classes[j] < classes[k]).astype(jnp.int32)
        plan[0, place] = codes[k]
        plan[1, place] = rank
        plan[2, place] = rows[k]
        plan[3, place] = jnp.int32(k)

    def one(fragment, carry):
        picked, _ = lists.pick(fragment, me)
        for r in range(CAP):
            target[fragment, r] = picked[r]
        return carry

    lax.fori_loop(0, frags, one, 0)


def plan_lists(ints, vir_list, sizes):
    frags, _, list_len = sizes
    return pl.pallas_call(
        functools.partial(plan_kernel, sizes),
        out_shape=(
            jax.ShapeDtypeStruct((4, list_len), jnp.int32),
            jax.ShapeDtypeStruct((frags, CAP), jnp.int32),
        ),
        in_specs=[SMEM, SMEM],
        out_specs=(SMEM, SMEM),
        compiler_params=pltpu.CompilerParams(vmem_limit_bytes=4 * MIB),
        cost_estimate=NO_COST,
        name="plan_lists",
    )(ints, vir_list)


def pack_kernel(first, codes, block, with_energy, plan, *refs):
    count = len(codes)
    if with_energy:
        own_energy, arrived, (out, levels, raw, wide, sems, tail_sems) = (
            refs[0],
            refs[1 : count + 1],
            refs[count + 1 :],
        )
    else:
        arrived, (out, sems) = refs[:count], refs[count:]
    for i in range(2):
        code = plan[0, first + i]
        begin = pl.multiple_of(plan[1, first + i] * block, block)
        rows = pl.ds(i * block, block)
        for source, ref in zip(codes, arrived):

            @pl.when(code == source)
            def _(ref=ref, begin=begin, rows=rows):
                pltpu.make_async_copy(
                    ref.at[pl.ds(begin, block)], out.at[rows], sems.at[i]
                ).start()

    if with_energy:
        own_count = own_energy.shape[0]
        copies = [
            pltpu.make_async_copy(
                ref.at[pl.ds(2 * block, TAIL), pl.ds(0, block)],
                raw.at[pl.ds(n * TAIL, TAIL)],
                tail_sems.at[n],
            )
            for n, ref in enumerate(arrived)
        ]
        for copy in copies:
            copy.start()
        wide[0:own_count, :] = own_energy[...].astype(jnp.float32)
        for copy in copies:
            copy.wait()
        wide[TAIL:, :] = raw[...].astype(jnp.float32)
        levels[...] = jnp.zeros_like(levels)
        for place in range(first + 2):
            row = plan[0, place] * TAIL + plan[2, place] % own_count
            levels[place : place + 1, :] = wide[pl.ds(row, 1), :]
    for i in range(2):
        rows = pl.ds(i * block, block)
        pltpu.make_async_copy(arrived[0].at[rows], out.at[rows], sems.at[i]).wait()


def pack_group(first, block, plan, arrived, own_energy=None):
    codes = tuple(arrived)
    refs = [arrived[c] for c in codes]
    cols, dtype = refs[0].shape[1], refs[0].dtype
    shapes = [jax.ShapeDtypeStruct((2 * block, cols), dtype)]
    scratch = [pltpu.SemaphoreType.DMA((2,))]
    extra = []
    if own_energy is not None:
        shapes.append(jax.ShapeDtypeStruct((plan.shape[1], block), jnp.float32))
        scratch = [
            pltpu.VMEM((len(codes) * TAIL, block), dtype),
            pltpu.VMEM(((len(codes) + 1) * TAIL, block), jnp.float32),
            *scratch,
            pltpu.SemaphoreType.DMA((len(codes),)),
        ]
        extra = [own_energy]
    return pl.pallas_call(
        functools.partial(pack_kernel, first, codes, block, own_energy is not None),
        out_shape=tuple(shapes),
        in_specs=[SMEM] + [VMEM] * len(extra) + [ANY] * len(refs),
        out_specs=(VMEM,) * len(shapes),
        scratch_shapes=scratch,
        compiler_params=pltpu.CompilerParams(vmem_limit_bytes=4 * MIB),
        cost_estimate=NO_COST,
        name="pack_group",
    )(plan, *extra, *refs)


def place_of(aux, b):
    return aux + 4 * b


def contract_kernel(stage, block, width, where, plan, levels, rows_ref, energy, *refs):
    groups = min(stage + 2, 4)
    parts, rest = refs[: groups * 4], refs[groups * 4 :]
    quarters = {2: (0, 2), 3: (1, 3)}.get(stage, (0, 1, 2, 3))
    partial = None
    if stage == 2:
        total, left, grid, occ, scaled, left_sems, grid_sems, occ_sems = rest
    elif stage == 3:
        before, partial, rest = rest[:2], rest[2], rest[3:]
        sent, stay, left, grid, occ, scaled, total, amps, tall, dens = rest[:10]
        left_sems, grid_sems, occ_sems = rest[10:]
    elif stage == 1:
        out, left, grid, occ, scaled, total, amps, tall, left_sems, grid_sems, occ_sems = rest
    else:
        out, left, grid, occ, scaled, total, amps, left_sems, grid_sems, occ_sems = rest
    aux = where[1]
    places = (place_of(aux, 0), place_of(aux, 1))

    def occ_copy(quarter):
        return pltpu.make_async_copy(
            parts[quarter].at[pl.ds(2 * block, TAIL)],
            occ.at[pl.ds(quarter * TAIL, TAIL)],
            occ_sems.at[quarter],
        )

    def left_copy(b, group, begin, quarter):
        return pltpu.make_async_copy(
            parts[group * 4 + quarter].at[pl.ds(begin, block)],
            left.at[pl.ds(b * block, block), pl.ds(quarter * width, width)],
            left_sems.at[b, quarter],
        )

    def grid_copy(slot, group, quarter):
        return pltpu.make_async_copy(
            parts[group * 4 + quarter].at[pl.ds(0, 2 * block)],
            grid.at[pl.ds(slot * 2 * block, 2 * block), pl.ds(quarter * width, width)],
            grid_sems.at[slot, quarter],
        )

    def run(row_count, group_list):
        for quarter in quarters:
            occ_copy(quarter).start()
            for b in range(row_count):
                begin = pl.multiple_of((places[b] % 2) * block, block)
                for group in range(groups):

                    @pl.when(places[b] // 2 == group)
                    def _(b=b, group=group, begin=begin, quarter=quarter):
                        left_copy(b, group, begin, quarter).start()

            for slot, group in enumerate(group_list):
                grid_copy(slot, group, quarter).start()
        height = len(PAIRS) * row_count * block
        span = len(group_list) * 2 * block

        def scale(turn):
            quarter = quarters[turn]
            cols = pl.ds(quarter * width, width)
            orbit = [
                occ[quarter * TAIL + i : quarter * TAIL + i + 1, :].astype(jnp.float32)
                for i in range(3)
            ]
            for b in range(row_count):
                rows = left[pl.ds(b * block, block), cols].astype(jnp.float32)
                for p, (i, j) in enumerate(PAIRS):
                    scaled[turn % 2, pl.ds((p * row_count + b) * block, block), :] = (
                        rows * (orbit[i] * orbit[j])
                    ).astype(jnp.bfloat16)

        def wait_left(turn):
            quarter = quarters[turn]
            occ_copy(quarter).wait()
            for b in range(row_count):
                left_copy(b, 0, 0, quarter).wait()

        wait_left(0)
        scale(0)
        for turn, quarter in enumerate(quarters):
            cols = pl.ds(quarter * width, width)
            for slot, group in enumerate(group_list):
                grid_copy(slot, group, quarter).wait()
            if turn + 1 < len(quarters):
                wait_left(turn + 1)
                scale(turn + 1)
            for step in range(height // 768):
                rows = pl.ds(step * 768, 768)
                term = lax.dot_general(
                    scaled[turn % 2, rows, :],
                    grid[pl.ds(0, span), cols],
                    (((1,), (1,)), ((), ())),
                    preferred_element_type=jnp.float32,
                )
                if turn:
                    total[rows, pl.ds(0, span)] += term
                elif partial is not None:
                    total[rows, pl.ds(0, span)] = term + partial[rows, :]
                else:
                    total[rows, pl.ds(0, span)] = term
        if stage == 2:
            return None
        lane = lax.broadcasted_iota(jnp.int32, (block, block), 1)
        sub = lax.broadcasted_iota(jnp.int32, (block, block), 0)
        sums = []
        for b in range(row_count):
            own_row = energy[pl.ds(places[b], 1), :]
            own_energy = jnp.transpose(jnp.broadcast_to(own_row, (block, block)))
            own_live = sub < rows_ref[where[0], plan[3, places[b]]]
            for q in range(2 * len(group_list)):
                place = 2 * group_list[q // 2] + q % 2
                their_energy = energy[place : place + 1, :]
                live = own_live & (lane < rows_ref[where[0], plan[3, place]])
                for p, (i, j) in enumerate(PAIRS):
                    gap = (levels[0, i] + levels[0, j]) - own_energy - their_energy
                    rows = pl.ds((p * row_count + b) * block, block)
                    value = total[rows, pl.ds(q * block, block)]
                    amp = jnp.where(live, value * pl.reciprocal(gap), 0.0).astype(jnp.bfloat16)
                    amps[:, pl.ds(p * span + q * block, block)] = amp
                    if stage == 3:
                        early = amp if b == 0 else jnp.where(aux < 2, amp, jnp.zeros_like(amp))
                        tall[rows, pl.ds(q * block, block)] = early
                    elif stage == 1 and b == 0:
                        tall[pl.ds(p * block, block), pl.ds(q * block, block)] = amp
            wide = amps[:, pl.ds(0, len(PAIRS) * span)]
            sums.append(
                lax.dot_general(
                    wide, wide, (((1,), (1,)), ((), ())), preferred_element_type=jnp.float32
                )
            )
        return sums

    def late_sum(q):
        late = tall[:, pl.ds(q * block, block)]
        return lax.dot_general(
            late, late, (((0,), (0,)), ((), ())), preferred_element_type=jnp.float32
        )

    if stage == 0:
        out[0] = run(1, (0, 1))[0]
    elif stage == 1:

        @pl.when(aux < 2)
        def _():
            out[0], out[1] = run(2, (2,))

        @pl.when(aux >= 2)
        def _():
            out[0] = run(1, (2,))[0]
            out[1] = jnp.zeros(out.shape[1:], out.dtype)

        for q in range(2):
            out[2 + q] = late_sum(q)
    elif stage == 2:
        run(2, (3,))
    else:
        first, second = before
        sums = run(2, (3,))
        dens[0] = sums[0] + (first[0] + second[0])
        share = sums[1] + second[1]
        for q in range(4):
            late = second[2 + q] if q < 2 else late_sum(q - 2)
            dens[1 + q] = late + jnp.where(aux == q, share, 0.0)
        half = block // 2
        side = aux // 2
        stay[...] = dens[:, pl.ds(pl.multiple_of(side * half, half), half), :]
        away = dens[:, pl.ds(pl.multiple_of((1 - side) * half, half), half), :]
        sent[...] = away.astype(jnp.bfloat16)


def contract(stage, where, plan, levels, vir_rows, energy, parts, before=()):
    block, width = energy.shape[1], parts[0].shape[1]
    height = len(PAIRS) * 2 * block
    span = (4, 2, 2, 2)[stage] * block
    scratch = [
        pltpu.VMEM((2 * block, 4 * width), jnp.bfloat16),
        pltpu.VMEM((span, 4 * width), jnp.bfloat16),
        pltpu.VMEM((4 * TAIL, width), jnp.bfloat16),
        pltpu.VMEM((2, height, width), jnp.bfloat16),
    ]
    if stage != 2:
        scratch += [
            pltpu.VMEM((height, span), jnp.float32),
            pltpu.VMEM((block, len(PAIRS) * span), jnp.bfloat16),
        ]
    out_specs = VMEM
    if stage == 3:
        scratch += [
            pltpu.VMEM((height, span), jnp.bfloat16),
            pltpu.VMEM((5, block, block), jnp.float32),
        ]
        out_shape = tuple(
            jax.ShapeDtypeStruct((5, block // 2, block), dtype)
            for dtype in (jnp.bfloat16, jnp.float32)
        )
        out_specs = (VMEM, VMEM)
    elif stage == 2:
        out_shape = jax.ShapeDtypeStruct((height, span), jnp.float32)
    elif stage == 1:
        scratch += [pltpu.VMEM((height // 2, span), jnp.bfloat16)]
        out_shape = jax.ShapeDtypeStruct((4, block, block), jnp.float32)
    else:
        out_shape = jax.ShapeDtypeStruct((1, block, block), jnp.float32)
    scratch += [
        pltpu.SemaphoreType.DMA((2, 4)),
        pltpu.SemaphoreType.DMA((3, 4)),
        pltpu.SemaphoreType.DMA((4,)),
    ]
    cost = NO_COST
    if stage in (1, 2):
        units = (4, 4, 2)[stage] * len(PAIRS) * block * block
        cost = pl.CostEstimate(
            flops=2 * units * 4 * width, bytes_accessed=units * 4, transcendentals=0
        )
    return pl.pallas_call(
        functools.partial(contract_kernel, stage, block, width),
        out_shape=out_shape,
        in_specs=[SMEM] * 4 + [VMEM] + [ANY] * len(parts) + [VMEM] * len(before),
        out_specs=out_specs,
        scratch_shapes=scratch,
        compiler_params=pltpu.CompilerParams(vmem_limit_bytes=26 * MIB),
        cost_estimate=cost,
        name="contract",
    )(where, plan, levels, vir_rows, energy, *parts, *before)


def spread_kernel(own_count, where, plan, kept, came, out):
    aux = where[1]
    out[...] = jnp.zeros_like(out)

    def put(place, value):
        out[plan[2, place] // own_count, plan[1, place]] = value.astype(out.dtype)

    put(aux, kept[0])
    put(aux ^ 2, kept[1])
    put(aux ^ 1, came[0])
    put(aux ^ 3, came[1])
    for q in range(4):
        put(4 + q, kept[2 + q] + came[2 + q])


def spread(ints, plan, kept, came, frags, own_count):
    return pl.pallas_call(
        functools.partial(spread_kernel, own_count),
        out_shape=jax.ShapeDtypeStruct((frags, CAP) + kept.shape[1:], jnp.bfloat16),
        in_specs=[SMEM, SMEM, VMEM, VMEM],
        out_specs=VMEM,
        compiler_params=pltpu.CompilerParams(vmem_limit_bytes=4 * MIB),
        name="spread",
    )(ints, plan, kept, came)


def collect_kernel(target, came, out):
    out[...] = jnp.zeros_like(out)

    def one(fragment, carry):
        for r in range(CAP):
            out[target[fragment, r]] += came[fragment, r].astype(jnp.float32)
        return carry

    lax.fori_loop(0, came.shape[0], one, 0)


def collect(target, came, own_count):
    return pl.pallas_call(
        collect_kernel,
        out_shape=jax.ShapeDtypeStruct((own_count,) + came.shape[2:], jnp.float32),
        in_specs=[SMEM, VMEM],
        out_specs=VMEM,
        compiler_params=pltpu.CompilerParams(vmem_limit_bytes=4 * MIB),
        name="collect",
    )(target, came)


def body(vir_grid, vir_energy, occ_grid, occ_energy, vir_list, vir_rows, owner_map):
    frags = lax.axis_size("frag")
    aux_count = lax.axis_size("aux")
    me = lax.axis_index("frag").astype(jnp.int32)
    aux = lax.axis_index("aux").astype(jnp.int32)
    own_count, block, width = vir_grid.shape
    list_len = vir_list.shape[1]
    sizes = (frags, own_count, list_len)
    ints = jnp.concatenate([me[None], aux[None], owner_map])
    occ_count = occ_grid.shape[1]
    tails = jnp.concatenate([
        jnp.pad(occ_grid[0], ((0, TAIL - occ_count), (0, 0))),
        jnp.pad(vir_energy, ((0, TAIL - own_count), (0, width - block))),
    ])
    far_pairs = [(i, i ^ 2) for i in range(aux_count)]
    near_pairs = [(i, i ^ 1) for i in range(aux_count)]

    *outgoing, own = pack_to_send(ints, vir_list, tails, vir_grid, sizes)

    def over_aux(here, *others):
        far = lax.ppermute(here, "aux", far_pairs)
        near = lax.ppermute(here, "aux", near_pairs)
        onward = after(far, *others) if others else far
        return [here, far, near, lax.ppermute(onward, "aux", near_pairs)]

    def after(value, *others):
        return lax.optimization_barrier((value, *others))[0]

    def send(index, *others):
        distance, parity = ROUNDS[index]
        payload = after(outgoing[index], *others) if others else outgoing[index]
        return lax.ppermute(payload, "frag", round_pairs(distance, parity, frags))

    arrived = {code: send(code - 1) for code in (1, 2, 3, 4)}
    parts = over_aux(own)
    arrived[5] = send(4, *(arrived[c] for c in (1, 2, 3, 4)))
    plan, target = plan_lists(after(ints, arrived[3]), vir_list, sizes)
    here = pack_group(2, block, plan, {c: arrived[c] for c in range(1, 5)})[0]
    parts += over_aux(here)
    arrived[6] = send(5, parts[5])
    here, early_energy = pack_group(
        4, block, plan, {c: arrived[c] for c in range(1, 6)}, vir_energy
    )
    shared = (ints, plan, occ_energy, vir_rows)
    first = contract(0, *shared, early_energy, parts[:8])
    arrived[6] = after(arrived[6], first)
    last, energy = pack_group(6, block, plan, arrived, vir_energy)
    near = lax.ppermute(last, "aux", near_pairs)
    far = lax.ppermute(last, "aux", far_pairs)
    parts += over_aux(here, near)
    second = contract(1, *shared, early_energy, parts[:12])
    partial = contract(2, *shared, energy, parts + [last, last, near, near])
    far_near = lax.ppermute(after(far, second, partial), "aux", near_pairs)
    parts += [last, far, near, far_near]
    sent, stay = contract(3, *shared, energy, parts, (first, second, partial))

    quarter = block // aux_count
    core = aux % 2
    met = lax.ppermute(sent, "aux", far_pairs).astype(jnp.float32)
    both = jnp.concatenate([stay[:1], met[:1], stay[1:] + met[1:]], axis=0)
    sent = lax.dynamic_slice_in_dim(both, (1 - core) * quarter, quarter, 1)
    kept = lax.dynamic_slice_in_dim(both, core * quarter, quarter, 1)
    came = lax.ppermute(sent, "aux", near_pairs)
    outgoing = spread(ints, plan, kept, came, frags, own_count)
    incoming = lax.all_to_all(outgoing, "frag", 0, 0, tiled=True)
    return collect(target, incoming, own_count)


def solution(mesh):
    return jax.shard_map(
        body,
        mesh=mesh,
        in_specs=(
            P("frag", None, "aux"),
            P("frag", None),
            P("frag", None, "aux"),
            P("frag", None),
            P(),
            P(),
            P(),
        ),
        out_specs=P("frag", "aux", None),
        check_vma=False,
    )
```

```python
import functools

import jax
import jax.numpy as jnp
from jax import lax
from jax.experimental import pallas as pl
from jax.experimental.pallas import tpu as pltpu
from jax.sharding import PartitionSpec as P

ROUNDS = ((1, 0), (1, 1), (2, 0), (2, 1), (3, 0), (3, 1))
CAP = 2
TAIL = 16
PAIRS = tuple((i, j) for i in range(3) for j in range(i, 3))
MIB = 2**20
NO_COST = pl.CostEstimate(flops=0, bytes_accessed=0, transcendentals=0)
ANY = pl.BlockSpec(memory_space=pl.ANY)
SMEM = pl.BlockSpec(memory_space=pltpu.SMEM)
VMEM = pl.BlockSpec(memory_space=pltpu.VMEM)


def round_pairs(distance, parity, frags):
    up = [(i, i + distance) for i in range(frags - distance) if (i // distance) % 2 == parity]
    return up + [(b, a) for a, b in up]


class Lists:
    def __init__(self, ints, listed, frags, own_count, list_len):
        self.ints, self.listed = ints, listed
        self.frags, self.own_count, self.list_len = frags, own_count, list_len
        self.me = ints[0]

    def row(self, fragment, k):
        return self.ints[2 + self.listed[fragment, k]]

    def pick(self, fragment, owner):
        count = jnp.int32(0)
        picked = [jnp.int32(0)] * CAP
        for k in range(self.list_len):
            row = self.row(fragment, k)
            hit = row // self.own_count == owner
            for r in range(CAP):
                picked[r] = jnp.where(hit & (count == r), row % self.own_count, picked[r])
            count = count + hit.astype(jnp.int32)
        return picked, count


def send_kernel(sizes, ints, listed, tails, table, *refs):
    outs, own, sems = refs[:6], refs[6], refs[7]
    lists = Lists(ints, listed, *sizes)
    me, frags = lists.me, lists.frags
    block = table.shape[1]
    copies = []

    def start(out, index, fragment, inside):
        picked, count = lists.pick(fragment, me)
        for r in range(CAP):
            copy = pltpu.make_async_copy(
                table.at[picked[r]], out.at[pl.ds(r * block, block)], sems.at[index, r]
            )
            needed = inside & (count > r)
            pl.when(needed)(copy.start)
            copies.append((needed, copy))

    for index, (distance, parity) in enumerate(ROUNDS):
        up = (me // distance) % 2 == parity
        partner = jnp.where(up, me + distance, me - distance)
        inside = (partner >= 0) & (partner < frags)
        start(outs[index], index, jnp.clip(partner, 0, frags - 1), inside)
    start(own, 6, me, me >= 0)
    own[pl.ds(CAP * block, TAIL), :] = tails[pl.ds(0, TAIL), :]
    for out in outs:
        out[pl.ds(CAP * block, TAIL), :] = tails[pl.ds(TAIL, TAIL), :]
    for needed, copy in copies:
        pl.when(needed)(copy.wait)


def pack_to_send(ints, vir_list, tails, table, sizes):
    _, block_rows, cols = table.shape
    part = jax.ShapeDtypeStruct((CAP * block_rows + TAIL, cols), table.dtype)
    return pl.pallas_call(
        functools.partial(send_kernel, sizes),
        out_shape=(part,) * 7,
        in_specs=[SMEM, SMEM, VMEM, ANY],
        out_specs=(VMEM,) * 7,
        scratch_shapes=[pltpu.SemaphoreType.DMA((7, CAP))],
        compiler_params=pltpu.CompilerParams(vmem_limit_bytes=50 * MIB),
        cost_estimate=NO_COST,
        name="pack_to_send",
    )(ints, vir_list, tails, table)


def plan_kernel(sizes, ints, listed, plan, target):
    lists = Lists(ints, listed, *sizes)
    me, (frags, own_count, list_len) = lists.me, sizes
    rows, owners, codes, classes = [], [], [], []
    for k in range(list_len):
        row = lists.row(me, k)
        owner = row // own_count
        low = jnp.minimum(me, owner)
        far = jnp.abs(owner - me)
        code = jnp.int32(0)
        for index, (distance, parity) in enumerate(ROUNDS):
            code = jnp.where(
                (far == distance) & ((low // distance) % 2 == parity), index + 1, code
            )
        rows.append(row)
        owners.append(owner)
        codes.append(code)
        classes.append(jnp.where(code == 0, 0, jnp.maximum(code - 3, 1)))
    for k in range(list_len):
        place = jnp.int32(0)
        rank = jnp.int32(0)
        for j in range(list_len):
            if j < k:
                place += (classes[j] <= classes[k]).astype(jnp.int32)
                rank += (owners[j] == owners[k]).astype(jnp.int32)
            elif j > k:
                place += (classes[j] < classes[k]).astype(jnp.int32)
        plan[0, place] = codes[k]
        plan[1, place] = rank
        plan[2, place] = rows[k]
        plan[3, place] = jnp.int32(k)

    def one(fragment, carry):
        picked, _ = lists.pick(fragment, me)
        for r in range(CAP):
            target[fragment, r] = picked[r]
        return carry

    lax.fori_loop(0, frags, one, 0)


def plan_lists(ints, vir_list, sizes):
    frags, _, list_len = sizes
    return pl.pallas_call(
        functools.partial(plan_kernel, sizes),
        out_shape=(
            jax.ShapeDtypeStruct((4, list_len), jnp.int32),
            jax.ShapeDtypeStruct((frags, CAP), jnp.int32),
        ),
        in_specs=[SMEM, SMEM],
        out_specs=(SMEM, SMEM),
        compiler_params=pltpu.CompilerParams(vmem_limit_bytes=4 * MIB),
        cost_estimate=NO_COST,
        name="plan_lists",
    )(ints, vir_list)


def pack_kernel(first, codes, block, with_energy, plan, *refs):
    count = len(codes)
    if with_energy:
        own_energy, arrived, (out, levels, raw, wide, sems, tail_sems) = (
            refs[0],
            refs[1 : count + 1],
            refs[count + 1 :],
        )
    else:
        arrived, (out, sems) = refs[:count], refs[count:]
    for i in range(2):
        code = plan[0, first + i]
        begin = pl.multiple_of(plan[1, first + i] * block, block)
        rows = pl.ds(i * block, block)
        for source, ref in zip(codes, arrived):

            @pl.when(code == source)
            def _(ref=ref, begin=begin, rows=rows):
                pltpu.make_async_copy(
                    ref.at[pl.ds(begin, block)], out.at[rows], sems.at[i]
                ).start()

    if with_energy:
        own_count = own_energy.shape[0]
        copies = [
            pltpu.make_async_copy(
                ref.at[pl.ds(2 * block, TAIL), pl.ds(0, block)],
                raw.at[pl.ds(n * TAIL, TAIL)],
                tail_sems.at[n],
            )
            for n, ref in enumerate(arrived)
        ]
        for copy in copies:
            copy.start()
        wide[0:own_count, :] = own_energy[...].astype(jnp.float32)
        for copy in copies:
            copy.wait()
        wide[TAIL:, :] = raw[...].astype(jnp.float32)
        levels[...] = jnp.zeros_like(levels)
        for place in range(first + 2):
            row = plan[0, place] * TAIL + plan[2, place] % own_count
            levels[place : place + 1, :] = wide[pl.ds(row, 1), :]
    for i in range(2):
        rows = pl.ds(i * block, block)
        pltpu.make_async_copy(arrived[0].at[rows], out.at[rows], sems.at[i]).wait()


def pack_group(first, block, plan, arrived, own_energy=None):
    codes = tuple(arrived)
    refs = [arrived[c] for c in codes]
    cols, dtype = refs[0].shape[1], refs[0].dtype
    shapes = [jax.ShapeDtypeStruct((2 * block, cols), dtype)]
    scratch = [pltpu.SemaphoreType.DMA((2,))]
    extra = []
    if own_energy is not None:
        shapes.append(jax.ShapeDtypeStruct((plan.shape[1], block), jnp.float32))
        scratch = [
            pltpu.VMEM((len(codes) * TAIL, block), dtype),
            pltpu.VMEM(((len(codes) + 1) * TAIL, block), jnp.float32),
            *scratch,
            pltpu.SemaphoreType.DMA((len(codes),)),
        ]
        extra = [own_energy]
    return pl.pallas_call(
        functools.partial(pack_kernel, first, codes, block, own_energy is not None),
        out_shape=tuple(shapes),
        in_specs=[SMEM] + [VMEM] * len(extra) + [ANY] * len(refs),
        out_specs=(VMEM,) * len(shapes),
        scratch_shapes=scratch,
        compiler_params=pltpu.CompilerParams(vmem_limit_bytes=4 * MIB),
        cost_estimate=NO_COST,
        name="pack_group",
    )(plan, *extra, *refs)


def place_of(aux, b):
    return aux + 4 * b


def contract_kernel(stage, block, width, where, plan, levels, rows_ref, energy, *refs):
    groups = min(stage + 2, 4)
    parts, rest = refs[: groups * 4], refs[groups * 4 :]
    quarters = {2: (0, 2), 3: (1, 3)}.get(stage, (0, 1, 2, 3))
    partial = None
    if stage == 2:
        total, left, grid, occ, scaled, left_sems, grid_sems, occ_sems = rest
    elif stage == 3:
        before, partial, rest = rest[:2], rest[2], rest[3:]
        sent, stay, left, grid, occ, scaled, total, amps, tall, dens = rest[:10]
        left_sems, grid_sems, occ_sems = rest[10:]
    elif stage == 1:
        out, left, grid, occ, scaled, total, amps, tall, left_sems, grid_sems, occ_sems = rest
    else:
        out, left, grid, occ, scaled, total, amps, left_sems, grid_sems, occ_sems = rest
    aux = where[1]
    places = (place_of(aux, 0), place_of(aux, 1))

    def occ_copy(quarter):
        return pltpu.make_async_copy(
            parts[quarter].at[pl.ds(2 * block, TAIL)],
            occ.at[pl.ds(quarter * TAIL, TAIL)],
            occ_sems.at[quarter],
        )

    def left_copy(b, group, begin, quarter):
        return pltpu.make_async_copy(
            parts[group * 4 + quarter].at[pl.ds(begin, block)],
            left.at[pl.ds(b * block, block), pl.ds(quarter * width, width)],
            left_sems.at[b, quarter],
        )

    def grid_copy(slot, group, quarter):
        return pltpu.make_async_copy(
            parts[group * 4 + quarter].at[pl.ds(0, 2 * block)],
            grid.at[pl.ds(slot * 2 * block, 2 * block), pl.ds(quarter * width, width)],
            grid_sems.at[slot, quarter],
        )

    def run(row_count, group_list):
        for quarter in quarters:
            occ_copy(quarter).start()
            for b in range(row_count):
                begin = pl.multiple_of((places[b] % 2) * block, block)
                for group in range(groups):

                    @pl.when(places[b] // 2 == group)
                    def _(b=b, group=group, begin=begin, quarter=quarter):
                        left_copy(b, group, begin, quarter).start()

            for slot, group in enumerate(group_list):
                grid_copy(slot, group, quarter).start()
        height = len(PAIRS) * row_count * block
        span = len(group_list) * 2 * block

        def scale(turn):
            quarter = quarters[turn]
            cols = pl.ds(quarter * width, width)
            orbit = [
                occ[quarter * TAIL + i : quarter * TAIL + i + 1, :].astype(jnp.float32)
                for i in range(3)
            ]
            for b in range(row_count):
                rows = left[pl.ds(b * block, block), cols].astype(jnp.float32)
                for p, (i, j) in enumerate(PAIRS):
                    scaled[turn % 2, pl.ds((p * row_count + b) * block, block), :] = (
                        rows * (orbit[i] * orbit[j])
                    ).astype(jnp.bfloat16)

        def wait_left(turn):
            quarter = quarters[turn]
            occ_copy(quarter).wait()
            for b in range(row_count):
                left_copy(b, 0, 0, quarter).wait()

        wait_left(0)
        scale(0)
        for turn, quarter in enumerate(quarters):
            cols = pl.ds(quarter * width, width)
            for slot, group in enumerate(group_list):
                grid_copy(slot, group, quarter).wait()
            if turn + 1 < len(quarters):
                wait_left(turn + 1)
                scale(turn + 1)
            for step in range(height // 768):
                rows = pl.ds(step * 768, 768)
                term = lax.dot_general(
                    scaled[turn % 2, rows, :],
                    grid[pl.ds(0, span), cols],
                    (((1,), (1,)), ((), ())),
                    preferred_element_type=jnp.float32,
                )
                if turn:
                    total[rows, pl.ds(0, span)] += term
                elif partial is not None:
                    total[rows, pl.ds(0, span)] = term + partial[rows, :]
                else:
                    total[rows, pl.ds(0, span)] = term
        if stage == 2:
            return None
        lane = lax.broadcasted_iota(jnp.int32, (block, block), 1)
        sub = lax.broadcasted_iota(jnp.int32, (block, block), 0)
        sums = []
        for b in range(row_count):
            own_row = energy[pl.ds(places[b], 1), :]
            own_energy = jnp.transpose(jnp.broadcast_to(own_row, (block, block)))
            own_live = sub < rows_ref[where[0], plan[3, places[b]]]
            for q in range(2 * len(group_list)):
                place = 2 * group_list[q // 2] + q % 2
                their_energy = energy[place : place + 1, :]
                live = own_live & (lane < rows_ref[where[0], plan[3, place]])
                for p, (i, j) in enumerate(PAIRS):
                    gap = (levels[0, i] + levels[0, j]) - own_energy - their_energy
                    rows = pl.ds((p * row_count + b) * block, block)
                    value = total[rows, pl.ds(q * block, block)]
                    amp = jnp.where(live, value * pl.reciprocal(gap), 0.0).astype(jnp.bfloat16)
                    amps[:, pl.ds(p * span + q * block, block)] = amp
                    if stage == 3:
                        early = amp if b == 0 else jnp.where(aux < 2, amp, jnp.zeros_like(amp))
                        tall[rows, pl.ds(q * block, block)] = early
                    elif stage == 1 and b == 0:
                        tall[pl.ds(p * block, block), pl.ds(q * block, block)] = amp
            wide = amps[:, pl.ds(0, len(PAIRS) * span)]
            sums.append(
                lax.dot_general(
                    wide, wide, (((1,), (1,)), ((), ())), preferred_element_type=jnp.float32
                )
            )
        return sums

    def late_sum(q):
        late = tall[:, pl.ds(q * block, block)]
        return lax.dot_general(
            late, late, (((0,), (0,)), ((), ())), preferred_element_type=jnp.float32
        )

    if stage == 0:
        out[0] = run(1, (0, 1))[0]
    elif stage == 1:

        @pl.when(aux < 2)
        def _():
            out[0], out[1] = run(2, (2,))

        @pl.when(aux >= 2)
        def _():
            out[0] = run(1, (2,))[0]
            out[1] = jnp.zeros(out.shape[1:], out.dtype)

        for q in range(2):
            out[2 + q] = late_sum(q)
    elif stage == 2:
        run(2, (3,))
    else:
        first, second = before
        sums = run(2, (3,))
        dens[0] = sums[0] + (first[0] + second[0])
        share = sums[1] + second[1]
        for q in range(4):
            late = second[2 + q] if q < 2 else late_sum(q - 2)
            dens[1 + q] = late + jnp.where(aux == q, share, 0.0)
        half = block // 2
        side = aux // 2
        stay[...] = dens[:, pl.ds(pl.multiple_of(side * half, half), half), :]
        away = dens[:, pl.ds(pl.multiple_of((1 - side) * half, half), half), :]
        sent[...] = away.astype(jnp.bfloat16)


def contract(stage, where, plan, levels, vir_rows, energy, parts, before=()):
    block, width = energy.shape[1], parts[0].shape[1]
    height = len(PAIRS) * 2 * block
    span = (4, 2, 2, 2)[stage] * block
    scratch = [
        pltpu.VMEM((2 * block, 4 * width), jnp.bfloat16),
        pltpu.VMEM((span, 4 * width), jnp.bfloat16),
        pltpu.VMEM((4 * TAIL, width), jnp.bfloat16),
        pltpu.VMEM((2, height, width), jnp.bfloat16),
    ]
    if stage != 2:
        scratch += [
            pltpu.VMEM((height, span), jnp.float32),
            pltpu.VMEM((block, len(PAIRS) * span), jnp.bfloat16),
        ]
    out_specs = VMEM
    if stage == 3:
        scratch += [
            pltpu.VMEM((height, span), jnp.bfloat16),
            pltpu.VMEM((5, block, block), jnp.float32),
        ]
        out_shape = tuple(
            jax.ShapeDtypeStruct((5, block // 2, block), dtype)
            for dtype in (jnp.bfloat16, jnp.float32)
        )
        out_specs = (VMEM, VMEM)
    elif stage == 2:
        out_shape = jax.ShapeDtypeStruct((height, span), jnp.float32)
    elif stage == 1:
        scratch += [pltpu.VMEM((height // 2, span), jnp.bfloat16)]
        out_shape = jax.ShapeDtypeStruct((4, block, block), jnp.float32)
    else:
        out_shape = jax.ShapeDtypeStruct((1, block, block), jnp.float32)
    scratch += [
        pltpu.SemaphoreType.DMA((2, 4)),
        pltpu.SemaphoreType.DMA((3, 4)),
        pltpu.SemaphoreType.DMA((4,)),
    ]
    cost = NO_COST
    if stage in (1, 2):
        units = (4, 4, 2)[stage] * len(PAIRS) * block * block
        cost = pl.CostEstimate(
            flops=2 * units * 4 * width, bytes_accessed=units * 4, transcendentals=0
        )
    return pl.pallas_call(
        functools.partial(contract_kernel, stage, block, width),
        out_shape=out_shape,
        in_specs=[SMEM] * 4 + [VMEM] + [ANY] * len(parts) + [VMEM] * len(before),
        out_specs=out_specs,
        scratch_shapes=scratch,
        compiler_params=pltpu.CompilerParams(vmem_limit_bytes=26 * MIB),
        cost_estimate=cost,
        name="contract",
    )(where, plan, levels, vir_rows, energy, *parts, *before)


def spread_kernel(own_count, where, plan, kept, came, out):
    aux = where[1]
    out[...] = jnp.zeros_like(out)

    def put(place, value):
        out[plan[2, place] // own_count, plan[1, place]] = value.astype(out.dtype)

    put(aux, kept[0])
    put(aux ^ 2, kept[1])
    put(aux ^ 1, came[0])
    put(aux ^ 3, came[1])
    for q in range(4):
        put(4 + q, kept[2 + q] + came[2 + q])


def spread(ints, plan, kept, came, frags, own_count):
    return pl.pallas_call(
        functools.partial(spread_kernel, own_count),
        out_shape=jax.ShapeDtypeStruct((frags, CAP) + kept.shape[1:], jnp.bfloat16),
        in_specs=[SMEM, SMEM, VMEM, VMEM],
        out_specs=VMEM,
        compiler_params=pltpu.CompilerParams(vmem_limit_bytes=4 * MIB),
        name="spread",
    )(ints, plan, kept, came)


def collect_kernel(target, came, out):
    out[...] = jnp.zeros_like(out)

    def one(fragment, carry):
        for r in range(CAP):
            out[target[fragment, r]] += came[fragment, r].astype(jnp.float32)
        return carry

    lax.fori_loop(0, came.shape[0], one, 0)


def collect(target, came, own_count):
    return pl.pallas_call(
        collect_kernel,
        out_shape=jax.ShapeDtypeStruct((own_count,) + came.shape[2:], jnp.float32),
        in_specs=[SMEM, VMEM],
        out_specs=VMEM,
        compiler_params=pltpu.CompilerParams(vmem_limit_bytes=4 * MIB),
        name="collect",
    )(target, came)


def body(vir_grid, vir_energy, occ_grid, occ_energy, vir_list, vir_rows, owner_map):
    frags = lax.axis_size("frag")
    aux_count = lax.axis_size("aux")
    me = lax.axis_index("frag").astype(jnp.int32)
    aux = lax.axis_index("aux").astype(jnp.int32)
    own_count, block, width = vir_grid.shape
    list_len = vir_list.shape[1]
    sizes = (frags, own_count, list_len)
    ints = jnp.concatenate([me[None], aux[None], owner_map])
    occ_count = occ_grid.shape[1]
    tails = jnp.concatenate([
        jnp.pad(occ_grid[0], ((0, TAIL - occ_count), (0, 0))),
        jnp.pad(vir_energy, ((0, TAIL - own_count), (0, width - block))),
    ])
    far_pairs = [(i, i ^ 2) for i in range(aux_count)]
    near_pairs = [(i, i ^ 1) for i in range(aux_count)]

    *outgoing, own = pack_to_send(ints, vir_list, tails, vir_grid, sizes)

    def over_aux(here, *others):
        far = lax.ppermute(here, "aux", far_pairs)
        near = lax.ppermute(here, "aux", near_pairs)
        onward = after(far, *others) if others else far
        return [here, far, near, lax.ppermute(onward, "aux", near_pairs)]

    def after(value, *others):
        return lax.optimization_barrier((value, *others))[0]

    def send(index, *others):
        distance, parity = ROUNDS[index]
        payload = after(outgoing[index], *others) if others else outgoing[index]
        return lax.ppermute(payload, "frag", round_pairs(distance, parity, frags))

    arrived = {code: send(code - 1) for code in (1, 2, 3, 4)}
    parts = over_aux(own)
    arrived[5] = send(4, *(arrived[c] for c in (1, 2, 3, 4)))
    plan, target = plan_lists(after(ints, arrived[3]), vir_list, sizes)
    here = pack_group(2, block, plan, {c: arrived[c] for c in range(1, 5)})[0]
    parts += over_aux(here)
    arrived[6] = send(5, parts[5])
    here, early_energy = pack_group(
        4, block, plan, {c: arrived[c] for c in range(1, 6)}, vir_energy
    )
    shared = (ints, plan, occ_energy, vir_rows)
    first = contract(0, *shared, early_energy, parts[:8])
    arrived[6] = after(arrived[6], first)
    last, energy = pack_group(6, block, plan, arrived, vir_energy)
    near = lax.ppermute(last, "aux", near_pairs)
    far = lax.ppermute(last, "aux", far_pairs)
    parts += over_aux(here, near)
    second = contract(1, *shared, early_energy, parts[:12])
    partial = contract(2, *shared, energy, parts + [last, last, near, near])
    far_near = lax.ppermute(after(far, second, partial), "aux", near_pairs)
    parts += [last, far, near, far_near]
    sent, stay = contract(3, *shared, energy, parts, (first, second, partial))

    quarter = block // aux_count
    core = aux % 2
    met = lax.ppermute(sent, "aux", far_pairs).astype(jnp.float32)
    both = jnp.concatenate([stay[:1], met[:1], stay[1:] + met[1:]], axis=0)
    sent = lax.dynamic_slice_in_dim(both, (1 - core) * quarter, quarter, 1)
    kept = lax.dynamic_slice_in_dim(both, core * quarter, quarter, 1)
    came = lax.ppermute(sent, "aux", near_pairs)
    outgoing = spread(ints, plan, kept, came, frags, own_count)
    incoming = lax.all_to_all(outgoing, "frag", 0, 0, tiled=True)
    return collect(target, incoming, own_count)


def solution(mesh):
    return jax.shard_map(
        body,
        mesh=mesh,
        in_specs=(
            P("frag", None, "aux"),
            P("frag", None),
            P("frag", None, "aux"),
            P("frag", None),
            P(),
            P(),
            P(),
        ),
        out_specs=P("frag", "aux", None),
        check_vma=False,
    )
```

```python
import functools

import jax
import jax.numpy as jnp
from jax import lax
from jax.experimental import pallas as pl
from jax.experimental.pallas import tpu as pltpu
from jax.sharding import PartitionSpec as P

ROUNDS = ((1, 0), (1, 1), (2, 0), (2, 1), (3, 0), (3, 1))
CAP = 2
TAIL = 16
PAIRS = tuple((i, j) for i in range(3) for j in range(i, 3))
MIB = 2**20
NO_COST = pl.CostEstimate(flops=0, bytes_accessed=0, transcendentals=0)
ANY = pl.BlockSpec(memory_space=pl.ANY)
SMEM = pl.BlockSpec(memory_space=pltpu.SMEM)
VMEM = pl.BlockSpec(memory_space=pltpu.VMEM)


def round_pairs(distance, parity, frags):
    up = [(i, i + distance) for i in range(frags - distance) if (i // distance) % 2 == parity]
    return up + [(b, a) for a, b in up]


class Lists:
    def __init__(self, ints, listed, frags, own_count, list_len):
        self.ints, self.listed = ints, listed
        self.frags, self.own_count, self.list_len = frags, own_count, list_len
        self.me = ints[0]

    def row(self, fragment, k):
        return self.ints[2 + self.listed[fragment, k]]

    def pick(self, fragment, owner):
        count = jnp.int32(0)
        picked = [jnp.int32(0)] * CAP
        for k in range(self.list_len):
            row = self.row(fragment, k)
            hit = row // self.own_count == owner
            for r in range(CAP):
                picked[r] = jnp.where(hit & (count == r), row % self.own_count, picked[r])
            count = count + hit.astype(jnp.int32)
        return picked, count


def send_kernel(sizes, ints, listed, tails, table, *refs):
    outs, own, sems = refs[:6], refs[6], refs[7]
    lists = Lists(ints, listed, *sizes)
    me, frags = lists.me, lists.frags
    block = table.shape[1]
    copies = []

    def start(out, index, fragment, inside):
        picked, count = lists.pick(fragment, me)
        for r in range(CAP):
            copy = pltpu.make_async_copy(
                table.at[picked[r]], out.at[pl.ds(r * block, block)], sems.at[index, r]
            )
            needed = inside & (count > r)
            pl.when(needed)(copy.start)
            copies.append((needed, copy))

    for index, (distance, parity) in enumerate(ROUNDS):
        up = (me // distance) % 2 == parity
        partner = jnp.where(up, me + distance, me - distance)
        inside = (partner >= 0) & (partner < frags)
        start(outs[index], index, jnp.clip(partner, 0, frags - 1), inside)
    start(own, 6, me, me >= 0)
    own[pl.ds(CAP * block, TAIL), :] = tails[pl.ds(0, TAIL), :]
    for out in outs:
        out[pl.ds(CAP * block, TAIL), :] = tails[pl.ds(TAIL, TAIL), :]
    for needed, copy in copies:
        pl.when(needed)(copy.wait)


def pack_to_send(ints, vir_list, tails, table, sizes):
    _, block_rows, cols = table.shape
    part = jax.ShapeDtypeStruct((CAP * block_rows + TAIL, cols), table.dtype)
    return pl.pallas_call(
        functools.partial(send_kernel, sizes),
        out_shape=(part,) * 7,
        in_specs=[SMEM, SMEM, VMEM, ANY],
        out_specs=(VMEM,) * 7,
        scratch_shapes=[pltpu.SemaphoreType.DMA((7, CAP))],
        compiler_params=pltpu.CompilerParams(vmem_limit_bytes=50 * MIB),
        cost_estimate=NO_COST,
        name="pack_to_send",
    )(ints, vir_list, tails, table)


def plan_kernel(sizes, ints, listed, plan, target):
    lists = Lists(ints, listed, *sizes)
    me, (frags, own_count, list_len) = lists.me, sizes
    rows, owners, codes, classes = [], [], [], []
    for k in range(list_len):
        row = lists.row(me, k)
        owner = row // own_count
        low = jnp.minimum(me, owner)
        far = jnp.abs(owner - me)
        code = jnp.int32(0)
        for index, (distance, parity) in enumerate(ROUNDS):
            code = jnp.where(
                (far == distance) & ((low // distance) % 2 == parity), index + 1, code
            )
        rows.append(row)
        owners.append(owner)
        codes.append(code)
        classes.append(jnp.where(code == 0, 0, jnp.maximum(code - 3, 1)))
    for k in range(list_len):
        place = jnp.int32(0)
        rank = jnp.int32(0)
        for j in range(list_len):
            if j < k:
                place += (classes[j] <= classes[k]).astype(jnp.int32)
                rank += (owners[j] == owners[k]).astype(jnp.int32)
            elif j > k:
                place += (classes[j] < classes[k]).astype(jnp.int32)
        plan[0, place] = codes[k]
        plan[1, place] = rank
        plan[2, place] = rows[k]
        plan[3, place] = jnp.int32(k)

    def one(fragment, carry):
        picked, _ = lists.pick(fragment, me)
        for r in range(CAP):
            target[fragment, r] = picked[r]
        return carry

    lax.fori_loop(0, frags, one, 0)


def plan_lists(ints, vir_list, sizes):
    frags, _, list_len = sizes
    return pl.pallas_call(
        functools.partial(plan_kernel, sizes),
        out_shape=(
            jax.ShapeDtypeStruct((4, list_len), jnp.int32),
            jax.ShapeDtypeStruct((frags, CAP), jnp.int32),
        ),
        in_specs=[SMEM, SMEM],
        out_specs=(SMEM, SMEM),
        compiler_params=pltpu.CompilerParams(vmem_limit_bytes=4 * MIB),
        cost_estimate=NO_COST,
        name="plan_lists",
    )(ints, vir_list)


def pack_kernel(first, codes, block, with_energy, plan, *refs):
    count = len(codes)
    if with_energy:
        own_energy, arrived, (out, levels, raw, wide, sems, tail_sems) = (
            refs[0],
            refs[1 : count + 1],
            refs[count + 1 :],
        )
    else:
        arrived, (out, sems) = refs[:count], refs[count:]
    for i in range(2):
        code = plan[0, first + i]
        begin = pl.multiple_of(plan[1, first + i] * block, block)
        rows = pl.ds(i * block, block)
        for source, ref in zip(codes, arrived):

            @pl.when(code == source)
            def _(ref=ref, begin=begin, rows=rows):
                pltpu.make_async_copy(
                    ref.at[pl.ds(begin, block)], out.at[rows], sems.at[i]
                ).start()

    if with_energy:
        own_count = own_energy.shape[0]
        copies = [
            pltpu.make_async_copy(
                ref.at[pl.ds(2 * block, TAIL), pl.ds(0, block)],
                raw.at[pl.ds(n * TAIL, TAIL)],
                tail_sems.at[n],
            )
            for n, ref in enumerate(arrived)
        ]
        for copy in copies:
            copy.start()
        wide[0:own_count, :] = own_energy[...].astype(jnp.float32)
        for copy in copies:
            copy.wait()
        wide[TAIL:, :] = raw[...].astype(jnp.float32)
        levels[...] = jnp.zeros_like(levels)
        for place in range(first + 2):
            row = plan[0, place] * TAIL + plan[2, place] % own_count
            levels[place : place + 1, :] = wide[pl.ds(row, 1), :]
    for i in range(2):
        rows = pl.ds(i * block, block)
        pltpu.make_async_copy(arrived[0].at[rows], out.at[rows], sems.at[i]).wait()


def pack_group(first, block, plan, arrived, own_energy=None):
    codes = tuple(arrived)
    refs = [arrived[c] for c in codes]
    cols, dtype = refs[0].shape[1], refs[0].dtype
    shapes = [jax.ShapeDtypeStruct((2 * block, cols), dtype)]
    scratch = [pltpu.SemaphoreType.DMA((2,))]
    extra = []
    if own_energy is not None:
        shapes.append(jax.ShapeDtypeStruct((plan.shape[1], block), jnp.float32))
        scratch = [
            pltpu.VMEM((len(codes) * TAIL, block), dtype),
            pltpu.VMEM(((len(codes) + 1) * TAIL, block), jnp.float32),
            *scratch,
            pltpu.SemaphoreType.DMA((len(codes),)),
        ]
        extra = [own_energy]
    return pl.pallas_call(
        functools.partial(pack_kernel, first, codes, block, own_energy is not None),
        out_shape=tuple(shapes),
        in_specs=[SMEM] + [VMEM] * len(extra) + [ANY] * len(refs),
        out_specs=(VMEM,) * len(shapes),
        scratch_shapes=scratch,
        compiler_params=pltpu.CompilerParams(vmem_limit_bytes=4 * MIB),
        cost_estimate=NO_COST,
        name="pack_group",
    )(plan, *extra, *refs)


def place_of(aux, b):
    return aux + 4 * b


def contract_kernel(stage, block, width, where, plan, levels, rows_ref, energy, *refs):
    groups = min(stage + 2, 4)
    parts, rest = refs[: groups * 4], refs[groups * 4 :]
    quarters = {2: (0, 2), 3: (1, 3)}.get(stage, (0, 1, 2, 3))
    partial = None
    if stage == 2:
        total, left, grid, occ, scaled, left_sems, grid_sems, occ_sems = rest
    elif stage == 3:
        before, partial, rest = rest[:2], rest[2], rest[3:]
        sent, stay, left, grid, occ, scaled, total, amps, tall, dens = rest[:10]
        left_sems, grid_sems, occ_sems = rest[10:]
    elif stage == 1:
        out, left, grid, occ, scaled, total, amps, tall, left_sems, grid_sems, occ_sems = rest
    else:
        out, left, grid, occ, scaled, total, amps, left_sems, grid_sems, occ_sems = rest
    aux = where[1]
    places = (place_of(aux, 0), place_of(aux, 1))

    def occ_copy(quarter):
        return pltpu.make_async_copy(
            parts[quarter].at[pl.ds(2 * block, TAIL)],
            occ.at[pl.ds(quarter * TAIL, TAIL)],
            occ_sems.at[quarter],
        )

    def left_copy(b, group, begin, quarter):
        return pltpu.make_async_copy(
            parts[group * 4 + quarter].at[pl.ds(begin, block)],
            left.at[pl.ds(b * block, block), pl.ds(quarter * width, width)],
            left_sems.at[b, quarter],
        )

    def grid_copy(slot, group, quarter):
        return pltpu.make_async_copy(
            parts[group * 4 + quarter].at[pl.ds(0, 2 * block)],
            grid.at[pl.ds(slot * 2 * block, 2 * block), pl.ds(quarter * width, width)],
            grid_sems.at[slot, quarter],
        )

    def run(row_count, group_list):
        for quarter in quarters:
            occ_copy(quarter).start()
            for b in range(row_count):
                begin = pl.multiple_of((places[b] % 2) * block, block)
                for group in range(groups):

                    @pl.when(places[b] // 2 == group)
                    def _(b=b, group=group, begin=begin, quarter=quarter):
                        left_copy(b, group, begin, quarter).start()

            for slot, group in enumerate(group_list):
                grid_copy(slot, group, quarter).start()
        height = len(PAIRS) * row_count * block
        span = len(group_list) * 2 * block

        def scale(turn):
            quarter = quarters[turn]
            cols = pl.ds(quarter * width, width)
            orbit = [
                occ[quarter * TAIL + i : quarter * TAIL + i + 1, :].astype(jnp.float32)
                for i in range(3)
            ]
            for b in range(row_count):
                rows = left[pl.ds(b * block, block), cols].astype(jnp.float32)
                for p, (i, j) in enumerate(PAIRS):
                    scaled[turn % 2, pl.ds((p * row_count + b) * block, block), :] = (
                        rows * (orbit[i] * orbit[j])
                    ).astype(jnp.bfloat16)

        def wait_left(turn):
            quarter = quarters[turn]
            occ_copy(quarter).wait()
            for b in range(row_count):
                left_copy(b, 0, 0, quarter).wait()

        wait_left(0)
        scale(0)
        for turn, quarter in enumerate(quarters):
            cols = pl.ds(quarter * width, width)
            for slot, group in enumerate(group_list):
                grid_copy(slot, group, quarter).wait()
            if turn + 1 < len(quarters):
                wait_left(turn + 1)
                scale(turn + 1)
            for step in range(height // 768):
                rows = pl.ds(step * 768, 768)
                term = lax.dot_general(
                    scaled[turn % 2, rows, :],
                    grid[pl.ds(0, span), cols],
                    (((1,), (1,)), ((), ())),
                    preferred_element_type=jnp.float32,
                )
                if turn:
                    total[rows, pl.ds(0, span)] += term
                elif partial is not None:
                    total[rows, pl.ds(0, span)] = term + partial[rows, :]
                else:
                    total[rows, pl.ds(0, span)] = term
        if stage == 2:
            return None
        lane = lax.broadcasted_iota(jnp.int32, (block, block), 1)
        sub = lax.broadcasted_iota(jnp.int32, (block, block), 0)
        sums = []
        for b in range(row_count):
            own_row = energy[pl.ds(places[b], 1), :]
            own_energy = jnp.transpose(jnp.broadcast_to(own_row, (block, block)))
            own_live = sub < rows_ref[where[0], plan[3, places[b]]]
            for q in range(2 * len(group_list)):
                place = 2 * group_list[q // 2] + q % 2
                their_energy = energy[place : place + 1, :]
                live = own_live & (lane < rows_ref[where[0], plan[3, place]])
                for p, (i, j) in enumerate(PAIRS):
                    gap = (levels[0, i] + levels[0, j]) - own_energy - their_energy
                    rows = pl.ds((p * row_count + b) * block, block)
                    value = total[rows, pl.ds(q * block, block)]
                    amp = jnp.where(live, value * pl.reciprocal(gap), 0.0).astype(jnp.bfloat16)
                    amps[:, pl.ds(p * span + q * block, block)] = amp
                    if stage == 3:
                        early = amp if b == 0 else jnp.where(aux < 2, amp, jnp.zeros_like(amp))
                        tall[rows, pl.ds(q * block, block)] = early
                    elif stage == 1 and b == 0:
                        tall[pl.ds(p * block, block), pl.ds(q * block, block)] = amp
            wide = amps[:, pl.ds(0, len(PAIRS) * span)]
            sums.append(
                lax.dot_general(
                    wide, wide, (((1,), (1,)), ((), ())), preferred_element_type=jnp.float32
                )
            )
        return sums

    def late_sum(q):
        late = tall[:, pl.ds(q * block, block)]
        return lax.dot_general(
            late, late, (((0,), (0,)), ((), ())), preferred_element_type=jnp.float32
        )

    if stage == 0:
        out[0] = run(1, (0, 1))[0]
    elif stage == 1:

        @pl.when(aux < 2)
        def _():
            out[0], out[1] = run(2, (2,))

        @pl.when(aux >= 2)
        def _():
            out[0] = run(1, (2,))[0]
            out[1] = jnp.zeros(out.shape[1:], out.dtype)

        for q in range(2):
            out[2 + q] = late_sum(q)
    elif stage == 2:
        run(2, (3,))
    else:
        first, second = before
        sums = run(2, (3,))
        dens[0] = sums[0] + (first[0] + second[0])
        share = sums[1] + second[1]
        for q in range(4):
            late = second[2 + q] if q < 2 else late_sum(q - 2)
            dens[1 + q] = late + jnp.where(aux == q, share, 0.0)
        half = block // 2
        side = aux // 2
        stay[...] = dens[:, pl.ds(pl.multiple_of(side * half, half), half), :]
        away = dens[:, pl.ds(pl.multiple_of((1 - side) * half, half), half), :]
        sent[...] = away.astype(jnp.bfloat16)


def contract(stage, where, plan, levels, vir_rows, energy, parts, before=()):
    block, width = energy.shape[1], parts[0].shape[1]
    height = len(PAIRS) * 2 * block
    span = (4, 2, 2, 2)[stage] * block
    scratch = [
        pltpu.VMEM((2 * block, 4 * width), jnp.bfloat16),
        pltpu.VMEM((span, 4 * width), jnp.bfloat16),
        pltpu.VMEM((4 * TAIL, width), jnp.bfloat16),
        pltpu.VMEM((2, height, width), jnp.bfloat16),
    ]
    if stage != 2:
        scratch += [
            pltpu.VMEM((height, span), jnp.float32),
            pltpu.VMEM((block, len(PAIRS) * span), jnp.bfloat16),
        ]
    out_specs = VMEM
    if stage == 3:
        scratch += [
            pltpu.VMEM((height, span), jnp.bfloat16),
            pltpu.VMEM((5, block, block), jnp.float32),
        ]
        out_shape = tuple(
            jax.ShapeDtypeStruct((5, block // 2, block), dtype)
            for dtype in (jnp.bfloat16, jnp.float32)
        )
        out_specs = (VMEM, VMEM)
    elif stage == 2:
        out_shape = jax.ShapeDtypeStruct((height, span), jnp.float32)
    elif stage == 1:
        scratch += [pltpu.VMEM((height // 2, span), jnp.bfloat16)]
        out_shape = jax.ShapeDtypeStruct((4, block, block), jnp.float32)
    else:
        out_shape = jax.ShapeDtypeStruct((1, block, block), jnp.float32)
    scratch += [
        pltpu.SemaphoreType.DMA((2, 4)),
        pltpu.SemaphoreType.DMA((3, 4)),
        pltpu.SemaphoreType.DMA((4,)),
    ]
    cost = NO_COST
    if stage in (1, 2):
        units = (4, 4, 2)[stage] * len(PAIRS) * block * block
        cost = pl.CostEstimate(
            flops=2 * units * 4 * width, bytes_accessed=units * 4, transcendentals=0
        )
    return pl.pallas_call(
        functools.partial(contract_kernel, stage, block, width),
        out_shape=out_shape,
        in_specs=[SMEM] * 4 + [VMEM] + [ANY] * len(parts) + [VMEM] * len(before),
        out_specs=out_specs,
        scratch_shapes=scratch,
        compiler_params=pltpu.CompilerParams(vmem_limit_bytes=26 * MIB),
        cost_estimate=cost,
        name="contract",
    )(where, plan, levels, vir_rows, energy, *parts, *before)


def spread_kernel(own_count, where, plan, kept, came, out):
    aux = where[1]
    out[...] = jnp.zeros_like(out)

    def put(place, value):
        out[plan[2, place] // own_count, plan[1, place]] = value.astype(out.dtype)

    put(aux, kept[0])
    put(aux ^ 2, kept[1])
    put(aux ^ 1, came[0])
    put(aux ^ 3, came[1])
    for q in range(4):
        put(4 + q, kept[2 + q] + came[2 + q])


def spread(ints, plan, kept, came, frags, own_count):
    return pl.pallas_call(
        functools.partial(spread_kernel, own_count),
        out_shape=jax.ShapeDtypeStruct((frags, CAP) + kept.shape[1:], jnp.bfloat16),
        in_specs=[SMEM, SMEM, VMEM, VMEM],
        out_specs=VMEM,
        compiler_params=pltpu.CompilerParams(vmem_limit_bytes=4 * MIB),
        name="spread",
    )(ints, plan, kept, came)


def collect_kernel(target, came, out):
    out[...] = jnp.zeros_like(out)

    def one(fragment, carry):
        for r in range(CAP):
            out[target[fragment, r]] += came[fragment, r].astype(jnp.float32)
        return carry

    lax.fori_loop(0, came.shape[0], one, 0, unroll=8)


def collect(target, came, own_count):
    return pl.pallas_call(
        collect_kernel,
        out_shape=jax.ShapeDtypeStruct((own_count,) + came.shape[2:], jnp.float32),
        in_specs=[SMEM, VMEM],
        out_specs=VMEM,
        compiler_params=pltpu.CompilerParams(vmem_limit_bytes=4 * MIB),
        name="collect",
    )(target, came)


def body(vir_grid, vir_energy, occ_grid, occ_energy, vir_list, vir_rows, owner_map):
    frags = lax.axis_size("frag")
    aux_count = lax.axis_size("aux")
    me = lax.axis_index("frag").astype(jnp.int32)
    aux = lax.axis_index("aux").astype(jnp.int32)
    own_count, block, width = vir_grid.shape
    list_len = vir_list.shape[1]
    sizes = (frags, own_count, list_len)
    ints = jnp.concatenate([me[None], aux[None], owner_map])
    occ_count = occ_grid.shape[1]
    tails = jnp.concatenate([
        jnp.pad(occ_grid[0], ((0, TAIL - occ_count), (0, 0))),
        jnp.pad(vir_energy, ((0, TAIL - own_count), (0, width - block))),
    ])
    far_pairs = [(i, i ^ 2) for i in range(aux_count)]
    near_pairs = [(i, i ^ 1) for i in range(aux_count)]

    *outgoing, own = pack_to_send(ints, vir_list, tails, vir_grid, sizes)

    def over_aux(here, *others):
        far = lax.ppermute(here, "aux", far_pairs)
        near = lax.ppermute(here, "aux", near_pairs)
        onward = after(far, *others) if others else far
        return [here, far, near, lax.ppermute(onward, "aux", near_pairs)]

    def after(value, *others):
        return lax.optimization_barrier((value, *others))[0]

    def send(index, *others):
        distance, parity = ROUNDS[index]
        payload = after(outgoing[index], *others) if others else outgoing[index]
        return lax.ppermute(payload, "frag", round_pairs(distance, parity, frags))

    arrived = {code: send(code - 1) for code in (1, 2, 3, 4)}
    parts = over_aux(own)
    arrived[5] = send(4, *(arrived[c] for c in (1, 2, 3, 4)))
    plan, target = plan_lists(after(ints, arrived[3]), vir_list, sizes)
    here = pack_group(2, block, plan, {c: arrived[c] for c in range(1, 5)})[0]
    parts += over_aux(here)
    arrived[6] = send(5, parts[5])
    here, early_energy = pack_group(
        4, block, plan, {c: arrived[c] for c in range(1, 6)}, vir_energy
    )
    shared = (ints, plan, occ_energy, vir_rows)
    first = contract(0, *shared, early_energy, parts[:8])
    arrived[6] = after(arrived[6], first)
    last, energy = pack_group(6, block, plan, arrived, vir_energy)
    near = lax.ppermute(last, "aux", near_pairs)
    far = lax.ppermute(last, "aux", far_pairs)
    parts += over_aux(here, near)
    second = contract(1, *shared, early_energy, parts[:12])
    partial = contract(2, *shared, energy, parts + [last, last, near, near])
    far_near = lax.ppermute(after(far, second, partial), "aux", near_pairs)
    parts += [last, far, near, far_near]
    sent, stay = contract(3, *shared, energy, parts, (first, second, partial))

    quarter = block // aux_count
    core = aux % 2
    met = lax.ppermute(sent, "aux", far_pairs).astype(jnp.float32)
    both = jnp.concatenate([stay[:1], met[:1], stay[1:] + met[1:]], axis=0)
    sent = lax.dynamic_slice_in_dim(both, (1 - core) * quarter, quarter, 1)
    kept = lax.dynamic_slice_in_dim(both, core * quarter, quarter, 1)
    came = lax.ppermute(sent, "aux", near_pairs)
    outgoing = spread(ints, plan, kept, came, frags, own_count)
    incoming = lax.all_to_all(outgoing, "frag", 0, 0, tiled=True)
    return collect(target, incoming, own_count)


def solution(mesh):
    return jax.shard_map(
        body,
        mesh=mesh,
        in_specs=(
            P("frag", None, "aux"),
            P("frag", None),
            P("frag", None, "aux"),
            P("frag", None),
            P(),
            P(),
            P(),
        ),
        out_specs=P("frag", "aux", None),
        check_vma=False,
    )
```

```python
import functools

import jax
import jax.numpy as jnp
from jax import lax
from jax.experimental import pallas as pl
from jax.experimental.pallas import tpu as pltpu
from jax.sharding import PartitionSpec as P

ROUNDS = ((1, 0), (1, 1), (2, 0), (2, 1), (3, 0), (3, 1))
CAP = 2
TAIL = 16
PAIRS = tuple((i, j) for i in range(3) for j in range(i, 3))
MIB = 2**20
NO_COST = pl.CostEstimate(flops=0, bytes_accessed=0, transcendentals=0)
ANY = pl.BlockSpec(memory_space=pl.ANY)
SMEM = pl.BlockSpec(memory_space=pltpu.SMEM)
VMEM = pl.BlockSpec(memory_space=pltpu.VMEM)


def round_pairs(distance, parity, frags):
    up = [(i, i + distance) for i in range(frags - distance) if (i // distance) % 2 == parity]
    return up + [(b, a) for a, b in up]


class Lists:
    def __init__(self, ints, listed, frags, own_count, list_len):
        self.ints, self.listed = ints, listed
        self.frags, self.own_count, self.list_len = frags, own_count, list_len
        self.me = ints[0]

    def row(self, fragment, k):
        return self.ints[2 + self.listed[fragment, k]]

    def pick(self, fragment, owner):
        count = jnp.int32(0)
        picked = [jnp.int32(0)] * CAP
        for k in range(self.list_len):
            row = self.row(fragment, k)
            hit = row // self.own_count == owner
            for r in range(CAP):
                picked[r] = jnp.where(hit & (count == r), row % self.own_count, picked[r])
            count = count + hit.astype(jnp.int32)
        return picked, count


def send_kernel(sizes, ints, listed, tails, table, *refs):
    outs, own, sems = refs[:6], refs[6], refs[7]
    lists = Lists(ints, listed, *sizes)
    me, frags = lists.me, lists.frags
    block = table.shape[1]
    copies = []

    def start(out, index, fragment, inside):
        picked, count = lists.pick(fragment, me)
        for r in range(CAP):
            copy = pltpu.make_async_copy(
                table.at[picked[r]], out.at[pl.ds(r * block, block)], sems.at[index, r]
            )
            needed = inside & (count > r)
            pl.when(needed)(copy.start)
            copies.append((needed, copy))

    for index, (distance, parity) in enumerate(ROUNDS):
        up = (me // distance) % 2 == parity
        partner = jnp.where(up, me + distance, me - distance)
        inside = (partner >= 0) & (partner < frags)
        start(outs[index], index, jnp.clip(partner, 0, frags - 1), inside)
    start(own, 6, me, me >= 0)
    own[pl.ds(CAP * block, TAIL), :] = tails[pl.ds(0, TAIL), :]
    for out in outs:
        out[pl.ds(CAP * block, TAIL), :] = tails[pl.ds(TAIL, TAIL), :]
    for needed, copy in copies:
        pl.when(needed)(copy.wait)


def pack_to_send(ints, vir_list, tails, table, sizes):
    _, block_rows, cols = table.shape
    part = jax.ShapeDtypeStruct((CAP * block_rows + TAIL, cols), table.dtype)
    return pl.pallas_call(
        functools.partial(send_kernel, sizes),
        out_shape=(part,) * 7,
        in_specs=[SMEM, SMEM, VMEM, ANY],
        out_specs=(VMEM,) * 7,
        scratch_shapes=[pltpu.SemaphoreType.DMA((7, CAP))],
        compiler_params=pltpu.CompilerParams(vmem_limit_bytes=50 * MIB),
        cost_estimate=NO_COST,
        name="pack_to_send",
    )(ints, vir_list, tails, table)


def plan_kernel(sizes, ints, listed, plan, target):
    lists = Lists(ints, listed, *sizes)
    me, (frags, own_count, list_len) = lists.me, sizes
    rows, owners, codes, classes = [], [], [], []
    for k in range(list_len):
        row = lists.row(me, k)
        owner = row // own_count
        low = jnp.minimum(me, owner)
        far = jnp.abs(owner - me)
        code = jnp.int32(0)
        for index, (distance, parity) in enumerate(ROUNDS):
            code = jnp.where(
                (far == distance) & ((low // distance) % 2 == parity), index + 1, code
            )
        rows.append(row)
        owners.append(owner)
        codes.append(code)
        classes.append(jnp.where(code == 0, 0, jnp.maximum(code - 3, 1)))
    for k in range(list_len):
        place = jnp.int32(0)
        rank = jnp.int32(0)
        for j in range(list_len):
            if j < k:
                place += (classes[j] <= classes[k]).astype(jnp.int32)
                rank += (owners[j] == owners[k]).astype(jnp.int32)
            elif j > k:
                place += (classes[j] < classes[k]).astype(jnp.int32)
        plan[0, place] = codes[k]
        plan[1, place] = rank
        plan[2, place] = rows[k]
        plan[3, place] = jnp.int32(k)

    def one(fragment, carry):
        picked, _ = lists.pick(fragment, me)
        for r in range(CAP):
            target[fragment, r] = picked[r]
        return carry

    lax.fori_loop(0, frags, one, 0)


def plan_lists(ints, vir_list, sizes):
    frags, _, list_len = sizes
    return pl.pallas_call(
        functools.partial(plan_kernel, sizes),
        out_shape=(
            jax.ShapeDtypeStruct((4, list_len), jnp.int32),
            jax.ShapeDtypeStruct((frags, CAP), jnp.int32),
        ),
        in_specs=[SMEM, SMEM],
        out_specs=(SMEM, SMEM),
        compiler_params=pltpu.CompilerParams(vmem_limit_bytes=4 * MIB),
        cost_estimate=NO_COST,
        name="plan_lists",
    )(ints, vir_list)


def pack_kernel(first, codes, block, with_energy, plan, *refs):
    count = len(codes)
    if with_energy:
        own_energy, arrived, (out, levels, raw, wide, sems, tail_sems) = (
            refs[0],
            refs[1 : count + 1],
            refs[count + 1 :],
        )
    else:
        arrived, (out, sems) = refs[:count], refs[count:]
    for i in range(2):
        code = plan[0, first + i]
        begin = pl.multiple_of(plan[1, first + i] * block, block)
        rows = pl.ds(i * block, block)
        for source, ref in zip(codes, arrived):

            @pl.when(code == source)
            def _(ref=ref, begin=begin, rows=rows):
                pltpu.make_async_copy(
                    ref.at[pl.ds(begin, block)], out.at[rows], sems.at[i]
                ).start()

    if with_energy:
        own_count = own_energy.shape[0]
        copies = [
            pltpu.make_async_copy(
                ref.at[pl.ds(2 * block, TAIL), pl.ds(0, block)],
                raw.at[pl.ds(n * TAIL, TAIL)],
                tail_sems.at[n],
            )
            for n, ref in enumerate(arrived)
        ]
        for copy in copies:
            copy.start()
        wide[0:own_count, :] = own_energy[...].astype(jnp.float32)
        for copy in copies:
            copy.wait()
        wide[TAIL:, :] = raw[...].astype(jnp.float32)
        levels[...] = jnp.zeros_like(levels)
        for place in range(first + 2):
            row = plan[0, place] * TAIL + plan[2, place] % own_count
            levels[place : place + 1, :] = wide[pl.ds(row, 1), :]
    for i in range(2):
        rows = pl.ds(i * block, block)
        pltpu.make_async_copy(arrived[0].at[rows], out.at[rows], sems.at[i]).wait()


def pack_group(first, block, plan, arrived, own_energy=None):
    codes = tuple(arrived)
    refs = [arrived[c] for c in codes]
    cols, dtype = refs[0].shape[1], refs[0].dtype
    shapes = [jax.ShapeDtypeStruct((2 * block, cols), dtype)]
    scratch = [pltpu.SemaphoreType.DMA((2,))]
    extra = []
    if own_energy is not None:
        shapes.append(jax.ShapeDtypeStruct((plan.shape[1], block), jnp.float32))
        scratch = [
            pltpu.VMEM((len(codes) * TAIL, block), dtype),
            pltpu.VMEM(((len(codes) + 1) * TAIL, block), jnp.float32),
            *scratch,
            pltpu.SemaphoreType.DMA((len(codes),)),
        ]
        extra = [own_energy]
    return pl.pallas_call(
        functools.partial(pack_kernel, first, codes, block, own_energy is not None),
        out_shape=tuple(shapes),
        in_specs=[SMEM] + [VMEM] * len(extra) + [ANY] * len(refs),
        out_specs=(VMEM,) * len(shapes),
        scratch_shapes=scratch,
        compiler_params=pltpu.CompilerParams(vmem_limit_bytes=4 * MIB),
        cost_estimate=NO_COST,
        name="pack_group",
    )(plan, *extra, *refs)


def place_of(aux, b):
    return aux + 4 * b


def contract_kernel(stage, block, width, where, plan, levels, rows_ref, energy, *refs):
    groups = min(stage + 2, 4)
    parts, rest = refs[: groups * 4], refs[groups * 4 :]
    quarters = {2: (0, 2), 3: (1, 3)}.get(stage, (0, 1, 2, 3))
    partial = None
    if stage == 2:
        total, left, grid, occ, scaled, left_sems, grid_sems, occ_sems = rest
    elif stage == 3:
        before, partial, rest = rest[:2], rest[2], rest[3:]
        sent, stay, left, grid, occ, scaled, total, amps, tall, dens = rest[:10]
        left_sems, grid_sems, occ_sems = rest[10:]
    elif stage == 1:
        out, left, grid, occ, scaled, total, amps, tall, left_sems, grid_sems, occ_sems = rest
    else:
        out, left, grid, occ, scaled, total, amps, left_sems, grid_sems, occ_sems = rest
    aux = where[1]
    places = (place_of(aux, 0), place_of(aux, 1))

    def occ_copy(quarter):
        return pltpu.make_async_copy(
            parts[quarter].at[pl.ds(2 * block, TAIL)],
            occ.at[pl.ds(quarter * TAIL, TAIL)],
            occ_sems.at[quarter],
        )

    def left_copy(b, group, begin, quarter):
        return pltpu.make_async_copy(
            parts[group * 4 + quarter].at[pl.ds(begin, block)],
            left.at[pl.ds(b * block, block), pl.ds(quarter * width, width)],
            left_sems.at[b, quarter],
        )

    def grid_copy(slot, group, quarter):
        return pltpu.make_async_copy(
            parts[group * 4 + quarter].at[pl.ds(0, 2 * block)],
            grid.at[pl.ds(slot * 2 * block, 2 * block), pl.ds(quarter * width, width)],
            grid_sems.at[slot, quarter],
        )

    def run(row_count, group_list):
        for quarter in quarters:
            occ_copy(quarter).start()
            for b in range(row_count):
                begin = pl.multiple_of((places[b] % 2) * block, block)
                for group in range(groups):

                    @pl.when(places[b] // 2 == group)
                    def _(b=b, group=group, begin=begin, quarter=quarter):
                        left_copy(b, group, begin, quarter).start()

            for slot, group in enumerate(group_list):
                grid_copy(slot, group, quarter).start()
        height = len(PAIRS) * row_count * block
        span = len(group_list) * 2 * block

        def scale(turn):
            quarter = quarters[turn]
            cols = pl.ds(quarter * width, width)
            orbit = [
                occ[quarter * TAIL + i : quarter * TAIL + i + 1, :].astype(jnp.float32)
                for i in range(3)
            ]
            for b in range(row_count):
                rows = left[pl.ds(b * block, block), cols].astype(jnp.float32)
                for p, (i, j) in enumerate(PAIRS):
                    scaled[turn % 2, pl.ds((p * row_count + b) * block, block), :] = (
                        rows * (orbit[i] * orbit[j])
                    ).astype(jnp.bfloat16)

        def wait_left(turn):
            quarter = quarters[turn]
            occ_copy(quarter).wait()
            for b in range(row_count):
                left_copy(b, 0, 0, quarter).wait()

        wait_left(0)
        scale(0)
        for turn, quarter in enumerate(quarters):
            cols = pl.ds(quarter * width, width)
            for slot, group in enumerate(group_list):
                grid_copy(slot, group, quarter).wait()
            if turn + 1 < len(quarters):
                wait_left(turn + 1)
                scale(turn + 1)
            for step in range(height // 768):
                rows = pl.ds(step * 768, 768)
                term = lax.dot_general(
                    scaled[turn % 2, rows, :],
                    grid[pl.ds(0, span), cols],
                    (((1,), (1,)), ((), ())),
                    preferred_element_type=jnp.float32,
                )
                if turn:
                    total[rows, pl.ds(0, span)] += term
                elif partial is not None:
                    total[rows, pl.ds(0, span)] = term + partial[rows, :]
                else:
                    total[rows, pl.ds(0, span)] = term
        if stage == 2:
            return None
        lane = lax.broadcasted_iota(jnp.int32, (block, block), 1)
        sub = lax.broadcasted_iota(jnp.int32, (block, block), 0)
        sums = []
        for b in range(row_count):
            own_row = energy[pl.ds(places[b], 1), :]
            own_energy = jnp.transpose(jnp.broadcast_to(own_row, (block, block)))
            own_live = sub < rows_ref[where[0], plan[3, places[b]]]
            for q in range(2 * len(group_list)):
                place = 2 * group_list[q // 2] + q % 2
                their_energy = energy[place : place + 1, :]
                live = own_live & (lane < rows_ref[where[0], plan[3, place]])
                for p, (i, j) in enumerate(PAIRS):
                    gap = (levels[0, i] + levels[0, j]) - own_energy - their_energy
                    rows = pl.ds((p * row_count + b) * block, block)
                    value = total[rows, pl.ds(q * block, block)]
                    amp = jnp.where(live, value * pl.reciprocal(gap), 0.0).astype(jnp.bfloat16)
                    amps[:, pl.ds(p * span + q * block, block)] = amp
                    if stage == 3:
                        early = amp if b == 0 else jnp.where(aux < 2, amp, jnp.zeros_like(amp))
                        tall[rows, pl.ds(q * block, block)] = early
                    elif stage == 1 and b == 0:
                        tall[pl.ds(p * block, block), pl.ds(q * block, block)] = amp
            wide = amps[:, pl.ds(0, len(PAIRS) * span)]
            sums.append(
                lax.dot_general(
                    wide, wide, (((1,), (1,)), ((), ())), preferred_element_type=jnp.float32
                )
            )
        return sums

    def late_sum(q):
        late = tall[:, pl.ds(q * block, block)]
        return lax.dot_general(
            late, late, (((0,), (0,)), ((), ())), preferred_element_type=jnp.float32
        )

    if stage == 0:
        out[0] = run(1, (0, 1))[0]
    elif stage == 1:

        @pl.when(aux < 2)
        def _():
            out[0], out[1] = run(2, (2,))

        @pl.when(aux >= 2)
        def _():
            out[0] = run(1, (2,))[0]
            out[1] = jnp.zeros(out.shape[1:], out.dtype)

        for q in range(2):
            out[2 + q] = late_sum(q)
    elif stage == 2:
        run(2, (3,))
    else:
        first, second = before
        sums = run(2, (3,))
        dens[0] = sums[0] + (first[0] + second[0])
        share = sums[1] + second[1]
        for q in range(4):
            late = second[2 + q] if q < 2 else late_sum(q - 2)
            dens[1 + q] = late + jnp.where(aux == q, share, 0.0)
        half = block // 2
        side = aux // 2
        stay[...] = dens[:, pl.ds(pl.multiple_of(side * half, half), half), :]
        away = dens[:, pl.ds(pl.multiple_of((1 - side) * half, half), half), :]
        sent[...] = away.astype(jnp.bfloat16)


def contract(stage, where, plan, levels, vir_rows, energy, parts, before=()):
    block, width = energy.shape[1], parts[0].shape[1]
    height = len(PAIRS) * 2 * block
    span = (4, 2, 2, 2)[stage] * block
    scratch = [
        pltpu.VMEM((2 * block, 4 * width), jnp.bfloat16),
        pltpu.VMEM((span, 4 * width), jnp.bfloat16),
        pltpu.VMEM((4 * TAIL, width), jnp.bfloat16),
        pltpu.VMEM((2, height, width), jnp.bfloat16),
    ]
    if stage != 2:
        scratch += [
            pltpu.VMEM((height, span), jnp.float32),
            pltpu.VMEM((block, len(PAIRS) * span), jnp.bfloat16),
        ]
    out_specs = VMEM
    if stage == 3:
        scratch += [
            pltpu.VMEM((height, span), jnp.bfloat16),
            pltpu.VMEM((5, block, block), jnp.float32),
        ]
        out_shape = tuple(
            jax.ShapeDtypeStruct((5, block // 2, block), dtype)
            for dtype in (jnp.bfloat16, jnp.float32)
        )
        out_specs = (VMEM, VMEM)
    elif stage == 2:
        out_shape = jax.ShapeDtypeStruct((height, span), jnp.float32)
    elif stage == 1:
        scratch += [pltpu.VMEM((height // 2, span), jnp.bfloat16)]
        out_shape = jax.ShapeDtypeStruct((4, block, block), jnp.float32)
    else:
        out_shape = jax.ShapeDtypeStruct((1, block, block), jnp.float32)
    scratch += [
        pltpu.SemaphoreType.DMA((2, 4)),
        pltpu.SemaphoreType.DMA((3, 4)),
        pltpu.SemaphoreType.DMA((4,)),
    ]
    cost = NO_COST
    if stage in (1, 2):
        units = (4, 4, 2)[stage] * len(PAIRS) * block * block
        cost = pl.CostEstimate(
            flops=2 * units * 4 * width, bytes_accessed=units * 4, transcendentals=0
        )
    return pl.pallas_call(
        functools.partial(contract_kernel, stage, block, width),
        out_shape=out_shape,
        in_specs=[SMEM] * 4 + [VMEM] + [ANY] * len(parts) + [VMEM] * len(before),
        out_specs=out_specs,
        scratch_shapes=scratch,
        compiler_params=pltpu.CompilerParams(vmem_limit_bytes=26 * MIB),
        cost_estimate=cost,
        name="contract",
    )(where, plan, levels, vir_rows, energy, *parts, *before)


def spread_kernel(own_count, where, plan, kept, came, out):
    aux = where[1]
    out[...] = jnp.zeros_like(out)

    def put(place, value):
        out[plan[2, place] // own_count, plan[1, place]] = value.astype(out.dtype)

    put(aux, kept[0])
    put(aux ^ 2, kept[1])
    put(aux ^ 1, came[0])
    put(aux ^ 3, came[1])
    for q in range(4):
        put(4 + q, kept[2 + q] + came[2 + q])


def spread(ints, plan, kept, came, frags, own_count):
    return pl.pallas_call(
        functools.partial(spread_kernel, own_count),
        out_shape=jax.ShapeDtypeStruct((frags, CAP) + kept.shape[1:], jnp.bfloat16),
        in_specs=[SMEM, SMEM, VMEM, VMEM],
        out_specs=VMEM,
        compiler_params=pltpu.CompilerParams(vmem_limit_bytes=4 * MIB),
        name="spread",
    )(ints, plan, kept, came)


def collect_kernel(target, came, out):
    out[...] = jnp.zeros_like(out)

    def one(fragment, carry):
        for r in range(CAP):
            out[target[fragment, r]] += came[fragment, r].astype(jnp.float32)
        return carry

    lax.fori_loop(0, came.shape[0], one, 0, unroll=8)


def collect(target, came, own_count):
    return pl.pallas_call(
        collect_kernel,
        out_shape=jax.ShapeDtypeStruct((own_count,) + came.shape[2:], jnp.float32),
        in_specs=[SMEM, VMEM],
        out_specs=VMEM,
        compiler_params=pltpu.CompilerParams(vmem_limit_bytes=4 * MIB),
        name="collect",
    )(target, came)


def body(vir_grid, vir_energy, occ_grid, occ_energy, vir_list, vir_rows, owner_map):
    frags = lax.axis_size("frag")
    aux_count = lax.axis_size("aux")
    me = lax.axis_index("frag").astype(jnp.int32)
    aux = lax.axis_index("aux").astype(jnp.int32)
    own_count, block, width = vir_grid.shape
    list_len = vir_list.shape[1]
    sizes = (frags, own_count, list_len)
    ints = jnp.concatenate([me[None], aux[None], owner_map])
    occ_count = occ_grid.shape[1]
    tails = jnp.concatenate([
        jnp.pad(occ_grid[0], ((0, TAIL - occ_count), (0, 0))),
        jnp.pad(vir_energy, ((0, TAIL - own_count), (0, width - block))),
    ])
    far_pairs = [(i, i ^ 2) for i in range(aux_count)]
    near_pairs = [(i, i ^ 1) for i in range(aux_count)]

    *outgoing, own = pack_to_send(ints, vir_list, tails, vir_grid, sizes)

    def over_aux(here, *others):
        far = lax.ppermute(here, "aux", far_pairs)
        near = lax.ppermute(here, "aux", near_pairs)
        onward = after(far, *others) if others else far
        return [here, far, near, lax.ppermute(onward, "aux", near_pairs)]

    def after(value, *others):
        return lax.optimization_barrier((value, *others))[0]

    def send(index, *others):
        distance, parity = ROUNDS[index]
        payload = after(outgoing[index], *others) if others else outgoing[index]
        return lax.ppermute(payload, "frag", round_pairs(distance, parity, frags))

    arrived = {code: send(code - 1) for code in (1, 2, 3, 4)}
    parts = over_aux(own)
    plan, target = plan_lists(after(ints, arrived[3]), vir_list, sizes)
    here = pack_group(2, block, plan, {c: arrived[c] for c in range(1, 5)})[0]
    arrived[5] = send(4, here)
    parts += over_aux(here)
    arrived[6] = send(5, parts[5])
    here, early_energy = pack_group(
        4, block, plan, {c: arrived[c] for c in range(1, 6)}, vir_energy
    )
    shared = (ints, plan, occ_energy, vir_rows)
    first = contract(0, *shared, early_energy, parts[:8])
    arrived[6] = after(arrived[6], first)
    last, energy = pack_group(6, block, plan, arrived, vir_energy)
    near = lax.ppermute(last, "aux", near_pairs)
    far = lax.ppermute(last, "aux", far_pairs)
    parts += over_aux(here, near)
    second = contract(1, *shared, early_energy, parts[:12])
    partial = contract(2, *shared, energy, parts + [last, last, near, near])
    far_near = lax.ppermute(after(far, second, partial), "aux", near_pairs)
    parts += [last, far, near, far_near]
    sent, stay = contract(3, *shared, energy, parts, (first, second, partial))

    quarter = block // aux_count
    core = aux % 2
    met = lax.ppermute(sent, "aux", far_pairs).astype(jnp.float32)
    both = jnp.concatenate([stay[:1], met[:1], stay[1:] + met[1:]], axis=0)
    sent = lax.dynamic_slice_in_dim(both, (1 - core) * quarter, quarter, 1)
    kept = lax.dynamic_slice_in_dim(both, core * quarter, quarter, 1)
    came = lax.ppermute(sent, "aux", near_pairs)
    outgoing = spread(ints, plan, kept, came, frags, own_count)
    incoming = lax.all_to_all(outgoing, "frag", 0, 0, tiled=True)
    return collect(target, incoming, own_count)


def solution(mesh):
    return jax.shard_map(
        body,
        mesh=mesh,
        in_specs=(
            P("frag", None, "aux"),
            P("frag", None),
            P("frag", None, "aux"),
            P("frag", None),
            P(),
            P(),
            P(),
        ),
        out_specs=P("frag", "aux", None),
        check_vma=False,
    )
```
